32 devices in a mesh: section: 2 (over core), dp: 16 (over z, y, x).
Axes of the slice: x: 2, y: 2, z: 4, core: 2. Of those that a mesh axis runs over, the one named last changes fastest.
Arguments:
- patches: bfloat16 [12800, 1024], P('dp'), may hold values from -6 to 6
- live: int32 [256], P('dp'), may hold values 0 or 1
- cotangent: bfloat16 [12800, 1024], P('dp'), may hold values from -6 to 6
- w_qkv: float32 [2, 1024, 3072], P('section', 'dp'), may hold values from -0.25 to 0.25
- w_proj: float32 [2, 1024, 1024], P('section', 'dp'), may hold values from -0.5 to 0.5
- w_in: float32 [2, 1024, 4096], P('section', 'dp'), may hold values from -0.1875 to 0.1875
- w_out: float32 [2, 4096, 1024], P('section', 'dp'), may hold values from -0.125 to 0.125
- vectors: float32 [2, 12, 1024], P('section', None, 'dp'), may hold values from -1.2 to 2.4, as said below
- first_qkv: float32 [2, 1024, 3072], P('section', 'dp'), may hold values from -0.0001454472 to 0.0001454472
- first_proj: float32 [2, 1024, 1024], P('section', 'dp'), may hold values from -7.571223e-05 to 7.571223e-05
- first_in: float32 [2, 1024, 4096], P('section', 'dp'), may hold values from -0.00013349262 to 0.00013349262
- first_out: float32 [2, 4096, 1024], P('section', 'dp'), may hold values from -0.00011356835 to 0.00011356835
- first_vectors: float32 [2, 12, 1024], P('section', None, 'dp'), may hold values from -0.00018529574 to 0.00018529574
- second_qkv: float32 [2, 1024, 3072], P('section', 'dp'), may hold values from 2.5406504e-09 to 1.0162601e-08
- second_proj: float32 [2, 1024, 1024], P('section', 'dp'), may hold values from 6.748603e-10 to 2.6994411e-09
- second_in: float32 [2, 1024, 4096], P('section', 'dp'), may hold values from 2.103976e-09 to 8.415904e-09
- second_out: float32 [2, 4096, 1024], P('section', 'dp'), may hold values from 1.5085112e-09 to 6.034045e-09
- second_vectors: float32 [2, 12, 1024], P('section', None, 'dp'), may hold values from 4.1682546e-09 to 1.6673019e-08
Outputs:
- blocks: bfloat16 [2, 12800, 1024], P('section', 'dp')
- input_grad: bfloat16 [2, 12800, 1024], P('section', 'dp')
- grad_qkv: float32 [2, 1024, 3072], P('section', 'dp')
- grad_proj: float32 [2, 1024, 1024], P('section', 'dp')
- grad_in: float32 [2, 1024, 4096], P('section', 'dp')
- grad_out: float32 [2, 4096, 1024], P('section', 'dp')
- grad_vectors: float32 [2, 12, 1024], P('section', None, 'dp')
- grad_norm: float32 [], replicated
- new_qkv: float32 [2, 1024, 3072], P('section', 'dp')
- new_proj: float32 [2, 1024, 1024], P('section', 'dp')
- new_in: float32 [2, 1024, 4096], P('section', 'dp')
- new_out: float32 [2, 4096, 1024], P('section', 'dp')
- new_vectors: float32 [2, 12, 1024], P('section', None, 'dp')
- lowered_qkv: bfloat16 [2, 1024, 3072], P('section', 'dp')
- lowered_proj: bfloat16 [2, 1024, 1024], P('section', 'dp')
- lowered_in: bfloat16 [2, 1024, 4096], P('section', 'dp')
- lowered_out: bfloat16 [2, 4096, 1024], P('section', 'dp')
- lowered_vectors: bfloat16 [2, 12, 1024], P('section', None, 'dp')
- momentum_qkv: float32 [2, 1024, 3072], P('section', 'dp')
- momentum_proj: float32 [2, 1024, 1024], P('section', 'dp')
- momentum_in: float32 [2, 1024, 4096], P('section', 'dp')
- momentum_out: float32 [2, 4096, 1024], P('section', 'dp')
- momentum_vectors: float32 [2, 12, 1024], P('section', None, 'dp')
- variance_qkv: float32 [2, 1024, 3072], P('section', 'dp')
- variance_proj: float32 [2, 1024, 1024], P('section', 'dp')
- variance_in: float32 [2, 1024, 4096], P('section', 'dp')
- variance_out: float32 [2, 4096, 1024], P('section', 'dp')
- variance_vectors: float32 [2, 12, 1024], P('section', None, 'dp')
The draws below stay inside these ranges and needn't reach their ends.
Inputs may be any that keep to these rules, and one draw needn't show every extreme that they name: `vectors`: rows 0 and 5 of each layer are positive gains.
All inputs are finite; a program needn't handle non-finite values. No bound on the sum of `live` on one device may be relied on, other than what follows from the above.
Results may differ from the reference program's by a relative error of at most 0.03.
Values may be sent and summed in bfloat16 or wider, within the bound.
No kernel may reach another device: no remote copies, remote signals or barrier semaphores. Data moves between devices by JAX's collectives and lax.ppermute only.
A program may use at most 320 MiB of HBM per device.

```python
import math
import jax
import jax.numpy as jnp
from jax import lax

D = 1024
HEADS = 16
HEAD = 64
FF = 4096
SEQ = 50
STEP = 10
TOK_DEV = 800
IMAGES = 256
TOKENS = 12800
PARAMS = 25190400
N_DP = 16


def draw_vectors(key, part):
    key = jax.random.fold_in(key, 11)
    key_gain, key_bias = jax.random.split(key)
    position = jnp.arange(D, dtype=jnp.float32) / (D - 1)
    rising = 0.5 + position
    jitter = jax.random.uniform(key_gain, (2, 12, D), jnp.float32, 0.8, 1.25)
    offsets = jnp.clip(0.3 * jax.random.normal(key_bias, (2, 12, D), jnp.float32), -1.2, 1.2)
    gains = rising * jitter
    row_slot = jnp.arange(12)[None, :, None]
    return jnp.where((row_slot == 0) | (row_slot == 5), gains, offsets)


def draw_w_in(key, part):
    key = jax.random.fold_in(key, 13)
    key_rows = jax.random.fold_in(key, 0)
    scale = D ** (-0.5)
    return jnp.clip(jax.random.normal(key_rows, (2, D, FF), jnp.float32), -6.0, 6.0) * scale


def touch_ends(result, key, low, largest):
    extent = result.shape
    place = [jax.random.randint(jax.random.fold_in(key, axis), (), 0, extent[axis]) for axis in range(len(extent))]
    result = result.at[tuple(place)].set(low)
    longest = extent.index(max(extent))
    place[longest] = (place[longest] + 1) % extent[longest]
    return result.at[tuple(place)].set(largest)


def steps_of(stream_key, dims, cuts, low, largest):
    factor_of, own = 1.0, jax.random.fold_in(stream_key, 6)
    for dim, blocks in cuts:
        heights = jnp.exp(jax.random.uniform(jax.random.fold_in(own, dim), (blocks,), jnp.float32, low / len(cuts), largest / len(cuts)))
        factor_of = factor_of * jnp.repeat(heights, dims[dim] // blocks).reshape([-1 if axis == dim else 1 for axis in range(len(dims))])
    return factor_of


def noise(rng, shape, scale, most, shards=(), kind=jnp.bfloat16):
    array = jax.random.normal(rng, shape, jnp.float32) * scale
    if len(shards) > 0:
        array = steps_of(rng, shape, shards, -0.22, 0.18) * array
    return jnp.clip(array, min=-most, max=most).astype(kind)


def setup_inputs(seed: int = 0) -> dict:
    keys = jax.random.split(jax.random.key(seed), 19)
    patches = noise(keys[0], (TOKENS, D), 1.0, 6.0, ((0, 16),))
    live = touch_ends((jax.random.randint(keys[1], (IMAGES,), 0, 4) < 3).astype(jnp.int32), jax.random.fold_in(keys[1], 1), 0, 1)
    cotangent = noise(keys[2], (TOKENS, D), 1.0, 6.0, ((0, 16),))
    w_qkv = noise(keys[3], (2, D, 3 * D), (D // 2) ** -0.5, 0.25, ((0, 2), (1, 16)), jnp.float32)
    w_proj = noise(keys[4], (2, D, D), (D // 8) ** -0.5, 0.5, ((0, 2), (1, 16)), jnp.float32)
    w_in = draw_w_in(jax.random.fold_in(keys[18], 71), 0)
    w_out = noise(keys[6], (2, FF, D), (FF // 2) ** -0.5, 0.125, ((0, 2), (1, 16)), jnp.float32)
    vectors = draw_vectors(jax.random.fold_in(keys[18], 71), 0)
    first_qkv = noise(keys[8], (2, D, 3 * D), (0.122 / PARAMS ** 0.5), 0.0001454472, ((0, 2), (1, 16)), jnp.float32)
    first_proj = noise(keys[9], (2, D, D), (0.063 / PARAMS ** 0.5), 7.571223250124604e-05, ((0, 2), (1, 16)), jnp.float32)
    first_in = noise(keys[10], (2, D, FF), (0.111 / PARAMS ** 0.5), 0.00013349262, ((0, 2), (1, 16)), jnp.float32)
    first_out = noise(keys[11], (2, FF, D), (0.094 / PARAMS ** 0.5), 0.00011356835, ((0, 2), (1, 16)), jnp.float32)
    first_vectors = noise(keys[12], (2, 12, D), (0.155 / PARAMS ** 0.5), 0.00018529574, ((0, 2), (2, 16)), jnp.float32)
    second_qkv = jnp.clip(jnp.exp(math.log(1.0162601427055051e-08) - 1.3862944 * jax.random.uniform(keys[13], (2, D, 3 * D), jnp.float32) ** steps_of(keys[13], (2, D, 3 * D), ((0, 2), (1, 16)), -0.2, 0.2)), 2.540650356763763e-09, 1.0162601427055051e-08)
    second_proj = jnp.clip(jnp.exp(math.log(2.6994411150838005e-09) - 1.3862944 * jax.random.uniform(keys[14], (2, D, D), jnp.float32) ** steps_of(keys[14], (2, D, D), ((0, 2), (1, 16)), -0.2, 0.2)), 6.748602787709501e-10, 2.6994411150838005e-09)
    second_in = jnp.clip(jnp.exp(math.log(8.415904417802267e-09) - 1.3862944 * jax.random.uniform(keys[15], (2, D, FF), jnp.float32) ** steps_of(keys[15], (2, D, FF), ((0, 2), (1, 16)), -0.2, 0.2)), 2.1039761044505667e-09, 8.415904417802267e-09)
    second_out = jnp.clip(jnp.exp(math.log(6.034044819358542e-09) - 1.3862944 * jax.random.uniform(keys[16], (2, FF, D), jnp.float32) ** steps_of(keys[16], (2, FF, D), ((0, 2), (1, 16)), -0.2, 0.2)), 1.5085112048396354e-09, 6.034044819358542e-09)
    second_vectors = jnp.clip(jnp.exp(math.log(1.6673018521373706e-08) - 1.3862944 * jax.random.uniform(keys[17], (2, 12, D), jnp.float32) ** steps_of(keys[17], (2, 12, D), ((0, 2), (2, 16)), -0.2, 0.2)), 4.1682546303434265e-09, 1.6673018521373706e-08)
    return {"patches": patches, "live": live, "cotangent": cotangent, "w_qkv": w_qkv, "w_proj": w_proj, "w_in": w_in, "w_out": w_out, "vectors": vectors, "first_qkv": first_qkv, "first_proj": first_proj, "first_in": first_in, "first_out": first_out, "first_vectors": first_vectors, "second_qkv": second_qkv, "second_proj": second_proj, "second_in": second_in, "second_out": second_out, "second_vectors": second_vectors}


@jax.custom_vjp
def low(v):
    return lax.optimization_barrier(v.astype(jnp.bfloat16)).astype(jnp.float32)

@jax.custom_vjp
def low_back(v):
    return v

def low_keep(v):
    return (low(v), None)

def low_pass(kept, grad):
    return (grad,)

def back_keep(v):
    return (v, None)

def back_low(kept, grad):
    return (low(grad),)
low.defvjp(low_keep, low_pass)
low_back.defvjp(back_keep, back_low)
norm_epsilon = 1e-06
clip_norm = 1.0
beta_one = 0.9
beta_two = 0.95
rate_matrix = 0.05
rate_vector = 1.0
decay_matrix = 0.1
epsilon = 1e-08

def highest(left, right):
    return jnp.dot(left, right, precision=lax.Precision.HIGHEST, preferred_element_type=jnp.float32)

def normalize(inputs):
    centered = inputs - lax.optimization_barrier(jnp.mean(inputs, axis=-1, keepdims=True))
    return centered * lax.rsqrt(lax.optimization_barrier(jnp.mean(centered * centered, axis=-1, keepdims=True)) + norm_epsilon)

def block_forward(inputs, w_qkv, w_proj, w_in, w_out, vectors):
    count_rows = inputs.shape[0]
    count_images = count_rows // SEQ
    bias_in = vectors[8:12].reshape(-1)
    hidden = low(normalize(inputs) * vectors[0] + vectors[1])
    bias_all = jnp.concatenate([vectors[2], jnp.zeros_like(vectors[2]), vectors[3]])
    packed = low(low_back(highest(hidden, w_qkv) + bias_all))
    shaped = packed.reshape(count_images, SEQ, 3, HEADS, HEAD)
    queries = shaped[:, :, 0]
    key_part = shaped[:, :, 1]
    values = shaped[:, :, 2]
    scaling = HEAD ** (-0.5)
    scores = low_back(jnp.einsum('ishd,ithd->ihst', queries, key_part, precision=lax.Precision.HIGHEST) * scaling)
    attention = low(jax.nn.softmax(scores, axis=-1))
    mixed_rows = jnp.einsum('ihst,ithd->ishd', attention, values, precision=lax.Precision.HIGHEST)
    mixed_rows = low(low_back(mixed_rows.reshape(count_rows, D)))
    branch = low_back(highest(mixed_rows, w_proj) + vectors[4])
    middle = inputs + branch
    hidden_two = low(normalize(middle) * vectors[5] + vectors[6])
    pre_act = low_back(highest(hidden_two, w_in) + bias_in)
    active = low(jax.nn.gelu(pre_act, approximate=False))
    return middle + low_back(highest(active, w_out) + vectors[7])

def stacked_forward(params, inputs, probe_zero):
    layer_one = tuple((p[0] for p in params))
    layer_two = tuple((p[1] for p in params))
    entry_rows = low_back(inputs)
    output_one = block_forward(entry_rows, *layer_one)
    entry_two = low(low_back(output_one + probe_zero))
    output_two = block_forward(entry_two, *layer_two)
    return (output_one, output_two)

def adam_update(weight, grad, first, second, factor, rate, decay):
    clipped = grad * factor
    momentum = beta_one * first + (1.0 - beta_one) * clipped
    variance = beta_two * second + (1.0 - beta_two) * clipped * clipped
    corrected_m = momentum / (1.0 - beta_one ** STEP)
    corrected_v = variance / (1.0 - beta_two ** STEP)
    updated = weight - rate * (corrected_m / (jnp.sqrt(corrected_v) + epsilon) + decay * weight)
    return (updated, momentum, variance)

def reference(patches, live, cotangent, w_qkv, w_proj, w_in, w_out, vectors, first_qkv, first_proj, first_in, first_out, first_vectors, second_qkv, second_proj, second_in, second_out, second_vectors):
    masters = (w_qkv, w_proj, w_in, w_out, vectors)

    def forward(params, inputs, probe_zero):
        lowered = tuple((low(p) for p in params))
        return stacked_forward(lowered, inputs, probe_zero)
    weighting = live.astype(jnp.float32).reshape(IMAGES, 1, 1)
    targets = (cotangent.astype(jnp.float32).reshape(IMAGES, SEQ, D) * weighting).reshape(N_DP, TOK_DEV, D)
    inputs_all = patches.astype(jnp.float32).reshape(N_DP, TOK_DEV, D)

    def group_pass(totals, pair):
        inputs, target = pair
        probe_zero = jnp.zeros_like(inputs)
        outputs, pullback = jax.vjp(forward, masters, inputs, probe_zero)
        weight_grads, grad_entry, grad_middle = pullback((jnp.zeros_like(outputs[0]), target))
        totals = jax.tree.map(jnp.add, totals, weight_grads)
        return (totals, (outputs[0].astype(jnp.bfloat16), outputs[1].astype(jnp.bfloat16), grad_entry.astype(jnp.bfloat16), grad_middle.astype(jnp.bfloat16)))
    zero_totals = tuple((jnp.zeros_like(m) for m in masters))
    totals, (block_one, block_two, grad_entry, grad_middle) = lax.scan(group_pass, zero_totals, (inputs_all, targets))
    blocks = jnp.stack([block_one.reshape(TOKENS, D), block_two.reshape(TOKENS, D)])
    input_grad = jnp.stack([grad_entry.reshape(TOKENS, D), grad_middle.reshape(TOKENS, D)])
    square_sum = sum((jnp.sum(g * g) for g in totals))
    grad_norm = jnp.sqrt(square_sum)
    factor = clip_norm / jnp.maximum(grad_norm, clip_norm)
    firsts = (first_qkv, first_proj, first_in, first_out, first_vectors)
    seconds = (second_qkv, second_proj, second_in, second_out, second_vectors)
    rates = (rate_matrix, rate_matrix, rate_matrix, rate_matrix, rate_vector)
    decays = (decay_matrix, decay_matrix, decay_matrix, decay_matrix, 0.0)
    results = [adam_update(w, g, f, s, factor, r, d) for w, g, f, s, r, d in zip(masters, totals, firsts, seconds, rates, decays)]
    news = tuple((item[0] for item in results))
    momenta = tuple((item[1] for item in results))
    variances = tuple((item[2] for item in results))
    copies = tuple((n.astype(jnp.bfloat16) for n in news))
    return (blocks, input_grad, totals[0], totals[1], totals[2], totals[3], totals[4], grad_norm, news[0], news[1], news[2], news[3], news[4], copies[0], copies[1], copies[2], copies[3], copies[4], momenta[0], momenta[1], momenta[2], momenta[3], momenta[4], variances[0], variances[1], variances[2], variances[3], variances[4])
```

```python
import functools
import jax
import jax.numpy as jnp
from jax import lax
from jax.experimental import pallas as pl
from jax.experimental.pallas import tpu as pltpu
from jax.sharding import PartitionSpec as P

HEADS = 16
HEAD = 64
SEQ = 50
STEP = 10
SIDE = 4
LEVELS = 4

norm_epsilon = 1e-06
clip_norm = 1.0
beta_one = 0.9
beta_two = 0.95
rate_matrix = 0.05
rate_vector = 1.0
decay_matrix = 0.1
epsilon = 1e-08
PAD = 128
low_type = jnp.bfloat16
wide = jnp.float32


def swap_cores(x):
    return lax.ppermute(x, "section", [(0, 1), (1, 0)])


def flip(x, bit):
    count = lax.axis_size("dp")
    return lax.ppermute(x, "dp", [(i, i ^ bit) for i in range(count)])


def shift(x, levels, by):
    pairs = [
        (level * SIDE + q, (level + by) * SIDE + q) for level in levels for q in range(SIDE)
    ]
    return lax.ppermute(x, "dp", pairs)


def split_halves(own, first):
    rows = own.shape[0] // 2
    below, above = own[:rows], own[rows:]
    keep = jnp.where(first, below, above)
    got = swap_cores(jnp.where(first, above, below))
    return jnp.where(first, keep, got), jnp.where(first, got, keep)


def join_halves(part_zero, part_one, first):
    got = swap_cores(jnp.where(first, part_one, part_zero))
    mine = jnp.where(first, part_zero, part_one)
    return jnp.where(
        first, jnp.concatenate([mine, got], axis=0), jnp.concatenate([got, mine], axis=0)
    )


def gather_column(part, level):
    ups, downs = [], []
    up = down = part
    for step in range(1, LEVELS):
        up = shift(up, range(step - 1, LEVELS - 1), 1)
        down = shift(down, range(1, LEVELS + 1 - step), -1)
        ups.append(up)
        downs.append(down)
    line = jnp.stack(ups[::-1] + [part] + downs)
    return lax.dynamic_slice_in_dim(line, LEVELS - 1 - level, LEVELS, axis=0)


def gather_pieces(part, level):
    column = gather_column(part, level)
    across = flip(column, 1)
    along = flip(column, 2)
    half = LEVELS // 2
    corner_low = flip(along[:half], 1)
    corner_high = flip(across[half:], 2)
    mine = [column, across, along, corner_low, corner_high]
    return mine, [swap_cores(piece) for piece in mine]


def assemble_kernel(cuts, rows, place_ref, *refs):
    pieces, outs, sems = refs[:10], refs[10:-1], refs[-1]
    me, core = place_ref[0], place_ref[1]
    half = LEVELS // 2
    copies = []
    for side in range(2):
        owner = lax.rem(core + side, 2)
        for slot in range(5):
            relative = min(slot, 3)
            first_level = half if slot == 4 else 0
            levels = LEVELS if slot < 3 else half
            chip = jnp.bitwise_xor(me, relative)
            for j in range(levels):
                row = ((first_level + j) * SIDE + chip) * 2 + owner
                for k, (start, width) in enumerate(cuts):
                    copies.append(
                        pltpu.make_async_copy(
                            pieces[side * 5 + slot].at[j, :, pl.ds(start, width)],
                            outs[k].at[pl.ds(pl.multiple_of(row * rows, rows), rows)],
                            sems.at[len(copies)],
                        )
                    )
    for copy in copies:
        copy.start()
    for copy in copies:
        copy.wait()


def assemble(mine, theirs, place, cuts):
    rows, columns = mine[0].shape[1:]
    total = LEVELS * SIDE * 2 * rows
    count = 2 * (3 * LEVELS + LEVELS) * len(cuts)
    size = total * sum(width for _, width in cuts) * 2
    outs = pl.pallas_call(
        functools.partial(assemble_kernel, cuts, rows),
        out_shape=[jax.ShapeDtypeStruct((total, width), low_type) for _, width in cuts],
        in_specs=[pl.BlockSpec(memory_space=pltpu.SMEM)] + [pl.BlockSpec(memory_space=pl.ANY)] * 10,
        out_specs=[pl.BlockSpec(memory_space=pl.ANY)] * len(cuts),
        scratch_shapes=[pltpu.SemaphoreType.DMA((count,))],
        cost_estimate=pl.CostEstimate(flops=0, bytes_accessed=2 * size, transcendentals=0),
        name="assemble",
    )(place, *mine, *theirs)
    return outs


def scatter_pieces(grad, core, me, level):
    columns = grad.shape[1]
    rows = grad.shape[0] // (LEVELS * SIDE * 2)
    shaped = grad.reshape(LEVELS * SIDE, 2, rows, columns)
    other = lax.dynamic_index_in_dim(shaped, 1 - core, 1, keepdims=False)
    mine = lax.dynamic_index_in_dim(shaped, core, 1, keepdims=False)
    got = swap_cores(other)
    chip = (mine.astype(wide) + got.astype(wide)).astype(low_type)
    chip = chip.reshape(LEVELS, SIDE, rows, columns)
    half = LEVELS // 2

    def toward(relative):
        return lax.dynamic_index_in_dim(chip, jnp.bitwise_xor(me, relative), 1, keepdims=False)

    corner = toward(3)
    from_across = flip(corner[:half], 1)
    from_along = flip(corner[half:], 2)
    along, across = toward(2), toward(1)
    along = jnp.concatenate(
        [(along[:half].astype(wide) + from_across.astype(wide)).astype(low_type), along[half:]]
    )
    across = jnp.concatenate(
        [across[:half], (across[half:].astype(wide) + from_along.astype(wide)).astype(low_type)]
    )
    got_across = flip(across, 1)
    got_along = flip(along, 2)
    line = toward(0).astype(wide) + got_across.astype(wide) + got_along.astype(wide)

    def pick(target):
        return lax.dynamic_index_in_dim(line, jnp.clip(target, 0, LEVELS - 1), 0, keepdims=False)

    up = down = 0.0
    for step in range(1, LEVELS):
        far = LEVELS - step
        up = shift((pick(level + far) + up).astype(low_type), range(0, step), 1).astype(wide)
        down = shift(
            (pick(level - far) + down).astype(low_type), range(LEVELS - step, LEVELS), -1
        ).astype(wide)
    return pick(level) + up + down


def total_of(value):
    value = value + swap_cores(value)
    across, along, corner = flip(value, 1), flip(value, 2), flip(value, 3)
    value = (value + across) + (along + corner)
    count = lax.axis_size("dp")

    def turn(by):
        pairs = [(i, (i + by * SIDE) % count) for i in range(count)]
        return lax.ppermute(value, "dp", pairs)

    one, two, three = turn(1), turn(2), turn(3)
    return (value + two) + (one + three)


def normalize(inputs):
    centered = inputs - jnp.mean(inputs, axis=-1, keepdims=True)
    inverse = lax.rsqrt(jnp.mean(centered * centered, axis=-1, keepdims=True) + norm_epsilon)
    return (centered * inverse, inverse)


def normalize_back(upstream, scaled, inverse):
    return inverse * (
        upstream
        - jnp.mean(upstream, axis=-1, keepdims=True)
        - scaled * jnp.mean(upstream * scaled, axis=-1, keepdims=True)
    )


def dot_nt(left, right):
    return lax.dot_general(left, right, (((1,), (1,)), ((), ())), preferred_element_type=wide)


def dot_nn(left, right):
    return lax.dot_general(left, right, (((1,), (0,)), ((), ())), preferred_element_type=wide)


def dot_tn(left, right):
    return lax.dot_general(left, right, (((0,), (0,)), ((), ())), preferred_element_type=wide)


def same_image(rows):
    image_row = lax.broadcasted_iota(jnp.int32, (rows, rows), 0) // SEQ
    image_col = lax.broadcasted_iota(jnp.int32, (rows, rows), 1) // SEQ
    return image_row == image_col


def attend_kernel(q_ref, k_ref, v_ref, o_ref):
    rows = q_ref.shape[0]
    mask = same_image(rows)
    lane = lax.broadcasted_iota(jnp.int32, (rows, 2 * HEAD), 1)
    queries, keys, values = q_ref[...], k_ref[...], v_ref[...]
    mixed = []
    for head in range(2):
        inside = (lane >= head * HEAD) & (lane < (head + 1) * HEAD)
        own = jnp.where(inside, queries, jnp.zeros_like(queries))
        scores = jnp.where(mask, dot_nt(own, keys) * HEAD ** (-0.5), -jnp.inf)
        raised = jnp.exp(scores - jnp.max(scores, axis=1, keepdims=True))
        weights = raised / jnp.sum(raised, axis=1, keepdims=True)
        mixed.append(dot_nn(weights.astype(low_type), values))
    o_ref[...] = jnp.where(lane < HEAD, mixed[0], mixed[1]).astype(low_type)


def attend(packed):
    rows, columns = packed.shape
    blocks = columns // 3 // (2 * HEAD)
    width = 2 * HEAD

    def at(third):
        return pl.BlockSpec((rows, width), lambda j: (0, third * blocks + j))

    return pl.pallas_call(
        attend_kernel,
        grid=(blocks,),
        in_specs=[at(0), at(1), at(2)],
        out_specs=at(0),
        out_shape=jax.ShapeDtypeStruct((rows, columns // 3), low_type),
        cost_estimate=pl.CostEstimate(
            flops=8 * rows * rows * columns // 3,
            bytes_accessed=8 * rows * columns // 3,
            transcendentals=rows * rows * HEADS,
        ),
        compiler_params=pltpu.CompilerParams(vmem_limit_bytes=32 * 1024 * 1024),
        name="attend",
    )(packed, packed, packed)


def attend_back_kernel(q_ref, k_ref, v_ref, g_ref, dq_ref, dk_ref, dv_ref):
    rows = q_ref.shape[0]
    mask = same_image(rows)
    lane = lax.broadcasted_iota(jnp.int32, (rows, 2 * HEAD), 1)
    queries, keys, values, upstream = q_ref[...], k_ref[...], v_ref[...], g_ref[...]
    scaling = HEAD ** (-0.5)
    to_queries, to_keys, to_values = [], [], []
    for head in range(2):
        inside = (lane >= head * HEAD) & (lane < (head + 1) * HEAD)
        zero = jnp.zeros_like(queries)
        own_queries = jnp.where(inside, queries, zero)
        own_upstream = jnp.where(inside, upstream, zero)
        scores = jnp.where(mask, dot_nt(keys, own_queries) * scaling, -jnp.inf)
        raised = jnp.exp(scores - jnp.max(scores, axis=0, keepdims=True))
        weights = raised / jnp.sum(raised, axis=0, keepdims=True)
        to_values.append(dot_nn(weights.astype(low_type), upstream))
        slope = dot_nt(values, own_upstream)
        inner = jnp.sum(weights * slope, axis=0, keepdims=True)
        change = (weights * (slope - inner)).astype(low_type)
        to_keys.append(dot_nn(change, queries))
        to_queries.append(dot_tn(keys, change))
    lower = lane < HEAD
    dv_ref[...] = jnp.where(lower, to_values[0], to_values[1]).astype(low_type)
    dk_ref[...] = (jnp.where(lower, to_keys[0], to_keys[1]) * scaling).astype(low_type)
    turned = jnp.concatenate([to_queries[0][:HEAD], to_queries[1][HEAD:]], axis=0)
    dq_ref[...] = (turned.T * scaling).astype(low_type)


def attend_back(packed, upstream):
    rows, columns = packed.shape
    blocks = columns // 3 // (2 * HEAD)
    width = 2 * HEAD

    def at(third):
        return pl.BlockSpec((rows, width), lambda j: (0, third * blocks + j))

    shape = jax.ShapeDtypeStruct((rows, columns // 3), low_type)
    return pl.pallas_call(
        attend_back_kernel,
        grid=(blocks,),
        in_specs=[at(0), at(1), at(2), at(0)],
        out_specs=[at(0)] * 3,
        out_shape=[shape] * 3,
        cost_estimate=pl.CostEstimate(
            flops=20 * rows * rows * columns // 3,
            bytes_accessed=14 * rows * columns // 3,
            transcendentals=rows * rows * HEADS,
        ),
        compiler_params=pltpu.CompilerParams(vmem_limit_bytes=48 * 1024 * 1024),
        name="attend_back",
    )(packed, packed, packed, upstream)


def dot(left, right):
    return jnp.dot(left, right, preferred_element_type=wide)


def back_dot(left, right):
    return jnp.einsum("nf,df->nd", left, right, preferred_element_type=wide)


def weight_dot(left, right):
    return jnp.einsum("nd,nf->df", left, right, preferred_element_type=wide).astype(low_type)


def layer_forward(inputs, weights, rows_all):
    w_qkv, w_proj, w_in, w_out = weights
    scaled_one, inverse_one = normalize(inputs)
    hidden = (scaled_one * rows_all[0] + rows_all[1]).astype(low_type)
    bias_all = jnp.concatenate([rows_all[2], jnp.zeros_like(rows_all[2]), rows_all[3]])
    packed = (dot(hidden, w_qkv) + bias_all).astype(low_type)
    mixed_low = attend(packed)
    middle = inputs + (dot(mixed_low, w_proj) + rows_all[4])
    scaled_two, inverse_two = normalize(middle)
    hidden_two = (scaled_two * rows_all[5] + rows_all[6]).astype(low_type)
    pre_act = dot(hidden_two, w_in) + rows_all[8:12].reshape(-1)
    active_low = jax.nn.gelu(pre_act, approximate=False).astype(low_type)
    output = middle + (dot(active_low, w_out) + rows_all[7])
    kept = (inputs, hidden, packed, mixed_low, middle, hidden_two, pre_act, active_low)
    return output, kept


def layer_backward(upstream, weights, rows_all, kept):
    w_qkv, w_proj, w_in, w_out = weights
    inputs, hidden, packed, mixed_low, middle, hidden_two, pre_act, active_low = kept
    scaled_one, inverse_one = normalize(inputs)
    scaled_two, inverse_two = normalize(middle)
    model_width = inputs.shape[1]
    grad_out_low = upstream.astype(low_type)
    grad_w_out = weight_dot(active_low, grad_out_low)
    grad_b_out = jnp.sum(grad_out_low.astype(wide), axis=0)
    grad_active = back_dot(grad_out_low, w_out)
    normal_cdf = 0.5 * (1.0 + lax.erf(pre_act * 0.7071067811865476))
    density = jnp.exp(-0.5 * pre_act * pre_act) * 0.3989422804014327
    grad_pre_low = (grad_active * (normal_cdf + pre_act * density)).astype(low_type)
    grad_w_in = weight_dot(hidden_two, grad_pre_low)
    grad_b_in = jnp.sum(grad_pre_low.astype(wide), axis=0)
    grad_hidden_two = back_dot(grad_pre_low, w_in)
    grad_gain_two = jnp.sum(grad_hidden_two * scaled_two, axis=0)
    grad_shift_two = jnp.sum(grad_hidden_two, axis=0)
    grad_middle = upstream + normalize_back(grad_hidden_two * rows_all[5], scaled_two, inverse_two)
    grad_branch_low = grad_middle.astype(low_type)
    grad_w_proj = weight_dot(mixed_low, grad_branch_low)
    grad_b_proj = jnp.sum(grad_branch_low.astype(wide), axis=0)
    grad_mixed_low = back_dot(grad_branch_low, w_proj).astype(low_type)
    grad_packed_low = jnp.concatenate(attend_back(packed, grad_mixed_low), axis=1)
    grad_w_qkv = weight_dot(hidden, grad_packed_low)
    column_sums = jnp.sum(grad_packed_low.astype(wide), axis=0)
    grad_hidden = back_dot(grad_packed_low, w_qkv)
    grad_gain_one = jnp.sum(grad_hidden * scaled_one, axis=0)
    grad_shift_one = jnp.sum(grad_hidden, axis=0)
    grad_entry = grad_middle + normalize_back(grad_hidden * rows_all[0], scaled_one, inverse_one)
    grad_rows = jnp.stack(
        [
            grad_gain_one,
            grad_shift_one,
            column_sums[:model_width],
            column_sums[2 * model_width :],
            grad_b_proj,
            grad_gain_two,
            grad_shift_two,
            grad_b_out,
        ]
    )
    grad_vectors = jnp.concatenate([grad_rows, grad_b_in.reshape(4, model_width)], axis=0)
    turned = jnp.pad(grad_vectors.T, ((0, 0), (0, PAD - grad_vectors.shape[0]))).astype(low_type)
    first_group = jnp.concatenate([grad_w_qkv, grad_w_proj, turned], axis=1)
    return grad_entry, (first_group, grad_w_in, grad_w_out)


def adam_update(weight, grad, first, second, factor, rate, decay):
    clipped = grad * factor
    momentum = beta_one * first + (1.0 - beta_one) * clipped
    variance = beta_two * second + (1.0 - beta_two) * clipped * clipped
    corrected_m = momentum / (1.0 - beta_one**STEP)
    corrected_v = variance / (1.0 - beta_two**STEP)
    updated = weight - rate * (corrected_m / (jnp.sqrt(corrected_v) + epsilon) + decay * weight)
    return (updated, momentum, variance)


def body(
    patches,
    live,
    cotangent,
    w_qkv,
    w_proj,
    w_in,
    w_out,
    vectors,
    first_qkv,
    first_proj,
    first_in,
    first_out,
    first_vectors,
    second_qkv,
    second_proj,
    second_in,
    second_out,
    second_vectors,
):
    core = lax.axis_index("section")
    first = core == 0
    chip = lax.axis_index("dp")
    count_dp = lax.axis_size("dp")
    tuned = count_dp == LEVELS * SIDE
    level = chip // SIDE
    me = chip % SIDE
    place = jnp.stack([me, core]).astype(jnp.int32)
    masters = (w_qkv[0], w_proj[0], w_in[0], w_out[0], vectors[0])
    count_vectors = vectors.shape[1]
    width = patches.shape[1]
    wide_qkv, wide_proj = w_qkv.shape[2], w_proj.shape[2]
    wide_first = wide_qkv + wide_proj + PAD
    turned = jnp.pad(vectors[0].T, ((0, 0), (0, PAD - count_vectors)))
    packs = (
        jnp.concatenate(
            [w_qkv[0].astype(low_type), w_proj[0].astype(low_type), turned.astype(low_type)], axis=1
        ),
        w_in[0].astype(low_type),
        w_out[0].astype(low_type),
    )
    cuts = (
        ((0, wide_qkv), (wide_qkv, wide_proj), (wide_qkv + wide_proj, PAD)),
        ((0, w_in.shape[2]),),
        ((0, w_out.shape[2]),),
    )

    gathered = [[], []]
    if tuned:
        parts = [split_halves(pack, first) for pack in packs]
        for layer in range(2):
            for part, cut in zip(parts, cuts):
                mine, theirs = gather_pieces(part[layer], level)
                gathered[layer].extend(assemble(mine, theirs, place, cut))
    else:
        for pack, cut in zip(packs, cuts):
            own = lax.all_gather(pack, "dp", axis=0, tiled=True)
            other = swap_cores(own)
            for layer in range(2):
                full = jnp.where(core == layer, own, other)
                gathered[layer].extend(full[:, start : start + size] for start, size in cut)

    layers = []
    for layer in range(2):
        g_qkv, g_proj, g_turned, g_in, g_out = gathered[layer]
        rows_all = g_turned[:, :count_vectors].T.astype(wide)
        layers.append(((g_qkv, g_proj, g_in, g_out), rows_all))

    tokens = patches.shape[0] // 2
    images = live.shape[0] // 2
    entry = lax.dynamic_slice_in_dim(patches, core * tokens, tokens, axis=0).astype(wide)
    weighting = lax.dynamic_slice_in_dim(live, core * images, images, axis=0).astype(wide)
    target = lax.dynamic_slice_in_dim(cotangent, core * tokens, tokens, axis=0).astype(wide)
    target = (
        target.reshape(images, SEQ, width) * weighting.reshape(images, 1, 1)
    ).reshape(tokens, width)

    output_zero, kept_zero = layer_forward(entry, *layers[0])
    block_zero = output_zero.astype(low_type)
    output_one, kept_one = layer_forward(block_zero.astype(wide), *layers[1])
    block_one = output_one.astype(low_type)

    def reduce_group(grad):
        if tuned:
            return scatter_pieces(grad, core, me, level)
        return grad

    entry_one, terms_one = layer_backward(target, *layers[1], kept_one)
    entry_one = entry_one.astype(low_type)
    halves_one = [reduce_group(term) for term in terms_one[::-1]][::-1]
    entry_zero, terms_zero = layer_backward(entry_one.astype(wide), *layers[0], kept_zero)
    entry_zero = entry_zero.astype(low_type)
    halves_zero = [reduce_group(term) for term in terms_zero[::-1]][::-1]

    if tuned:
        sums = [join_halves(a, b, first) for a, b in zip(halves_zero, halves_one)]
    else:
        sums = []
        for a, b in zip(terms_zero, terms_one):
            got = swap_cores(jnp.where(first, b, a))
            own = jnp.where(first, a, b).astype(wide) + got.astype(wide)
            sums.append(lax.psum_scatter(own, "dp", scatter_dimension=0, tiled=True))
    blocks = join_halves(block_zero, block_one, first)
    input_grad = join_halves(entry_zero, entry_one, first)

    shards = (
        sums[0][:, :wide_qkv],
        sums[0][:, wide_qkv : wide_qkv + wide_proj],
        sums[1],
        sums[2],
        sums[0][:, wide_qkv + wide_proj : wide_qkv + wide_proj + count_vectors].T,
    )
    local_sum = sum((jnp.sum(s * s) for s in shards))
    if tuned:
        global_sum = total_of(local_sum)
    else:
        global_sum = lax.psum(local_sum, ("section", "dp"))
    grad_norm = jnp.sqrt(global_sum)
    factor = clip_norm / jnp.maximum(grad_norm, clip_norm)
    firsts = (first_qkv[0], first_proj[0], first_in[0], first_out[0], first_vectors[0])
    seconds = (second_qkv[0], second_proj[0], second_in[0], second_out[0], second_vectors[0])
    rates = (rate_matrix, rate_matrix, rate_matrix, rate_matrix, rate_vector)
    decays = (decay_matrix, decay_matrix, decay_matrix, decay_matrix, 0.0)
    results = [
        adam_update(w, g, f, s, factor, r, d)
        for w, g, f, s, r, d in zip(masters, shards, firsts, seconds, rates, decays)
    ]
    news = tuple((item[0][None] for item in results))
    momenta = tuple((item[1][None] for item in results))
    variances = tuple((item[2][None] for item in results))
    copies = tuple((n.astype(low_type) for n in news))
    grads_out = tuple((s[None] for s in shards))
    return (
        blocks[None],
        input_grad[None],
        *grads_out,
        grad_norm,
        *news,
        *copies,
        *momenta,
        *variances,
    )


def solution(mesh):
    in_specs = (
        P("dp", None),
        P("dp"),
        P("dp", None),
        P("section", "dp", None),
        P("section", "dp", None),
        P("section", "dp", None),
        P("section", "dp", None),
        P("section", None, "dp"),
        P("section", "dp", None),
        P("section", "dp", None),
        P("section", "dp", None),
        P("section", "dp", None),
        P("section", None, "dp"),
        P("section", "dp", None),
        P("section", "dp", None),
        P("section", "dp", None),
        P("section", "dp", None),
        P("section", None, "dp"),
    )
    out_specs = (
        P("section", "dp", None),
        P("section", "dp", None),
        P("section", "dp", None),
        P("section", "dp", None),
        P("section", "dp", None),
        P("section", "dp", None),
        P("section", None, "dp"),
        P(),
        P("section", "dp", None),
        P("section", "dp", None),
        P("section", "dp", None),
        P("section", "dp", None),
        P("section", None, "dp"),
        P("section", "dp", None),
        P("section", "dp", None),
        P("section", "dp", None),
        P("section", "dp", None),
        P("section", None, "dp"),
        P("section", "dp", None),
        P("section", "dp", None),
        P("section", "dp", None),
        P("section", "dp", None),
        P("section", None, "dp"),
        P("section", "dp", None),
        P("section", "dp", None),
        P("section", "dp", None),
        P("section", "dp", None),
        P("section", None, "dp"),
    )
    return jax.shard_map(body, mesh=mesh, in_specs=in_specs, out_specs=out_specs, check_vma=False)
```

```python
import functools
import jax
import jax.numpy as jnp
from jax import lax
from jax.experimental import pallas as pl
from jax.experimental.pallas import tpu as pltpu
from jax.sharding import PartitionSpec as P

HEADS = 16
HEAD = 64
SEQ = 50
STEP = 10
SIDE = 4
LEVELS = 4
GROUP = 200

norm_epsilon = 1e-06
clip_norm = 1.0
beta_one = 0.9
beta_two = 0.95
rate_matrix = 0.05
rate_vector = 1.0
decay_matrix = 0.1
epsilon = 1e-08
PAD = 128
LATE = ("G30", "H30",)
ORDER = (
    "G10", "G20", "G30", "G10", "G31", "G20", "G30", "G10", "G21", "G20", "G10", "G31", "G11",
    "G21", "G31", "G20", "G11", "G21", "G30", "G10", "G20", "G11", "G10", "G21", "G30", "G20",
    "G10", "F10", "F20", "G11", "G30", "G20", "F30", "G11", "G30", "G21", "G11", "G30", "G31",
    "F40", "G21", "G11", "F11", "F21", "G21", "F31", "G31", "H31", "G31", "H31", "G31", "B21",
    "B31", "B41", "H31", "B51", "H30", "B20", "H21", "H30", "H11", "H21", "H20", "H11", "H30",
    "H21", "B30", "B40", "H11", "H30", "B50", "H10", "H20", "H21", "H10", "H21", "H31", "H20",
    "H11", "H21", "F41", "H31", "H11", "H10", "H21", "H31", "H20", "H11", "H31", "H30", "H20",
    "H11", "H10", "H30", "H20", "H10", "H30", "H20", "H10", "H10",
)
low_type = jnp.bfloat16
wide = jnp.float32


def swap_cores(x):
    return lax.ppermute(x, "section", [(0, 1), (1, 0)])


def flip(x, bit):
    count = lax.axis_size("dp")
    return lax.ppermute(x, "dp", [(i, i ^ bit) for i in range(count)])


def shift(x, levels, by):
    pairs = [
        (level * SIDE + q, (level + by) * SIDE + q) for level in levels for q in range(SIDE)
    ]
    return lax.ppermute(x, "dp", pairs)


class Line:
    def __init__(self):
        self.token = jnp.zeros((), wide)

    def sync(self, *values):
        fenced = lax.optimization_barrier((self.token, *values))
        self.token = fenced[0]
        return fenced[1:]


def swap_halves(here, there, first):
    got = swap_cores(there)
    return jnp.where(first, here, got), jnp.where(first, got, here)


def place_blocks(blocks, me, axis):
    shape = list(blocks[0].shape)
    shape.insert(axis, SIDE)
    full = jnp.zeros(shape, blocks[0].dtype)
    for relative, block in enumerate(blocks):
        start = [0] * len(shape)
        start[axis] = jnp.bitwise_xor(me, relative)
        full = lax.dynamic_update_slice(full, jnp.expand_dims(block, axis), start)
    return full


def gather_flow(line, part, level, me, key, state):
    half = LEVELS // 2
    (part,) = line.sync(part)
    ups, downs = [], []
    up = down = part
    for step in range(1, LEVELS):
        up = shift(up, range(step - 1, LEVELS - 1), 1)
        down = shift(down, range(1, LEVELS + 1 - step), -1)
        yield
        up, down = line.sync(up, down)
        ups.append(up)
        downs.append(down)
    chain = jnp.stack(ups[::-1] + [part] + downs)
    column = lax.dynamic_slice_in_dim(chain, LEVELS - 1 - level, LEVELS, axis=0)
    across = flip(column, 1)
    along = flip(column, 2)
    yield
    across, along, column = line.sync(across, along, column)
    corner_low = flip(along[:half], 1)
    corner_high = flip(across[half:], 2)
    full = place_blocks([column, across, along], me, 1)
    yield
    corner_low, corner_high, full = line.sync(corner_low, corner_high, full)
    corner = jnp.bitwise_xor(me, 3)
    full = lax.dynamic_update_slice(full, corner_low[:, None], (0, corner, 0, 0))
    full = lax.dynamic_update_slice(full, corner_high[:, None], (half, corner, 0, 0))
    mine = full.reshape(-1, part.shape[1])
    theirs = swap_cores(mine)
    yield
    state[key] = line.sync(mine, theirs)
    yield


def gather_flow_late(line, part, level, me, key, state):
    rows = part.shape[0]
    half = rows // 2
    (part,) = line.sync(part)
    across = flip(part, 1)
    along = flip(part, 2)
    yield
    across, along = line.sync(across, along)
    corner_low = flip(along[:half], 1)
    corner_high = flip(across[half:], 2)
    yield
    corner_low, corner_high = line.sync(corner_low, corner_high)
    block = place_blocks([part, across, along, jnp.concatenate([corner_low, corner_high])], me, 0)
    ups, downs = [], []
    up = down = block
    for step in range(1, LEVELS):
        up = shift(up, range(step - 1, LEVELS - 1), 1)
        down = shift(down, range(1, LEVELS + 1 - step), -1)
        yield
        up, down = line.sync(up, down)
        ups.append(up)
        downs.append(down)
    chain = jnp.stack(ups[::-1] + [block] + downs)
    full = lax.dynamic_slice_in_dim(chain, LEVELS - 1 - level, LEVELS, axis=0)
    mine = full.reshape(-1, part.shape[1])
    theirs = swap_cores(mine)
    yield
    state[key] = line.sync(mine, theirs)
    yield


def add_low(left, right):
    return (left.astype(wide) + right.astype(wide)).astype(low_type)


def pick(array, index, axis):
    last = array.shape[axis] - 1
    return lax.dynamic_index_in_dim(array, jnp.clip(index, 0, last), axis, keepdims=False)


def chip_sum(line, make_there, make_here):
    there = make_there()
    got = swap_cores(there)
    yield
    (got,) = line.sync(got)
    total = make_here(got)
    return total.reshape(LEVELS, SIDE, total.shape[0] // (LEVELS * SIDE), total.shape[1])


def scatter_flow(line, make_there, make_here, level, me, key, state):
    half = LEVELS // 2
    chip = yield from chip_sum(line, make_there, make_here)
    corner = pick(chip, jnp.bitwise_xor(me, 3), 1)
    from_across = flip(corner[:half], 1)
    from_along = flip(corner[half:], 2)
    yield
    from_across, from_along, chip = line.sync(from_across, from_along, chip)
    along = pick(chip, jnp.bitwise_xor(me, 2), 1)
    across = pick(chip, jnp.bitwise_xor(me, 1), 1)
    along = jnp.concatenate([add_low(along[:half], from_across), along[half:]])
    across = jnp.concatenate([across[:half], add_low(across[half:], from_along)])
    got_across = flip(across, 1)
    got_along = flip(along, 2)
    own = pick(chip, me, 1)
    yield
    got_across, got_along, own = line.sync(got_across, got_along, own)
    column = own.astype(wide) + got_across.astype(wide) + got_along.astype(wide)
    up = down = jnp.zeros((), wide)
    for step in range(1, LEVELS):
        far = LEVELS - step
        up = shift((pick(column, level + far, 0) + up).astype(low_type), range(0, step), 1)
        down = shift(
            (pick(column, level - far, 0) + down).astype(low_type),
            range(LEVELS - step, LEVELS),
            -1,
        )
        yield
        up, down, column = line.sync(up, down, column)
        up, down = up.astype(wide), down.astype(wide)
    state[key] = line.sync(pick(column, level, 0) + up + down)[0]
    yield


def scatter_flow_late(line, make_there, make_here, level, me, key, state):
    chip = yield from chip_sum(line, make_there, make_here)
    half = chip.shape[2] // 2
    up = down = jnp.zeros((), wide)
    for step in range(1, LEVELS):
        far = LEVELS - step
        up = shift((pick(chip, level + far, 0) + up).astype(low_type), range(0, step), 1)
        down = shift(
            (pick(chip, level - far, 0) + down).astype(low_type), range(LEVELS - step, LEVELS), -1
        )
        yield
        up, down, chip = line.sync(up, down, chip)
        up, down = up.astype(wide), down.astype(wide)
    block = pick(chip, level, 0).astype(wide) + up + down
    corner = pick(block, jnp.bitwise_xor(me, 3), 0).astype(low_type)
    from_across = flip(corner[:half], 1)
    from_along = flip(corner[half:], 2)
    yield
    from_across, from_along, block = line.sync(from_across, from_along, block)
    along = pick(block, jnp.bitwise_xor(me, 2), 0)
    across = pick(block, jnp.bitwise_xor(me, 1), 0)
    along = jnp.concatenate([along[:half] + from_across.astype(wide), along[half:]])
    across = jnp.concatenate([across[:half], across[half:] + from_along.astype(wide)])
    got_across = flip(across.astype(low_type), 1)
    got_along = flip(along.astype(low_type), 2)
    yield
    got_across, got_along, block = line.sync(got_across, got_along, block)
    total = pick(block, me, 0) + got_across.astype(wide) + got_along.astype(wide)
    state[key] = line.sync(total)[0]
    yield


def gather_plain(line, part, key, state):
    (part,) = line.sync(part)
    mine = lax.all_gather(part, "dp", axis=0, tiled=True)
    state[key] = line.sync(mine, swap_cores(mine))
    yield


def scatter_plain(line, make_there, make_here, key, state):
    (got,) = line.sync(swap_cores(make_there()))
    total = make_here(got).astype(wide)
    state[key] = line.sync(lax.psum_scatter(total, "dp", scatter_dimension=0, tiled=True))[0]
    yield


def total_of(value):
    value = value + swap_cores(value)
    across, along, corner = flip(value, 1), flip(value, 2), flip(value, 3)
    value = (value + across) + (along + corner)
    count = lax.axis_size("dp")

    def turn(by):
        pairs = [(i, (i + by * SIDE) % count) for i in range(count)]
        return lax.ppermute(value, "dp", pairs)

    one, two, three = turn(1), turn(2), turn(3)
    return (value + two) + (one + three)


def normalize(inputs):
    centered = inputs - jnp.mean(inputs, axis=-1, keepdims=True)
    inverse = lax.rsqrt(jnp.mean(centered * centered, axis=-1, keepdims=True) + norm_epsilon)
    return (centered * inverse, inverse)


def normalize_back(upstream, scaled, inverse):
    return inverse * (
        upstream
        - jnp.mean(upstream, axis=-1, keepdims=True)
        - scaled * jnp.mean(upstream * scaled, axis=-1, keepdims=True)
    )


def dot_nt(left, right):
    return lax.dot_general(left, right, (((1,), (1,)), ((), ())), preferred_element_type=wide)


def dot_nn(left, right):
    return lax.dot_general(left, right, (((1,), (0,)), ((), ())), preferred_element_type=wide)


def dot_tn(left, right):
    return lax.dot_general(left, right, (((0,), (0,)), ((), ())), preferred_element_type=wide)


def same_image(rows):
    image_row = lax.broadcasted_iota(jnp.int32, (rows, rows), 0) // SEQ
    image_col = lax.broadcasted_iota(jnp.int32, (rows, rows), 1) // SEQ
    return image_row == image_col


def attend_kernel(q_ref, k_ref, v_ref, o_ref):
    rows = q_ref.shape[1]
    mask = same_image(rows)
    lane = lax.broadcasted_iota(jnp.int32, (rows, 2 * HEAD), 1)
    queries, keys, values = q_ref[0], k_ref[0], v_ref[0]
    queries = queries * jnp.asarray(HEAD ** (-0.5), low_type)
    mixed = []
    for head in range(2):
        inside = (lane >= head * HEAD) & (lane < (head + 1) * HEAD)
        own = jnp.where(inside, queries, jnp.zeros_like(queries))
        scores = jnp.where(mask, dot_nt(own, keys), -jnp.inf)
        raised = jnp.exp(scores - jnp.max(scores, axis=1, keepdims=True))
        weights = raised * (1.0 / jnp.sum(raised, axis=1, keepdims=True))
        mixed.append(dot_nn(weights.astype(low_type), values))
    o_ref[0] = jnp.where(lane < HEAD, mixed[0], mixed[1]).astype(low_type)


def block_at(third, blocks, rows):
    return pl.BlockSpec((1, rows, 2 * HEAD), lambda i, j: (i, 0, third * blocks + j))


def attend(packed):
    rows, columns = packed.shape
    blocks = columns // 3 // (2 * HEAD)
    groups = rows // GROUP
    packed = packed.reshape(groups, GROUP, columns)
    mixed = pl.pallas_call(
        attend_kernel,
        grid=(groups, blocks),
        in_specs=[block_at(third, blocks, GROUP) for third in range(3)],
        out_specs=block_at(0, blocks, GROUP),
        out_shape=jax.ShapeDtypeStruct((groups, GROUP, columns // 3), low_type),
        cost_estimate=pl.CostEstimate(
            flops=8 * rows * GROUP * columns // 3,
            bytes_accessed=8 * rows * columns // 3,
            transcendentals=rows * GROUP * columns // 3 // HEAD,
        ),
        compiler_params=pltpu.CompilerParams(vmem_limit_bytes=32 * 1024 * 1024),
        name="attend",
    )(packed, packed, packed)
    return mixed.reshape(rows, columns // 3)


def attend_back_kernel(q_ref, k_ref, v_ref, g_ref, dq_ref, dk_ref, dv_ref):
    rows = q_ref.shape[1]
    mask = same_image(rows)
    lane = lax.broadcasted_iota(jnp.int32, (rows, 2 * HEAD), 1)
    queries, keys, values, upstream = q_ref[0], k_ref[0], v_ref[0], g_ref[0]
    scaling = HEAD ** (-0.5)
    queries = queries * jnp.asarray(scaling, low_type)
    to_queries, to_keys, to_values = [], [], []
    for head in range(2):
        inside = (lane >= head * HEAD) & (lane < (head + 1) * HEAD)
        zero = jnp.zeros_like(queries)
        own_queries = jnp.where(inside, queries, zero)
        own_upstream = jnp.where(inside, upstream, zero)
        scores = jnp.where(mask, dot_nt(keys, own_queries), -jnp.inf)
        raised = jnp.exp(scores - jnp.max(scores, axis=0, keepdims=True))
        weights = raised * (1.0 / jnp.sum(raised, axis=0, keepdims=True))
        to_values.append(dot_nn(weights.astype(low_type), upstream))
        slope = dot_nt(values, own_upstream)
        inner = jnp.sum(weights * slope, axis=0, keepdims=True)
        change = (weights * (slope - inner)).astype(low_type)
        to_keys.append(dot_nn(change, queries))
        to_queries.append(dot_tn(keys, change))
    lower = lane < HEAD
    dv_ref[0] = jnp.where(lower, to_values[0], to_values[1]).astype(low_type)
    dk_ref[0] = jnp.where(lower, to_keys[0], to_keys[1]).astype(low_type)
    turned = jnp.concatenate([to_queries[0][:HEAD], to_queries[1][HEAD:]], axis=0)
    dq_ref[0] = (turned.T * scaling).astype(low_type)


def attend_back(packed, upstream):
    rows, columns = packed.shape
    blocks = columns // 3 // (2 * HEAD)
    groups = rows // GROUP
    packed = packed.reshape(groups, GROUP, columns)
    upstream = upstream.reshape(groups, GROUP, columns // 3)
    shape = jax.ShapeDtypeStruct((groups, GROUP, columns // 3), low_type)
    slopes = pl.pallas_call(
        attend_back_kernel,
        grid=(groups, blocks),
        in_specs=[block_at(third, blocks, GROUP) for third in (0, 1, 2, 0)],
        out_specs=[block_at(0, blocks, GROUP)] * 3,
        out_shape=[shape] * 3,
        cost_estimate=pl.CostEstimate(
            flops=20 * rows * GROUP * columns // 3,
            bytes_accessed=14 * rows * columns // 3,
            transcendentals=rows * GROUP * columns // 3 // HEAD,
        ),
        compiler_params=pltpu.CompilerParams(vmem_limit_bytes=32 * 1024 * 1024),
        name="attend_back",
    )(packed, packed, packed, upstream)
    return jnp.concatenate([part.reshape(rows, columns // 3) for part in slopes], axis=1)


def dot(left, right):
    return jnp.dot(left, right, preferred_element_type=wide)


def back_dot(left, right):
    return jnp.einsum("nf,df->nd", left, right, preferred_element_type=wide)


def weight_dot(left, right):
    return jnp.einsum("nd,nf->df", left, right, preferred_element_type=wide)


def adam_update(weight, grad, first, second, factor, rate, decay):
    clipped = grad * factor
    momentum = beta_one * first + (1.0 - beta_one) * clipped
    variance = beta_two * second + (1.0 - beta_two) * clipped * clipped
    corrected_m = momentum / (1.0 - beta_one**STEP)
    corrected_v = variance / (1.0 - beta_two**STEP)
    updated = weight - rate * (corrected_m / (jnp.sqrt(corrected_v) + epsilon) + decay * weight)
    return (updated, momentum, variance)


def body(
    patches,
    live,
    cotangent,
    w_qkv,
    w_proj,
    w_in,
    w_out,
    vectors,
    first_qkv,
    first_proj,
    first_in,
    first_out,
    first_vectors,
    second_qkv,
    second_proj,
    second_in,
    second_out,
    second_vectors,
):
    core = lax.axis_index("section")
    first = core == 0
    chip = lax.axis_index("dp")
    count_dp = lax.axis_size("dp")
    tuned = count_dp == LEVELS * SIDE
    level = chip // SIDE
    me = chip % SIDE
    masters = (w_qkv[0], w_proj[0], w_in[0], w_out[0], vectors[0])
    width = patches.shape[1]
    half_width = width // 2
    hidden_width = w_in.shape[2]
    half_vectors = vectors.shape[1] // 2
    half_qkv = w_qkv.shape[2] // 2
    stripe = hidden_width // (2 * count_dp)
    tokens = patches.shape[0] // 2
    images = live.shape[0] // 2
    line = Line()
    state = {}

    def halves_of(array, groups):
        rows = array.shape[0]
        shaped = array.reshape(rows, groups, 2, -1)
        return tuple(shaped[:, :, side].reshape(rows, -1) for side in range(2))

    def choose(pair):
        return jnp.where(first, pair[0], pair[1]), jnp.where(first, pair[1], pair[0])

    def join(here, there):
        return jnp.where(
            first,
            jnp.concatenate([here, there], axis=-1),
            jnp.concatenate([there, here], axis=-1),
        )

    def prepare():
        lowered = [m.astype(low_type) for m in masters]
        qkv, proj = halves_of(lowered[0], 3), halves_of(lowered[1], 1)
        turned = lowered[4].T
        pad = jnp.zeros((turned.shape[0], PAD - half_vectors), low_type)
        packs = [
            tuple(
                jnp.concatenate(
                    [
                        qkv[side],
                        proj[side],
                        turned[:, side * half_vectors : (side + 1) * half_vectors],
                        pad,
                    ],
                    axis=1,
                )
                for side in range(2)
            ),
            halves_of(lowered[2], count_dp),
            tuple(jnp.split(lowered[3], 2, axis=0)),
        ]
        for number, pack in enumerate(packs):
            here, there = choose(pack)
            parts = swap_halves(here, there, first)
            for layer in range(2):
                state[f"part{number + 1}{layer}"] = parts[layer]
        entry = lax.dynamic_slice_in_dim(patches, core * tokens, tokens, axis=0)
        state["x0"] = entry.astype(wide)
        weighting = lax.dynamic_slice_in_dim(live, core * images, images, axis=0).astype(wide)
        target = lax.dynamic_slice_in_dim(cotangent, core * tokens, tokens, axis=0).astype(wide)
        target = target.reshape(images, SEQ, width) * weighting.reshape(images, 1, 1)
        state["dy1"] = target.reshape(tokens, width)

    def take(*names):
        values = line.sync(*[state[name] for name in names])
        state.update(zip(names, values))
        return values

    def give(**values):
        state.update(zip(values, line.sync(*values.values())))

    def two(name):
        return [f"{name}_here", f"{name}_there"]

    def split_first(layer):
        halves = state[f"G1{layer}"]
        qkv = [h[:, :half_qkv] for h in halves]
        proj = [h[:, half_qkv : half_qkv + half_width] for h in halves]
        start = half_qkv + half_width
        rows = join(*[h[:, start : start + half_vectors] for h in halves]).T.astype(wide)
        return qkv, proj, rows

    def forward_one(layer):
        (inputs,) = take(f"x{layer}")
        qkv, proj, rows = split_first(layer)
        scaled, _ = normalize(inputs)
        hidden = (scaled * rows[0] + rows[1]).astype(low_type)
        biases = [halves_of(rows[i : i + 1], 1) for i in (2, 3)]
        query_bias, value_bias = [choose(pair) for pair in biases]
        packed = []
        for side in range(2):
            zero = jnp.zeros_like(query_bias[side])
            bias = jnp.concatenate([query_bias[side], zero, value_bias[side]], axis=1)
            packed.append((dot(hidden, qkv[side]) + bias).astype(low_type))
        give(
            **{
                f"rows{layer}": rows,
                f"hidden{layer}": hidden,
                f"packed_here{layer}": packed[0],
                f"packed_there{layer}": packed[1],
            }
        )

    def forward_two(layer):
        here, there, rows, inputs = take(
            f"packed_here{layer}", f"packed_there{layer}", f"rows{layer}", f"x{layer}"
        )
        _, proj, _ = split_first(layer)
        mixed = join(attend(here), attend(there))
        branch = join(*[dot(mixed, w) for w in proj])
        middle = inputs + (branch + rows[4])
        scaled, _ = normalize(middle)
        hidden = (scaled * rows[5] + rows[6]).astype(low_type)
        give(**{f"mixed{layer}": mixed, f"middle{layer}": middle, f"hidden_two{layer}": hidden})

    def forward_three(layer):
        hidden, rows = take(f"hidden_two{layer}", f"rows{layer}")
        bias = choose(halves_of(rows[8:12].reshape(1, -1), count_dp))
        out = {}
        for side, name in enumerate(("here", "there")):
            pre_act = dot(hidden, state[f"G2{layer}"][side]) + bias[side]
            cdf = 0.5 * (1.0 + lax.erf(pre_act * 0.7071067811865476))
            density = jnp.exp(-0.5 * pre_act * pre_act) * 0.3989422804014327
            out[f"active_{name}{layer}"] = (pre_act * cdf).astype(low_type)
            out[f"slope_{name}{layer}"] = (cdf + pre_act * density).astype(low_type)
        give(**out)

    def forward_four(layer):
        here, there, middle, rows = take(
            f"active_here{layer}", f"active_there{layer}", f"middle{layer}", f"rows{layer}"
        )
        weights = state[f"G3{layer}"]
        output = middle + (dot(here, weights[0]) + dot(there, weights[1]) + rows[7])
        output = output.astype(low_type)
        give(**{f"block{layer}": output, f"x{layer + 1}": output.astype(wide)})

    def out_grad(layer, side):
        def make(got=None):
            name = "here" if side == 0 else "there"
            active, upstream = take(f"active_{name}{layer}", f"dy{layer}")
            grad = weight_dot(active, upstream.astype(low_type))
            return finish(grad, got)

        return make

    def finish(grad, got):
        if got is not None:
            grad = grad + got.astype(wide)
        return line.sync(grad.astype(low_type))[0]

    def in_grad(layer, side):
        def make(got=None):
            name = "here" if side == 0 else "there"
            hidden, grad_pre = take(f"hidden_two{layer}", f"grad_pre_{name}{layer}")
            return finish(weight_dot(hidden, grad_pre), got)

        return make

    def first_grad(layer, side):
        def make(got=None):
            name = "here" if side == 0 else "there"
            hidden, grad_packed, mixed, branch, rows = take(
                f"hidden{layer}",
                f"grad_packed_{name}{layer}",
                f"mixed{layer}",
                f"grad_branch_{name}{layer}",
                f"grad_rows{layer}",
            )
            parts = jnp.split(rows, 2, axis=0)
            turned = choose(parts)[side].T
            turned = jnp.pad(turned, ((0, 0), (0, PAD - half_vectors)))
            grads = [weight_dot(hidden, grad_packed), weight_dot(mixed, branch), turned]
            if got is not None:
                start = half_qkv + half_width
                cuts = (got[:, :half_qkv], got[:, half_qkv:start], got[:, start:])
                grads = [a + b.astype(wide) for a, b in zip(grads, cuts)]
            return line.sync(jnp.concatenate([g.astype(low_type) for g in grads], axis=1))[0]

        return make

    def backward_two(layer):
        (upstream,) = take(f"dy{layer}")
        upstream_low = upstream.astype(low_type)
        out = {}
        sums = []
        for side, name in enumerate(("here", "there")):
            (slope,) = take(f"slope_{name}{layer}")
            grad_active = back_dot(upstream_low, state[f"G3{layer}"][side])
            grad_pre = (grad_active * slope.astype(wide)).astype(low_type)
            out[f"grad_pre_{name}{layer}"] = grad_pre
            sums.append(jnp.sum(grad_pre.astype(wide), axis=0))
        give(**out)
        state[f"bias_in{layer}"] = sums
        state[f"bias_out{layer}"] = jnp.sum(upstream_low.astype(wide), axis=0)

    def backward_three(layer):
        here, there, middle, rows, upstream = take(
            f"grad_pre_here{layer}",
            f"grad_pre_there{layer}",
            f"middle{layer}",
            f"rows{layer}",
            f"dy{layer}",
        )
        weights = state[f"G2{layer}"]
        _, proj, _ = split_first(layer)
        scaled, inverse = normalize(middle)
        grad_hidden = back_dot(here, weights[0]) + back_dot(there, weights[1])
        gain, bias = jnp.sum(grad_hidden * scaled, axis=0), jnp.sum(grad_hidden, axis=0)
        grad_middle = upstream + normalize_back(grad_hidden * rows[5], scaled, inverse)
        branch = grad_middle.astype(low_type)
        sides = choose(halves_of(branch, 1))
        grad_mixed = back_dot(sides[0], proj[0]) + back_dot(sides[1], proj[1])
        mixed_sides = choose(halves_of(grad_mixed.astype(low_type), 1))
        state[f"norm_two{layer}"] = (gain, bias, jnp.sum(branch.astype(wide), axis=0))
        give(
            **{
                f"grad_middle{layer}": grad_middle,
                f"grad_branch_here{layer}": sides[0],
                f"grad_branch_there{layer}": sides[1],
                f"grad_mixed_here{layer}": mixed_sides[0],
                f"grad_mixed_there{layer}": mixed_sides[1],
            }
        )

    def backward_four(layer):
        out = {}
        for name in ("here", "there"):
            packed, upstream = take(f"packed_{name}{layer}", f"grad_mixed_{name}{layer}")
            out[f"grad_packed_{name}{layer}"] = attend_back(packed, upstream)
        give(**out)

    def backward_five(layer):
        here, there, inputs, rows, grad_middle = take(
            f"grad_packed_here{layer}",
            f"grad_packed_there{layer}",
            f"x{layer}",
            f"rows{layer}",
            f"grad_middle{layer}",
        )
        qkv, _, _ = split_first(layer)
        scaled, inverse = normalize(inputs)
        grad_hidden = back_dot(here, qkv[0]) + back_dot(there, qkv[1])
        gain, bias = jnp.sum(grad_hidden * scaled, axis=0), jnp.sum(grad_hidden, axis=0)
        grad_entry = grad_middle + normalize_back(grad_hidden * rows[0], scaled, inverse)
        grad_entry = grad_entry.astype(low_type)
        third = half_qkv // 3
        columns = [jnp.sum(side.astype(wide), axis=0)[None] for side in (here, there)]
        query = join(*[c[:, :third] for c in columns])[0]
        value = join(*[c[:, 2 * third :] for c in columns])[0]
        gain_two, bias_two, bias_proj = state[f"norm_two{layer}"]
        bias_in = jnp.where(
            first,
            jnp.stack([s.reshape(count_dp, stripe) for s in state[f"bias_in{layer}"]], axis=1),
            jnp.stack([s.reshape(count_dp, stripe) for s in state[f"bias_in{layer}"][::-1]], axis=1),
        )
        grad_rows = jnp.stack(
            [gain, bias, query, value, bias_proj, gain_two, bias_two, state[f"bias_out{layer}"]]
        )
        grad_rows = jnp.concatenate([grad_rows, bias_in.reshape(4, width)], axis=0)
        give(**{f"entry{layer}": grad_entry, f"grad_rows{layer}": grad_rows})
        if layer == 1:
            state["dy0"] = state["entry1"].astype(wide)

    steps = {
        "F1": forward_one,
        "F2": forward_two,
        "F3": forward_three,
        "F4": forward_four,
        "B2": backward_two,
        "B3": backward_three,
        "B4": backward_four,
        "B5": backward_five,
    }
    makers = {"1": first_grad, "2": in_grad, "3": out_grad}
    prepare()
    flows = {}
    for layer in range(2):
        for number in "123":
            key = f"G{number}{layer}"
            part = state[f"part{number}{layer}"]
            if not tuned:
                flows[key] = gather_plain(line, part, key, state)
            elif key in LATE:
                flows[key] = gather_flow_late(line, part, level, me, key, state)
            else:
                flows[key] = gather_flow(line, part, level, me, key, state)
            key = f"H{number}{layer}"
            there, here = makers[number](layer, 1), makers[number](layer, 0)
            if not tuned:
                flows[key] = scatter_plain(line, there, here, key, state)
            elif key in LATE:
                flows[key] = scatter_flow_late(line, there, here, level, me, key, state)
            else:
                flows[key] = scatter_flow(line, there, here, level, me, key, state)
    for event in ORDER:
        if event in flows:
            next(flows[event], None)
        else:
            steps[event[:2]](int(event[2]))
    for key in flows:
        for _ in flows[key]:
            pass

    halves = [[state[f"H{number}{layer}"] for layer in range(2)] for number in "123"]
    local_sum = sum((jnp.sum(part * part) for pair in halves for part in pair))
    if tuned:
        global_sum = total_of(local_sum)
    else:
        global_sum = lax.psum(local_sum, ("section", "dp"))
    grad_norm = jnp.sqrt(global_sum)
    factor = clip_norm / jnp.maximum(grad_norm, clip_norm)

    def own_layer(pair):
        got = swap_cores(jnp.where(first, pair[1], pair[0]))
        mine = jnp.where(first, pair[0], pair[1])
        return jnp.where(first, mine, got), jnp.where(first, got, mine)

    def woven(pair, groups):
        rows = pair[0].shape[0]
        return jnp.stack([p.reshape(rows, groups, -1) for p in pair], axis=2).reshape(rows, -1)

    one, inner, outer = [own_layer(pair) for pair in halves]
    start = half_qkv + half_width
    shards = (
        woven([p[:, :half_qkv] for p in one], 3),
        jnp.concatenate([p[:, half_qkv:start] for p in one], axis=1),
        woven(inner, count_dp),
        jnp.concatenate(outer, axis=0),
        jnp.concatenate([p[:, start : start + half_vectors] for p in one], axis=1).T,
    )

    def own_tokens(zero, one):
        got = swap_cores(jnp.where(first, one, zero))
        mine = jnp.where(first, zero, one)
        return jnp.where(
            first, jnp.concatenate([mine, got], axis=0), jnp.concatenate([got, mine], axis=0)
        )

    blocks = own_tokens(state["block0"], state["block1"])
    input_grad = own_tokens(state["entry0"], state["entry1"])
    firsts = (first_qkv[0], first_proj[0], first_in[0], first_out[0], first_vectors[0])
    seconds = (second_qkv[0], second_proj[0], second_in[0], second_out[0], second_vectors[0])
    rates = (rate_matrix, rate_matrix, rate_matrix, rate_matrix, rate_vector)
    decays = (decay_matrix, decay_matrix, decay_matrix, decay_matrix, 0.0)
    results = [
        adam_update(w, g, f, s, factor, r, d)
        for w, g, f, s, r, d in zip(masters, shards, firsts, seconds, rates, decays)
    ]
    news = tuple((item[0][None] for item in results))
    momenta = tuple((item[1][None] for item in results))
    variances = tuple((item[2][None] for item in results))
    copies = tuple((n.astype(low_type) for n in news))
    grads_out = tuple((s[None] for s in shards))
    return (
        blocks[None],
        input_grad[None],
        *grads_out,
        grad_norm,
        *news,
        *copies,
        *momenta,
        *variances,
    )


def solution(mesh):
    in_specs = (
        P("dp", None),
        P("dp"),
        P("dp", None),
        P("section", "dp", None),
        P("section", "dp", None),
        P("section", "dp", None),
        P("section", "dp", None),
        P("section", None, "dp"),
        P("section", "dp", None),
        P("section", "dp", None),
        P("section", "dp", None),
        P("section", "dp", None),
        P("section", None, "dp"),
        P("section", "dp", None),
        P("section", "dp", None),
        P("section", "dp", None),
        P("section", "dp", None),
        P("section", None, "dp"),
    )
    out_specs = (
        P("section", "dp", None),
        P("section", "dp", None),
        P("section", "dp", None),
        P("section", "dp", None),
        P("section", "dp", None),
        P("section", "dp", None),
        P("section", None, "dp"),
        P(),
        P("section", "dp", None),
        P("section", "dp", None),
        P("section", "dp", None),
        P("section", "dp", None),
        P("section", None, "dp"),
        P("section", "dp", None),
        P("section", "dp", None),
        P("section", "dp", None),
        P("section", "dp", None),
        P("section", None, "dp"),
        P("section", "dp", None),
        P("section", "dp", None),
        P("section", "dp", None),
        P("section", "dp", None),
        P("section", None, "dp"),
        P("section", "dp", None),
        P("section", "dp", None),
        P("section", "dp", None),
        P("section", "dp", None),
        P("section", None, "dp"),
    )
    return jax.shard_map(body, mesh=mesh, in_specs=in_specs, out_specs=out_specs, check_vma=False)
```

```python
import functools
import jax
import jax.numpy as jnp
from jax import lax
from jax.experimental import pallas as pl
from jax.experimental.pallas import tpu as pltpu
from jax.sharding import Mesh
from jax.sharding import PartitionSpec as P

HEAD = 64
SEQ = 50
STEP = 10
SIDE = 4
LEVELS = 4
GROUP = 200
SLABS = 16
TILE = 512
STEPS = 4
VMEM_MB = 48
SECTION = "section"
DP = ("z", "y", "x")
X, Y, Z = DP[2], DP[1], DP[0]
GATHERS = ((10, 0, 1), (20,), (30,), (11,), (21,), (31,))
SCATTERS = ((31,), (21,), (11,), (30,), (20,), (10,))
LATE_GATHERS = ()
LATE_SCATTERS = ()
ORDER = (
    101, 102, 104, 105, 100, 101, 103, 100, 102, 101, 100, 101, 103, 100, 100, 10,
    20, 102, 103, 102, 104, 103, 101, 30, 104, 102, 40, 104, 103, 105, 11, 21,
    105, 105, 104, 31, 331, 105, 621, 631, 200, 641, 200, 651, 311, 202, 620, 200,
    202, 321, 320, 201, 200, 204, 202, 630, 204, 640, 201, 202, 204, 330, 203, 650,
    201, 204, 203, 310, 205, 203, 201, 205, 41, 203, 402, 205, 403, 500, 205,
)

norm_epsilon = 1e-06
clip_norm = 1.0
beta_one = 0.9
beta_two = 0.95
rate_matrix = 0.05
rate_vector = 1.0
decay_matrix = 0.1
epsilon = 1e-08
low_type = jnp.bfloat16
wide = jnp.float32


def swap_cores(x):
    return lax.ppermute(x, SECTION, [(0, 1), (1, 0)])


def flip(x, axis):
    return lax.ppermute(x, axis, [(0, 1), (1, 0)])


class Line:
    def __init__(self):
        self.token = jnp.zeros((), wide)

    def sync(self, *values):
        fenced = lax.optimization_barrier((self.token, *values))
        self.token = fenced[0]
        return fenced[1:]


class Layer:
    def __init__(self):
        self.weights = {}
        self.chip_grads = {}
        self.grads = {}


def swap_halves(here, there, first):
    got = swap_cores(there)
    return jnp.where(first, here, got), jnp.where(first, got, here)


def place_blocks(blocks, me, axis):
    shape = list(blocks[0].shape)
    shape.insert(axis, SIDE)
    full = jnp.zeros(shape, blocks[0].dtype)
    for relative, block in enumerate(blocks):
        start = [0] * len(shape)
        start[axis] = jnp.bitwise_xor(me, relative)
        full = lax.dynamic_update_slice(full, jnp.expand_dims(block, axis), start)
    return full


def add_low(left, right):
    return (left.astype(wide) + right.astype(wide)).astype(low_type)


def pick(array, index, axis):
    last = array.shape[axis] - 1
    return lax.dynamic_index_in_dim(array, jnp.clip(index, 0, last), axis, keepdims=False)


def gather_flow(line, parts, me, keys, layers):
    half = LEVELS // 2
    counts = [part.shape[0] for part in parts]
    extras = {}
    while keys[-1] < 10:
        extras[keys[-1]] = (sum(counts[: len(keys) - 1]), counts[len(keys) - 1])
        keys = keys[:-1]
    counts = counts[: len(keys) - 1] + [sum(counts[len(keys) - 1 :])]
    (part,) = line.sync(jnp.concatenate(parts, axis=0))
    column = lax.all_gather(part, Z, axis=0, tiled=False)
    yield
    (column,) = line.sync(column)
    across = flip(column, X)
    along = flip(column, Y)
    yield
    across, along, column = line.sync(across, along, column)
    corner_low, corner_high = line.sync(along[:half], across[half:])
    corner_low = flip(corner_low, X)
    corner_high = flip(corner_high, Y)
    fulls = []
    start = 0
    for count in counts:
        stop = start + count
        fulls.append(
            place_blocks([piece[:, start:stop] for piece in (column, across, along)], me, 1)
        )
        start = stop
    fulls = line.sync(*fulls)
    yield
    corner_low, corner_high, *fulls = line.sync(corner_low, corner_high, *fulls)
    corner = jnp.bitwise_xor(me, 3)
    start = 0
    for key, count, full in zip(keys, counts, fulls):
        stop = start + count
        full = lax.dynamic_update_slice(full, corner_low[:, None, start:stop], (0, corner, 0, 0))
        full = lax.dynamic_update_slice(
            full, corner_high[:, None, start:stop], (half, corner, 0, 0)
        )
        start = stop
        (own,) = line.sync(full.reshape(LEVELS * SIDE, count, -1))
        for name, (row, size) in extras.items():
            layers[name].spread = own[:, row : row + size]
        other = swap_cores(own)
        yield
        layers[key % 10].weights[key // 10] = line.sync(own, other)
    yield


def gather_flow_late(line, parts, me, keys, layers):
    (part,) = line.sync(*parts)
    half = part.shape[0] // 2
    across = flip(part, X)
    along = flip(part, Y)
    yield
    across, along = line.sync(across, along)
    corner_low, corner_high = line.sync(along[:half], across[half:])
    corner_low = flip(corner_low, X)
    corner_high = flip(corner_high, Y)
    yield
    corner_low, corner_high = line.sync(corner_low, corner_high)
    block = place_blocks([part, across, along, jnp.concatenate([corner_low, corner_high])], me, 0)
    (block,) = line.sync(block)
    full = lax.all_gather(block, Z, axis=0, tiled=False)
    yield
    (own,) = line.sync(full.reshape(LEVELS * SIDE, *part.shape))
    other = swap_cores(own)
    yield
    layers[keys[0] % 10].weights[keys[0] // 10] = line.sync(own, other)
    yield


def scatter_flow(line, me, keys, layers):
    half = LEVELS // 2
    chips = [layers[key % 10].chip_grads[key // 10] for key in keys]
    chips = [chip.reshape(LEVELS, SIDE, *chip.shape[1:]) for chip in chips]
    counts = [chip.shape[2] for chip in chips]

    def toward(relative):
        to = jnp.bitwise_xor(me, relative)
        return jnp.concatenate([pick(chip, to, 1) for chip in chips], axis=1)

    chips = line.sync(*chips)
    corner = toward(3)
    from_across, from_along = line.sync(corner[:half], corner[half:])
    from_across = flip(from_across, X)
    from_along = flip(from_along, Y)
    yield
    from_across, from_along, *chips = line.sync(from_across, from_along, *chips)
    along, across = toward(2), toward(1)
    along = jnp.concatenate([add_low(along[:half], from_across), along[half:]])
    across = jnp.concatenate([across[:half], add_low(across[half:], from_along)])
    across, along = line.sync(across, along)
    got_across = flip(across, X)
    got_along = flip(along, Y)
    own = toward(0)
    yield
    got_across, got_along, own = line.sync(got_across, got_along, own)
    column = own.astype(wide) + got_across.astype(wide) + got_along.astype(wide)
    (column,) = line.sync(column.astype(low_type))
    total = lax.psum_scatter(column, Z, scatter_dimension=0, tiled=False)
    yield
    (total,) = line.sync(total)
    total = total.astype(wide)
    start = 0
    for key, count in zip(keys, counts):
        layers[key % 10].grads[key // 10] = total[start : start + count]
        start += count
    yield


def scatter_flow_late(line, me, keys, layers):
    chip = layers[keys[0] % 10].chip_grads[keys[0] // 10]
    (chip,) = line.sync(chip.reshape(LEVELS, SIDE, *chip.shape[1:]))
    half = chip.shape[2] // 2
    block = lax.psum_scatter(chip, Z, scatter_dimension=0, tiled=False)
    yield
    (block,) = line.sync(block)

    def toward(relative):
        return pick(block, jnp.bitwise_xor(me, relative), 0)

    corner = toward(3)
    from_across, from_along = line.sync(corner[:half], corner[half:])
    from_across = flip(from_across, X)
    from_along = flip(from_along, Y)
    yield
    from_across, from_along = line.sync(from_across, from_along)
    along, across = toward(2), toward(1)
    along = jnp.concatenate([add_low(along[:half], from_across), along[half:]])
    across = jnp.concatenate([across[:half], add_low(across[half:], from_along)])
    across, along = line.sync(across, along)
    got_across = flip(across, X)
    got_along = flip(along, Y)
    yield
    got_across, got_along = line.sync(got_across, got_along)
    total = toward(0).astype(wide) + got_across.astype(wide) + got_along.astype(wide)
    layers[keys[0] % 10].grads[keys[0] // 10] = line.sync(total)[0]
    yield


def total_of(line, value):
    (value,) = line.sync(value + swap_cores(value))
    value = value + flip(value, X)
    value = value + flip(value, Y)
    for bit in (1, 2):
        pairs = [(i, i ^ bit) for i in range(LEVELS)]
        value = value + lax.ppermute(value, Z, pairs)
    return value


def normalize(inputs):
    centered = inputs - jnp.mean(inputs, axis=-1, keepdims=True)
    inverse = lax.rsqrt(jnp.mean(centered * centered, axis=-1, keepdims=True) + norm_epsilon)
    return (centered * inverse, inverse)


def normalize_back(upstream, scaled, inverse):
    return inverse * (
        upstream
        - jnp.mean(upstream, axis=-1, keepdims=True)
        - scaled * jnp.mean(upstream * scaled, axis=-1, keepdims=True)
    )


def dot_nt(left, right):
    return lax.dot_general(left, right, (((1,), (1,)), ((), ())), preferred_element_type=wide)


def dot_nn(left, right):
    return lax.dot_general(left, right, (((1,), (0,)), ((), ())), preferred_element_type=wide)


def dot_tn(left, right):
    return lax.dot_general(left, right, (((0,), (0,)), ((), ())), preferred_element_type=wide)


def same_image(rows):
    image_row = lax.broadcasted_iota(jnp.int32, (rows, rows), 0) // SEQ
    image_col = lax.broadcasted_iota(jnp.int32, (rows, rows), 1) // SEQ
    return image_row == image_col


def attend_kernel(q_ref, k_ref, v_ref, o_ref):
    rows, columns = q_ref.shape[1:]
    mask = same_image(rows)
    lane = lax.broadcasted_iota(jnp.int32, (rows, 2 * HEAD), 1)
    for start in range(0, columns, 2 * HEAD):
        place = pl.ds(start, 2 * HEAD)
        queries, keys, values = q_ref[0, :, place], k_ref[0, :, place], v_ref[0, :, place]
        queries = queries * jnp.asarray(HEAD ** (-0.5), low_type)
        mixed = []
        for head in range(2):
            inside = (lane >= head * HEAD) & (lane < (head + 1) * HEAD)
            own = jnp.where(inside, queries, jnp.zeros_like(queries))
            scores = jnp.where(mask, dot_nt(own, keys), -jnp.inf)
            raised = jnp.exp(scores - jnp.max(scores, axis=1, keepdims=True))
            weights = raised * (1.0 / jnp.sum(raised, axis=1, keepdims=True))
            mixed.append(dot_nn(weights.astype(low_type), values))
        o_ref[0, :, place] = jnp.where(lane < HEAD, mixed[0], mixed[1]).astype(low_type)


def third_at(third, rows, columns):
    return pl.BlockSpec((1, rows, columns), lambda i: (i, 0, third))


def attend(packed):
    sides, rows, columns = packed.shape
    groups, width = sides * rows // GROUP, columns // 3
    packed = packed.reshape(groups, GROUP, columns)
    mixed = pl.pallas_call(
        attend_kernel,
        grid=(groups,),
        in_specs=[third_at(third, GROUP, width) for third in range(3)],
        out_specs=third_at(0, GROUP, width),
        out_shape=jax.ShapeDtypeStruct((groups, GROUP, width), low_type),
        cost_estimate=cost(8 * sides * rows * GROUP * width, 8 * sides * rows * width),
        compiler_params=limits(),
        name="attend",
    )(packed, packed, packed)
    return mixed.reshape(sides, rows, width)


def attend_back_kernel(q_ref, k_ref, v_ref, g_ref, b_ref, d_ref):
    rows, columns = q_ref.shape[1:]
    mask = same_image(rows)
    lane = lax.broadcasted_iota(jnp.int32, (rows, 2 * HEAD), 1)
    scaling = HEAD ** (-0.5)
    lower = lane < HEAD
    d_ref[0, :, pl.ds(3 * columns, columns)] = b_ref[0]
    for start in range(0, columns, 2 * HEAD):
        place = pl.ds(start, 2 * HEAD)
        queries, keys, values = q_ref[0, :, place], k_ref[0, :, place], v_ref[0, :, place]
        upstream = g_ref[0, :, place]
        queries = queries * jnp.asarray(scaling, low_type)
        to_queries, to_keys, to_values = [], [], []
        for head in range(2):
            inside = (lane >= head * HEAD) & (lane < (head + 1) * HEAD)
            zero = jnp.zeros_like(queries)
            own_queries = jnp.where(inside, queries, zero)
            own_upstream = jnp.where(inside, upstream, zero)
            scores = jnp.where(mask, dot_nt(keys, own_queries), -jnp.inf)
            raised = jnp.exp(scores - jnp.max(scores, axis=0, keepdims=True))
            weights = raised * (1.0 / jnp.sum(raised, axis=0, keepdims=True))
            to_values.append(dot_nn(weights.astype(low_type), upstream))
            slope = dot_nt(values, own_upstream)
            inner = jnp.sum(weights * slope, axis=0, keepdims=True)
            change = (weights * (slope - inner)).astype(low_type)
            to_keys.append(dot_nn(change, queries))
            to_queries.append(dot_tn(keys, change))
        turned = jnp.concatenate([to_queries[0][:HEAD], to_queries[1][HEAD:]], axis=0)
        d_ref[0, :, place] = (turned.T * scaling).astype(low_type)
        keys_place = pl.ds(columns + start, 2 * HEAD)
        d_ref[0, :, keys_place] = jnp.where(lower, to_keys[0], to_keys[1]).astype(low_type)
        values_place = pl.ds(2 * columns + start, 2 * HEAD)
        d_ref[0, :, values_place] = jnp.where(lower, to_values[0], to_values[1]).astype(low_type)


def attend_back(packed, upstream, branch):
    sides, rows, columns = packed.shape
    groups, width = sides * rows // GROUP, columns // 3
    packed = packed.reshape(groups, GROUP, columns)
    upstream = upstream.reshape(groups, GROUP, width)
    branch = branch.reshape(groups, GROUP, width)
    total = columns + width
    slopes = pl.pallas_call(
        attend_back_kernel,
        grid=(groups,),
        in_specs=[third_at(third, GROUP, width) for third in (0, 1, 2, 0, 0)],
        out_specs=pl.BlockSpec((1, GROUP, total), lambda i: (i, 0, 0)),
        out_shape=jax.ShapeDtypeStruct((groups, GROUP, total), low_type),
        cost_estimate=cost(20 * sides * rows * GROUP * width, 14 * sides * rows * width),
        compiler_params=limits(),
        name="attend_back",
    )(packed, packed, packed, upstream, branch)
    return slopes.reshape(sides, rows, total)


def limits():
    return pltpu.CompilerParams(vmem_limit_bytes=VMEM_MB * 1024 * 1024)


def cost(flops, moved, special=0):
    return pl.CostEstimate(flops=flops, bytes_accessed=moved, transcendentals=special)


def early(count):
    return lambda i: jnp.minimum(i, count - 1)


def late(count):
    return lambda i: jnp.maximum(i - count, 0)


def tile_spec(width, first, turn):
    per = width // TILE

    def at(i):
        tile = first + turn(i)
        return (0, tile // per, tile % per)

    return pl.BlockSpec((SLABS, width // SLABS, TILE), at)


def side_spec(count, *shape):
    return pl.BlockSpec((1, *shape), lambda i: (i // count, 0, i % count))


def flat(ref):
    return ref[...].reshape(ref.shape[0] * ref.shape[1], ref.shape[2])


def project_kernel(smooth, count, x_ref, here_ref, there_ref, b_ref, *outs):
    def work(w_ref):
        total = dot_nn(x_ref[...], flat(w_ref)) + b_ref[0]
        if smooth:
            cdf = 0.5 * (1.0 + lax.erf(total * 0.7071067811865476))
            density = jnp.exp(-0.5 * total * total) * 0.3989422804014327
            outs[0][0] = (total * cdf).astype(low_type)
            outs[1][0] = (cdf + total * density).astype(low_type)
        else:
            outs[0][0] = total.astype(outs[0].dtype)

    i = pl.program_id(0)
    pl.when(i < count)(lambda: work(here_ref))
    pl.when(i >= count)(lambda: work(there_ref))


def project(x, weights, first, count, bias, kind, smooth=False):
    rows, depth = x.shape
    number = 2 if smooth else 1
    return pl.pallas_call(
        functools.partial(project_kernel, smooth, count),
        grid=(2 * count,),
        in_specs=[
            pl.BlockSpec((rows, depth), lambda i: (0, 0)),
            tile_spec(depth, first, early(count)),
            tile_spec(depth, first, late(count)),
            side_spec(count, 1, TILE),
        ],
        out_specs=[side_spec(count, rows, TILE)] * number,
        out_shape=[jax.ShapeDtypeStruct((2, rows, count * TILE), kind)] * number,
        cost_estimate=cost(4 * rows * depth * count * TILE, 4 * depth * count * TILE),
        compiler_params=limits(),
        name="project",
    )(x, *weights, bias)


def output_kernel(active_ref, w_here, w_there, middle_ref, b_ref, o_ref):
    total = dot_nn(active_ref[0], flat(w_here)) + dot_nn(active_ref[1], flat(w_there))
    o_ref[...] = (total + middle_ref[...] + b_ref[...]).astype(low_type)


def output_rows(active, weights, middle, bias):
    _, rows, depth = active.shape
    width = middle.shape[1]
    tile = width // STEPS
    weight = pl.BlockSpec((SLABS, depth // SLABS, tile), lambda i: (0, 0, i))
    part = pl.BlockSpec((rows, tile), lambda i: (0, i))
    return pl.pallas_call(
        output_kernel,
        grid=(STEPS,),
        in_specs=[
            pl.BlockSpec(active.shape, lambda i: (0, 0, 0)),
            weight,
            weight,
            part,
            pl.BlockSpec((1, tile), lambda i: (0, i)),
        ],
        out_specs=part,
        out_shape=jax.ShapeDtypeStruct((rows, width), low_type),
        cost_estimate=cost(4 * rows * depth * width, 4 * depth * width),
        compiler_params=limits(),
        name="output",
    )(active, *weights, middle, bias)


def active_grad_kernel(count, up_ref, w_here, w_there, slope_ref, o_ref, sum_ref):
    def work(w_ref):
        low = (dot_nt(up_ref[...], flat(w_ref)) * slope_ref[0].astype(wide)).astype(low_type)
        o_ref[0] = low
        sum_ref[0] = jnp.sum(low.astype(wide), axis=0, keepdims=True)

    i = pl.program_id(0)
    pl.when(i < count)(lambda: work(w_here))
    pl.when(i >= count)(lambda: work(w_there))


def active_grad(upstream, weights, slope):
    rows, width = upstream.shape
    depth = slope.shape[2]
    count = depth // TILE
    slabs = SLABS // count

    def weight(turn):
        return pl.BlockSpec((slabs, depth // SLABS, width), lambda i: (turn(i), 0, 0))

    return pl.pallas_call(
        functools.partial(active_grad_kernel, count),
        grid=(2 * count,),
        in_specs=[
            pl.BlockSpec((rows, width), lambda i: (0, 0)),
            weight(early(count)),
            weight(late(count)),
            side_spec(count, rows, TILE),
        ],
        out_specs=[side_spec(count, rows, TILE), side_spec(count, 1, TILE)],
        out_shape=[
            jax.ShapeDtypeStruct((2, rows, depth), low_type),
            jax.ShapeDtypeStruct((2, 1, depth), wide),
        ],
        cost_estimate=cost(4 * rows * depth * width, 6 * depth * width),
        compiler_params=limits(),
        name="active",
    )(upstream, *weights, slope)


def back_tile(left, packed, depth):
    slabs, _, width = packed.shape
    rows = width // SLABS
    total = None
    for block in range(2):
        count = min(depth - block * width, width)
        part = packed[:, pl.ds(block * rows, rows), pl.ds(0, count)].reshape(slabs * rows, count)
        term = dot_nt(left[:, pl.ds(block * width, count)], part)
        total = term if total is None else total + term
    return total


def middle_grad_kernel(place, *refs):
    left, w_here, w_there, middle, gain, up, proj_here, proj_there = refs[:8]
    o_middle, o_branch, o_mixed, sums, acc = refs[8:]
    i = pl.program_id(0)
    tile = acc.shape[1] // STEPS
    columns = pl.ds(pl.multiple_of(i * tile, tile), tile)
    depth = left.shape[2]
    acc[:, columns] = back_tile(left.at[0], w_here, depth) + back_tile(left.at[1], w_there, depth)

    @pl.when(i == STEPS - 1)
    def _():
        first = place[0] == 0
        grad = acc[...]
        scaled, inverse = normalize(middle[...])
        sums[0:1] = jnp.sum(grad * scaled, axis=0, keepdims=True)
        sums[1:2] = jnp.sum(grad, axis=0, keepdims=True)
        total = up[...].astype(wide) + normalize_back(grad * gain[...], scaled, inverse)
        o_middle[...] = total
        branch = total.astype(low_type)
        sums[2:3] = jnp.sum(branch.astype(wide), axis=0, keepdims=True)
        width = branch.shape[1] // 2
        near = jnp.where(first, branch[:, :width], branch[:, width:])
        far = jnp.where(first, branch[:, width:], branch[:, :width])
        o_branch[0] = near
        o_branch[1] = far
        mixed = dot_nt(near, flat(proj_here)) + dot_nt(far, flat(proj_there))
        mixed = mixed.astype(low_type)
        o_mixed[0] = jnp.where(first, mixed[:, :width], mixed[:, width:])
        o_mixed[1] = jnp.where(first, mixed[:, width:], mixed[:, :width])


def few_slabs(width):
    return pl.BlockSpec((SLABS // STEPS, 2 * width // SLABS, width), lambda i: (i, 0, 0))


def middle_grad(place, left, weights, middle, gain, upstream, firsts):
    rows, width = middle.shape
    depth = left.shape[2]
    whole = pl.BlockSpec((rows, width), lambda i: (0, 0))
    pair = pl.BlockSpec((2, rows, width // 2), lambda i: (0, 0, 0))
    halves = jax.ShapeDtypeStruct((2, rows, width // 2), low_type)
    return pl.pallas_call(
        middle_grad_kernel,
        grid=(STEPS,),
        in_specs=[
            pl.BlockSpec(memory_space=pltpu.SMEM),
            pl.BlockSpec(left.shape, lambda i: (0, 0, 0)),
            few_slabs(width),
            few_slabs(width),
            whole,
            pl.BlockSpec((1, width), lambda i: (0, 0)),
            whole,
            tile_spec(width, 3, lambda i: 0),
            tile_spec(width, 3, lambda i: 0),
        ],
        out_specs=[whole, pair, pair, pl.BlockSpec((8, width), lambda i: (0, 0))],
        out_shape=[
            jax.ShapeDtypeStruct((rows, width), wide),
            halves,
            halves,
            jax.ShapeDtypeStruct((8, width), wide),
        ],
        scratch_shapes=[pltpu.VMEM((rows, width), wide)],
        cost_estimate=cost(4 * rows * width * (depth + width // 2), 4 * depth * width),
        compiler_params=limits(),
        name="middle",
    )(place, left, *weights, middle, gain, upstream, *firsts)


def entry_grad_kernel(depth, left, w_here, w_there, inputs, gain, middle, *rest):
    o_ref, sums, side_sums, acc = rest
    i = pl.program_id(0)
    tile = acc.shape[1] // STEPS
    columns = pl.ds(pl.multiple_of(i * tile, tile), tile)
    acc[:, columns] = back_tile(left.at[0], w_here, depth) + back_tile(left.at[1], w_there, depth)

    @pl.when(i == STEPS - 1)
    def _():
        for side in range(2):
            side_sums[side] = jnp.sum(left[side, :, :depth].astype(wide), axis=0, keepdims=True)
        grad = acc[...]
        scaled, inverse = normalize(inputs[...].astype(wide))
        sums[0:1] = jnp.sum(grad * scaled, axis=0, keepdims=True)
        sums[1:2] = jnp.sum(grad, axis=0, keepdims=True)
        total = middle[...] + normalize_back(grad * gain[...], scaled, inverse)
        o_ref[...] = total.astype(low_type)


def entry_grad(left, depth, weights, inputs, gain, middle):
    rows, width = inputs.shape
    whole = pl.BlockSpec((rows, width), lambda i: (0, 0))
    return pl.pallas_call(
        functools.partial(entry_grad_kernel, depth),
        grid=(STEPS,),
        in_specs=[
            pl.BlockSpec(left.shape, lambda i: (0, 0, 0)),
            few_slabs(width),
            few_slabs(width),
            whole,
            pl.BlockSpec((1, width), lambda i: (0, 0)),
            whole,
        ],
        out_specs=[
            whole,
            pl.BlockSpec((8, width), lambda i: (0, 0)),
            pl.BlockSpec((2, 1, depth), lambda i: (0, 0, 0)),
        ],
        out_shape=[
            jax.ShapeDtypeStruct((rows, width), low_type),
            jax.ShapeDtypeStruct((8, width), wide),
            jax.ShapeDtypeStruct((2, 1, depth), wide),
        ],
        scratch_shapes=[pltpu.VMEM((rows, width), wide)],
        cost_estimate=cost(4 * rows * width * depth, 4 * depth * width),
        compiler_params=limits(),
        name="entry",
    )(left, *weights, inputs, gain, middle)


def grad_kernel(pairs, count, extra, *refs):
    out_ref = refs[-1]
    slabs, deep = out_ref.shape[:2]

    def matrix(number):
        ref = refs[number]
        return ref.at[0] if len(ref.shape) == 3 else ref

    for left, right, start, size, row, rows, column in pairs:
        place = pl.ds(start, size)
        total = dot_tn(matrix(left)[...], matrix(right)[:, place])
        total = total + dot_tn(matrix(count + left)[...], matrix(count + right)[:, place])
        total = total.reshape(slabs, rows, size).astype(low_type)
        out_ref[:, pl.ds(row, rows), pl.ds(column, size)] = total
    if extra:
        out_ref[:, pl.ds(deep - SLABS, SLABS)] = refs[2 * count][...]


def weight_grad(own, other, moving, pairs, extra=None):
    rows, depth = own[0][0].shape[-2:]
    width = 1024
    block = depth // STEPS
    slabs = SLABS // STEPS
    deep = sum(p[3] * p[5] for p in pairs) // width
    operands = [array for array, _ in (*own, *other)]

    def spec(index, array, which):
        by = int(index < moving)
        size = block if by else array.shape[-1]
        if array.ndim == 3:
            return pl.BlockSpec((1, rows, size), lambda i: (which, 0, i * by))
        return pl.BlockSpec((rows, size), lambda i: (0, i * by))

    specs = [spec(i, *pair) for pairs_of in (own, other) for i, pair in enumerate(pairs_of)]
    if extra is not None:
        deep += extra.shape[1]
        operands.append(extra)
        specs.append(pl.BlockSpec((slabs, *extra.shape[1:]), lambda i: (i, 0, 0)))
    return pl.pallas_call(
        functools.partial(grad_kernel, pairs, len(own), extra is not None),
        grid=(STEPS,),
        in_specs=specs,
        out_specs=pl.BlockSpec((slabs, deep, width), lambda i: (i, 0, 0)),
        out_shape=jax.ShapeDtypeStruct((SLABS, deep, width), low_type),
        cost_estimate=cost(4 * rows * SLABS * deep * width, 4 * SLABS * deep * width),
        compiler_params=limits(),
        name="grad",
    )(*operands)


def adam_update(weight, grad, first, second, factor, rate, decay):
    clipped = grad * factor
    momentum = beta_one * first + (1.0 - beta_one) * clipped
    variance = beta_two * second + (1.0 - beta_two) * clipped * clipped
    corrected_m = momentum / (1.0 - beta_one**STEP)
    corrected_v = variance / (1.0 - beta_two**STEP)
    updated = weight - rate * (corrected_m / (jnp.sqrt(corrected_v) + epsilon) + decay * weight)
    return (updated, momentum, variance)


def body(
    patches,
    live,
    cotangent,
    w_qkv,
    w_proj,
    w_in,
    w_out,
    vectors,
    first_qkv,
    first_proj,
    first_in,
    first_out,
    first_vectors,
    second_qkv,
    second_proj,
    second_in,
    second_out,
    second_vectors,
):
    core = lax.axis_index(SECTION)
    first = core == 0
    count_dp = lax.axis_size(DP)
    tuned = count_dp == LEVELS * SIDE
    me = 2 * lax.axis_index(Y) + lax.axis_index(X)
    place = core.astype(jnp.int32).reshape(1)
    masters = (w_qkv[0], w_proj[0], w_in[0], w_out[0], vectors[0])
    width = patches.shape[1]
    deep = width // SLABS
    hidden_width = w_in.shape[2]
    count_vectors = vectors.shape[1]
    half_vectors = count_vectors // 2
    half_qkv = w_qkv.shape[2] // 2
    stripe = hidden_width // (2 * count_dp)
    tokens = patches.shape[0] // 2
    images = live.shape[0] // 2
    line = Line()
    layers = (Layer(), Layer())

    def halves_of(array, groups):
        rows, columns = array.shape
        if groups == 1:
            return array[:, : columns // 2], array[:, columns // 2 :]
        shaped = array.reshape(rows, groups, 2, -1)
        return tuple(shaped[:, :, side].reshape(rows, -1) for side in range(2))

    def choose(pair):
        return jnp.where(first, pair[0], pair[1]), jnp.where(first, pair[1], pair[0])

    def join(here, there, axis):
        return jnp.where(
            first,
            jnp.concatenate([here, there], axis=axis),
            jnp.concatenate([there, here], axis=axis),
        )

    def pack(array):
        return jnp.concatenate([array[:, :width], array[:, width:]], axis=0)

    def unpack(array):
        rows = array.shape[0] // 2
        return jnp.concatenate([array[:rows], array[rows:]], axis=1)

    def slabs_of(array):
        shaped = array.reshape(SLABS, -1, 2, width)
        return shaped.transpose(0, 2, 1, 3).reshape(SLABS, -1, width)

    def from_slabs(array):
        shaped = array.reshape(SLABS, 2, -1, width)
        return shaped.transpose(0, 2, 1, 3).reshape(-1, 2 * width)

    lowered = [m.astype(low_type) for m in masters]
    qkv, proj = halves_of(lowered[0], 3), halves_of(lowered[1], 1)
    pairs = {
        1: tuple(jnp.concatenate([a, b], axis=1) for a, b in zip(qkv, proj)),
        2: halves_of(lowered[2], count_dp),
        3: tuple(jnp.split(lowered[3], 2, axis=0)),
    }
    parts = ({}, {})
    if tuned:
        pairs[1] = tuple(pack(a) for a in pairs[1])
        pairs[2] = tuple(pack(a) for a in pairs[2])
        spread = jnp.pad(
            lowered[4], ((0, SLABS - count_vectors), (0, width - lowered[4].shape[1]))
        )
        pairs[0] = (spread, spread)
        names = list(pairs)
        here = jnp.concatenate([choose(pairs[name])[0] for name in names], axis=0)
        there = jnp.concatenate([choose(pairs[name])[1] for name in names], axis=0)
        both = swap_halves(here, there, first)
        start = 0
        for name in names:
            stop = start + pairs[name][0].shape[0]
            for layer in range(2):
                parts[layer][name] = both[layer][start:stop]
            start = stop
    else:
        for name in pairs:
            parts[0][name], parts[1][name] = swap_halves(*choose(pairs[name]), first)
        other = swap_cores(lowered[4])
        parts[0][0] = jnp.where(first, lowered[4], other)
        parts[1][0] = jnp.where(first, other, lowered[4])

    layers[0].x = lax.dynamic_slice_in_dim(patches, core * tokens, tokens, axis=0)

    def target_of(side):
        weighting = lax.dynamic_slice_in_dim(live, side * images, images, axis=0).astype(low_type)
        target = lax.dynamic_slice_in_dim(cotangent, side * tokens, tokens, axis=0)
        target = target.reshape(images, SEQ, width) * weighting.reshape(images, 1, 1)
        return target.reshape(tokens, width)

    layers[1].dy = target_of(core)
    layers[1].dy_other = target_of(1 - core)

    def forward_one(number):
        layer = layers[number]
        (inputs,) = line.sync(layer.x)
        if tuned:
            spread = layer.spread[:, :count_vectors, :deep]
            rows = spread.transpose(1, 0, 2).reshape(count_vectors, width).astype(wide)
        else:
            rows = layer.spread.astype(wide)
        scaled, _ = normalize(inputs.astype(wide))
        hidden = (scaled * rows[0] + rows[1]).astype(low_type)
        query, value = [choose(halves_of(rows[i : i + 1], 1)) for i in (2, 3)]
        zero = jnp.zeros_like(query[0])
        bias = jnp.stack(
            [jnp.concatenate([query[s], zero, value[s]], axis=1) for s in range(2)]
        )
        hidden, bias, layer.rows = line.sync(hidden, bias, rows)
        layer.hidden = hidden
        weights = layer.weights[1]
        (packed,) = project(hidden, weights, 0, half_qkv // TILE, bias, low_type)
        (layer.packed,) = line.sync(packed)

    def forward_two(number):
        layer = layers[number]
        packed, rows, inputs = line.sync(layer.packed, layer.rows, layer.x)
        mixed = attend(packed)
        mixed = join(mixed[0], mixed[1], 1)
        bias = jnp.stack(choose(halves_of(rows[4:5], 1)))
        (branch,) = project(mixed, layer.weights[1], half_qkv // TILE, 1, bias, wide)
        middle = inputs.astype(wide) + join(branch[0], branch[1], 1)
        scaled, _ = normalize(middle)
        hidden = (scaled * rows[5] + rows[6]).astype(low_type)
        layer.mixed, layer.middle, layer.hidden_two = line.sync(mixed, middle, hidden)
        (kept,) = line.sync(jnp.stack([layer.hidden, layer.mixed, layer.hidden_two]))
        layer.kept_other = swap_cores(kept)

    def forward_three(number):
        layer = layers[number]
        hidden, rows, layer.kept_other = line.sync(
            layer.hidden_two, layer.rows, layer.kept_other
        )
        bias = jnp.stack(choose(halves_of(rows[8:12].reshape(1, -1), count_dp)))
        count = hidden_width // 2 // TILE
        pair = project(hidden, layer.weights[2], 0, count, bias, low_type, True)
        layer.active, layer.slope = line.sync(*pair)
        layer.active_other = swap_cores(layer.active[1])

    def forward_four(number):
        layer = layers[number]
        active, middle, rows, layer.active_other = line.sync(
            layer.active, layer.middle, layer.rows, layer.active_other
        )
        output = output_rows(active, layer.weights[3], middle, rows[7:8])
        (layer.block,) = line.sync(output)
        if number == 0:
            layers[1].x = layer.block

    def out_grad(number):
        layer = layers[number]
        active, upstream, *other = line.sync(
            layer.active, layer.dy, layer.active_other, layer.dy_other
        )
        plan = ((0, 1, 0, width, 0, hidden_width // 2 // SLABS, 0),)
        grad = weight_grad([(active, 0), (upstream, 0)], [(o, 0) for o in other], 1, plan)
        (layer.chip_grads[3],) = line.sync(grad)

    def in_grad(number):
        layer = layers[number]
        hidden, grad_pre, kept, other = line.sync(
            layer.hidden_two, layer.grad_pre, layer.kept_other, layer.grad_pre_other
        )
        plan = tuple((0, 1, b * width, width, b * deep, deep, 0) for b in range(2))
        grad = weight_grad([(hidden, 0), (grad_pre, 0)], [(kept, 2), (other, 0)], 1, plan)
        (layer.chip_grads[2],) = line.sync(grad)

    def first_grad(number):
        layer = layers[number]
        rows, rows_other = line.sync(layer.grad_rows, layer.rows_other)
        extra = choose(jnp.split(rows + rows_other, 2, axis=0))[0]
        extra = extra.reshape(half_vectors, SLABS, deep).transpose(1, 0, 2).astype(low_type)
        extra = jnp.pad(extra, ((0, 0), (0, SLABS - half_vectors), (0, width - deep)))
        hidden, mixed, slopes, kept, other, extra = line.sync(
            layer.hidden, layer.mixed, layer.slopes, layer.kept_other, layer.slopes_other, extra
        )
        half = width // 2
        plan = (
            (0, 2, 0, width, 0, deep, 0),
            (0, 2, width, half, deep, deep, 0),
            (1, 2, half_qkv, half, deep, deep, half),
        )
        grad = weight_grad(
            [(hidden, 0), (mixed, 0), (slopes, 0)],
            [(kept, 0), (kept, 1), (other, 0)],
            2,
            plan,
            extra,
        )
        (layer.chip_grads[1],) = line.sync(grad)

    def backward_two(number):
        layer = layers[number]
        upstream, slope, layer.dy_other = line.sync(layer.dy, layer.slope, layer.dy_other)
        pair = active_grad(upstream, layer.weights[3], slope)
        layer.grad_pre, layer.bias_in = line.sync(*pair)
        layer.grad_pre_other = swap_cores(layer.grad_pre[1])
        layer.bias_out = jnp.sum(upstream.astype(wide), axis=0, keepdims=True)

    def backward_three(number):
        layer = layers[number]
        grad_pre, middle, rows, upstream = line.sync(
            layer.grad_pre, layer.middle, layer.rows, layer.dy
        )
        results = middle_grad(
            place, grad_pre, layer.weights[2], middle, rows[5:6], upstream, layer.weights[1]
        )
        layer.grad_middle, layer.branch, layer.grad_mixed, layer.norm_two = line.sync(*results)

    def backward_four(number):
        layer = layers[number]
        packed, upstream, branch = line.sync(layer.packed, layer.grad_mixed, layer.branch)
        (layer.slopes,) = line.sync(attend_back(packed, upstream, branch))
        layer.slopes_other = swap_cores(layer.slopes[1])

    def backward_five(number):
        layer = layers[number]
        slopes, inputs, rows, grad_middle = line.sync(
            layer.slopes, layer.x, layer.rows, layer.grad_middle
        )
        entry, sums, columns = entry_grad(
            slopes, half_qkv, layer.weights[1], inputs, rows[0:1], grad_middle
        )
        third = half_qkv // 3
        query = join(columns[0, :, :third], columns[1, :, :third], 1)
        value = join(columns[0, :, 2 * third :], columns[1, :, 2 * third :], 1)
        inner = [s.reshape(count_dp, stripe) for s in layer.bias_in]
        bias_in = jnp.where(first, jnp.stack(inner, axis=1), jnp.stack(inner[::-1], axis=1))
        grad_rows = jnp.concatenate(
            [
                sums[0:2],
                query,
                value,
                layer.norm_two[2:3],
                layer.norm_two[0:2],
                layer.bias_out,
                bias_in.reshape(4, width),
            ],
            axis=0,
        )
        layer.entry, layer.grad_rows = line.sync(entry, grad_rows)
        layer.rows_other = swap_cores(layer.grad_rows)
        if number == 1:
            layers[0].dy = layer.entry
            layers[0].dy_other = swap_cores(layer.entry)

    joined = {}
    squares = [jnp.zeros((), wide)]

    def add_squares(kind):
        pair = line.sync(layers[0].grads[kind], layers[1].grads[kind])
        squares[:] = line.sync(squares[0] + sum(jnp.sum(part * part) for part in pair))

    def join_layers(kind):
        pair = line.sync(layers[0].grads[kind], layers[1].grads[kind])
        got = swap_cores(jnp.where(first, pair[1], pair[0]))
        mine = jnp.where(first, pair[0], pair[1])
        joined[kind] = jnp.where(first, mine, got), jnp.where(first, got, mine)

    def own_tokens(zero, one):
        zero, one = line.sync(zero, one)
        got = swap_cores(jnp.where(first, one, zero))
        return join(jnp.where(first, zero, one), got, 0)

    tokens_out = []

    def token_outputs():
        tokens_out.append(own_tokens(layers[0].block, layers[1].block))
        tokens_out.append(own_tokens(layers[0].entry, layers[1].entry))

    steps = {
        1: forward_one,
        2: forward_two,
        3: forward_three,
        4: forward_four,
        62: backward_two,
        63: backward_three,
        64: backward_four,
        65: backward_five,
        31: first_grad,
        32: in_grad,
        33: out_grad,
    }
    flows = {}
    for index, batch in enumerate(GATHERS):
        values = [parts[key % 10][key // 10] for key in batch]
        if tuned:
            flow = gather_flow_late if index in LATE_GATHERS else gather_flow
            flows[100 + index] = flow(line, values, me, batch, layers)
            continue
        for key, value in zip(batch, values):
            layer = layers[key % 10]
            if key < 10:
                layer.spread = lax.all_gather(value, DP, axis=1, tiled=True)
                continue
            mine = lax.all_gather(value, DP, axis=0, tiled=True)
            mine = mine.reshape(SLABS, -1, width) if key // 10 == 3 else slabs_of(mine)
            layer.weights[key // 10] = (mine, swap_cores(mine))
    if tuned:
        for index, batch in enumerate(SCATTERS):
            flow = scatter_flow_late if index in LATE_SCATTERS else scatter_flow
            flows[200 + index] = flow(line, me, batch, layers)
    for event in ORDER:
        if event in flows:
            next(flows[event], None)
        elif event // 10 in steps:
            steps[event // 10](event % 10)
        elif event == 500:
            token_outputs()
        elif event > 400 and tuned:
            add_squares(event - 400)
            join_layers(event - 400)
    for key in [key for batch in SCATTERS for key in batch if not tuned]:
        layer = layers[key % 10]
        total = layer.chip_grads[key // 10].astype(wide)
        if key // 10 == 3:
            natural = total.reshape(-1, width)
        else:
            natural = from_slabs(total[:, : 2 * deep])
        layer.grads[key // 10] = lax.psum_scatter(natural, DP, scatter_dimension=0, tiled=True)
        if key // 10 == 1:
            thin = total[:, 2 * deep : 2 * deep + half_vectors, :deep].transpose(1, 0, 2)
            thin = thin.reshape(half_vectors, width)
            layer.grads[0] = lax.psum_scatter(thin, DP, scatter_dimension=1, tiled=True)

    kinds = [kind for kind in layers[0].grads if kind not in joined]
    for kind in kinds:
        add_squares(kind)
    if tuned:
        global_sum = total_of(line, squares[0])
    else:
        global_sum = lax.psum(squares[0], (SECTION, *DP))
    for kind in kinds:
        join_layers(kind)

    def woven(pair, groups):
        rows = pair[0].shape[0]
        return jnp.stack([p.reshape(rows, groups, -1) for p in pair], axis=2).reshape(rows, -1)

    one, inner, outer = [joined[kind] for kind in (1, 2, 3)]
    if tuned:
        thin = [p[2 * deep : 2 * deep + half_vectors, :deep] for p in one]
        one, inner = [tuple(unpack(p[: 2 * deep]) for p in pair) for pair in (one, inner)]
    else:
        thin = joined[0]
    shards = (
        woven([p[:, :half_qkv] for p in one], 3),
        jnp.concatenate([p[:, half_qkv:] for p in one], axis=1),
        woven(inner, count_dp),
        jnp.concatenate(outer, axis=0),
        jnp.concatenate(thin, axis=0),
    )
    global_sum, *shards = line.sync(global_sum, *shards)
    grad_norm = jnp.sqrt(global_sum)
    factor = clip_norm / jnp.maximum(grad_norm, clip_norm)
    blocks, input_grad = tokens_out
    firsts = (first_qkv[0], first_proj[0], first_in[0], first_out[0], first_vectors[0])
    seconds = (second_qkv[0], second_proj[0], second_in[0], second_out[0], second_vectors[0])
    rates = (rate_matrix, rate_matrix, rate_matrix, rate_matrix, rate_vector)
    decays = (decay_matrix, decay_matrix, decay_matrix, decay_matrix, 0.0)
    results = [
        adam_update(w, g, f, s, factor, r, d)
        for w, g, f, s, r, d in zip(masters, shards, firsts, seconds, rates, decays)
    ]
    news = tuple((item[0][None] for item in results))
    momenta = tuple((item[1][None] for item in results))
    variances = tuple((item[2][None] for item in results))
    copies = tuple((n.astype(low_type) for n in news))
    grads_out = tuple((s[None] for s in shards))
    return (
        blocks[None],
        input_grad[None],
        *grads_out,
        grad_norm,
        *news,
        *copies,
        *momenta,
        *variances,
    )


def solution(mesh):
    devices = mesh.devices
    split = devices.reshape(devices.shape[0], devices.shape[1] // SIDE, 2, 2)
    mesh = Mesh(split, (SECTION, *DP))
    tokens = P(DP, None)
    matrix = P(SECTION, DP, None)
    columns = P(SECTION, None, DP)
    group = (matrix, matrix, matrix, matrix, columns)
    in_specs = (tokens, P(DP), tokens, *group, *group, *group)
    out_specs = (matrix, matrix, *group, P(), *group, *group, *group, *group)
    return jax.shard_map(body, mesh=mesh, in_specs=in_specs, out_specs=out_specs, check_vma=False)
```

```python
import functools
import jax
import jax.numpy as jnp
from jax import lax
from jax.experimental import pallas as pl
from jax.experimental.pallas import tpu as pltpu
from jax.sharding import Mesh
from jax.sharding import PartitionSpec as P

HEAD = 64
SEQ = 50
STEP = 10
SIDE = 4
LEVELS = 4
GROUP = 200
SLABS = 16
TILE = 512
STEPS = 4
VMEM_MB = 48
SECTION = "section"
DP = ("z", "y", "x")
X, Y, Z = DP[2], DP[1], DP[0]
GATHERS = ((10, 0, 1), (20,), (30,), (11,), (21,), (31,))
SCATTERS = ((31,), (21,), (11,), (30,), (20,), (10,))
ORDER = (
    100, 105, 102, 101, 103, 100, 103, 100, 103, 101, 104, 100, 100, 10, 101, 103,
    102, 101, 104, 20, 102, 105, 104, 102, 101, 30, 104, 103, 102, 40, 11, 21,
    105, 104, 105, 31, 105, 621, 331, 200, 631, 200, 321, 201, 641, 651, 201, 200,
    620, 330, 201, 203, 311, 202, 203, 320, 630, 202, 204, 201, 640, 203, 650, 202,
    200, 204, 310, 205, 41, 205, 203, 500, 202, 204, 205, 403, 204, 402, 205,
)

norm_epsilon = 1e-06
clip_norm = 1.0
beta_one = 0.9
beta_two = 0.95
rate_matrix = 0.05
rate_vector = 1.0
decay_matrix = 0.1
epsilon = 1e-08
low_type = jnp.bfloat16
wide = jnp.float32


def swap_cores(x):
    return lax.ppermute(x, SECTION, [(0, 1), (1, 0)])


def flip(x, axis):
    return lax.ppermute(x, axis, [(0, 1), (1, 0)])


class Line:
    def __init__(self):
        self.token = jnp.zeros((), wide)

    def sync(self, *values):
        fenced = lax.optimization_barrier((self.token, *values))
        self.token = fenced[0]
        return fenced[1:]


class Layer:
    def __init__(self):
        self.weights = {}
        self.chip_grads = {}
        self.grads = {}


def swap_halves(here, there, first):
    got = swap_cores(there)
    return jnp.where(first, here, got), jnp.where(first, got, here)


def place_blocks(blocks, me, axis):
    shape = list(blocks[0].shape)
    shape.insert(axis, SIDE)
    full = jnp.zeros(shape, blocks[0].dtype)
    for relative, block in enumerate(blocks):
        start = [0] * len(shape)
        start[axis] = jnp.bitwise_xor(me, relative)
        full = lax.dynamic_update_slice(full, jnp.expand_dims(block, axis), start)
    return full


def add_low(left, right):
    return (left.astype(wide) + right.astype(wide)).astype(low_type)


def gather_flow(line, parts, me, keys, layers):
    half = LEVELS // 2
    counts = [part.shape[0] for part in parts]
    extras = {}
    while keys[-1] < 10:
        extras[keys[-1]] = (sum(counts[: len(keys) - 1]), counts[len(keys) - 1])
        keys = keys[:-1]
    counts = counts[: len(keys) - 1] + [sum(counts[len(keys) - 1 :])]
    (part,) = line.sync(jnp.concatenate(parts, axis=0))
    column = lax.all_gather(part, Z, axis=0, tiled=False)
    yield
    (column,) = line.sync(column)
    across = flip(column, X)
    along = flip(column, Y)
    yield
    across, along, column = line.sync(across, along, column)
    corner_low, corner_high = line.sync(along[:half], across[half:])
    corner_low = flip(corner_low, X)
    corner_high = flip(corner_high, Y)
    fulls = []
    start = 0
    for count in counts:
        stop = start + count
        fulls.append(
            place_blocks([piece[:, start:stop] for piece in (column, across, along)], me, 1)
        )
        start = stop
    fulls = line.sync(*fulls)
    yield
    corner_low, corner_high, *fulls = line.sync(corner_low, corner_high, *fulls)
    corner = jnp.bitwise_xor(me, 3)
    start = 0
    for key, count, full in zip(keys, counts, fulls):
        stop = start + count
        full = lax.dynamic_update_slice(full, corner_low[:, None, start:stop], (0, corner, 0, 0))
        full = lax.dynamic_update_slice(
            full, corner_high[:, None, start:stop], (half, corner, 0, 0)
        )
        start = stop
        (own,) = line.sync(full.reshape(LEVELS * SIDE, count, -1))
        for name, (row, size) in extras.items():
            layers[name].spread = own[:, row : row + size]
        other = swap_cores(own)
        yield
        layers[key % 10].weights[key // 10] = line.sync(own, other)
    yield


def scatter_flow(line, key, layers):
    blocks = layers[key % 10].chip_grads[key // 10]
    corner_low, corner_high, own, across, along = line.sync(*blocks)
    from_across = flip(corner_low, X)
    from_along = flip(corner_high, Y)
    yield
    from_across, from_along = line.sync(from_across, from_along)
    across, along = line.sync(*add_corners(across, along, from_across, from_along))
    got_across = flip(across, X)
    got_along = flip(along, Y)
    yield
    got_across, got_along = line.sync(got_across, got_along)
    column = own.astype(wide) + got_across.astype(wide) + got_along.astype(wide)
    (column,) = line.sync(column.astype(low_type))
    total = lax.psum_scatter(column, Z, scatter_dimension=0, tiled=False)
    yield
    (total,) = line.sync(total)
    layers[key % 10].grads[key // 10] = total.astype(wide)
    yield


def total_of(line, value):
    (value,) = line.sync(value + swap_cores(value))
    value = value + flip(value, X)
    value = value + flip(value, Y)
    for bit in (1, 2):
        pairs = [(i, i ^ bit) for i in range(LEVELS)]
        value = value + lax.ppermute(value, Z, pairs)
    return value


def normalize(inputs):
    centered = inputs - jnp.mean(inputs, axis=-1, keepdims=True)
    inverse = lax.rsqrt(jnp.mean(centered * centered, axis=-1, keepdims=True) + norm_epsilon)
    return (centered * inverse, inverse)


def normalize_back(upstream, scaled, inverse):
    return inverse * (
        upstream
        - jnp.mean(upstream, axis=-1, keepdims=True)
        - scaled * jnp.mean(upstream * scaled, axis=-1, keepdims=True)
    )


def dot_nt(left, right):
    return lax.dot_general(left, right, (((1,), (1,)), ((), ())), preferred_element_type=wide)


def dot_nn(left, right):
    return lax.dot_general(left, right, (((1,), (0,)), ((), ())), preferred_element_type=wide)


def dot_tn(left, right):
    return lax.dot_general(left, right, (((0,), (0,)), ((), ())), preferred_element_type=wide)


def same_image(rows):
    image_row = lax.broadcasted_iota(jnp.int32, (rows, rows), 0) // SEQ
    image_col = lax.broadcasted_iota(jnp.int32, (rows, rows), 1) // SEQ
    return image_row == image_col


def attend_kernel(q_ref, k_ref, v_ref, o_ref):
    rows, columns = q_ref.shape[1:]
    mask = same_image(rows)
    lane = lax.broadcasted_iota(jnp.int32, (rows, 2 * HEAD), 1)
    for start in range(0, columns, 2 * HEAD):
        place = pl.ds(start, 2 * HEAD)
        queries, keys, values = q_ref[0, :, place], k_ref[0, :, place], v_ref[0, :, place]
        queries = queries * jnp.asarray(HEAD ** (-0.5), low_type)
        mixed = []
        for head in range(2):
            inside = (lane >= head * HEAD) & (lane < (head + 1) * HEAD)
            own = jnp.where(inside, queries, jnp.zeros_like(queries))
            scores = jnp.where(mask, dot_nt(own, keys), -jnp.inf)
            raised = jnp.exp(scores - jnp.max(scores, axis=1, keepdims=True))
            weights = raised * (1.0 / jnp.sum(raised, axis=1, keepdims=True))
            mixed.append(dot_nn(weights.astype(low_type), values))
        o_ref[0, :, place] = jnp.where(lane < HEAD, mixed[0], mixed[1]).astype(low_type)


def third_at(third, rows, columns):
    return pl.BlockSpec((1, rows, columns), lambda i: (i, 0, third))


def attend(packed):
    sides, rows, columns = packed.shape
    groups, width = sides * rows // GROUP, columns // 3
    packed = packed.reshape(groups, GROUP, columns)
    mixed = pl.pallas_call(
        attend_kernel,
        grid=(groups,),
        in_specs=[third_at(third, GROUP, width) for third in range(3)],
        out_specs=third_at(0, GROUP, width),
        out_shape=jax.ShapeDtypeStruct((groups, GROUP, width), low_type),
        cost_estimate=cost(8 * sides * rows * GROUP * width, 8 * sides * rows * width),
        compiler_params=limits(),
        name="attend",
    )(packed, packed, packed)
    return mixed.reshape(sides, rows, width)


def attend_back_kernel(q_ref, k_ref, v_ref, g_ref, b_ref, d_ref):
    rows, columns = q_ref.shape[1:]
    mask = same_image(rows)
    lane = lax.broadcasted_iota(jnp.int32, (rows, 2 * HEAD), 1)
    scaling = HEAD ** (-0.5)
    lower = lane < HEAD
    d_ref[0, :, pl.ds(3 * columns, columns)] = b_ref[0]
    for start in range(0, columns, 2 * HEAD):
        place = pl.ds(start, 2 * HEAD)
        queries, keys, values = q_ref[0, :, place], k_ref[0, :, place], v_ref[0, :, place]
        upstream = g_ref[0, :, place]
        queries = queries * jnp.asarray(scaling, low_type)
        to_queries, to_keys, to_values = [], [], []
        for head in range(2):
            inside = (lane >= head * HEAD) & (lane < (head + 1) * HEAD)
            zero = jnp.zeros_like(queries)
            own_queries = jnp.where(inside, queries, zero)
            own_upstream = jnp.where(inside, upstream, zero)
            scores = jnp.where(mask, dot_nt(keys, own_queries), -jnp.inf)
            raised = jnp.exp(scores - jnp.max(scores, axis=0, keepdims=True))
            weights = raised * (1.0 / jnp.sum(raised, axis=0, keepdims=True))
            to_values.append(dot_nn(weights.astype(low_type), upstream))
            slope = dot_nt(values, own_upstream)
            inner = jnp.sum(weights * slope, axis=0, keepdims=True)
            change = (weights * (slope - inner)).astype(low_type)
            to_keys.append(dot_nn(change, queries))
            to_queries.append(dot_tn(keys, change))
        turned = jnp.concatenate([to_queries[0][:HEAD], to_queries[1][HEAD:]], axis=0)
        d_ref[0, :, place] = (turned.T * scaling).astype(low_type)
        keys_place = pl.ds(columns + start, 2 * HEAD)
        d_ref[0, :, keys_place] = jnp.where(lower, to_keys[0], to_keys[1]).astype(low_type)
        values_place = pl.ds(2 * columns + start, 2 * HEAD)
        d_ref[0, :, values_place] = jnp.where(lower, to_values[0], to_values[1]).astype(low_type)


def attend_back(packed, upstream, branch):
    sides, rows, columns = packed.shape
    groups, width = sides * rows // GROUP, columns // 3
    packed = packed.reshape(groups, GROUP, columns)
    upstream = upstream.reshape(groups, GROUP, width)
    branch = branch.reshape(groups, GROUP, width)
    total = columns + width
    slopes = pl.pallas_call(
        attend_back_kernel,
        grid=(groups,),
        in_specs=[third_at(third, GROUP, width) for third in (0, 1, 2, 0, 0)],
        out_specs=pl.BlockSpec((1, GROUP, total), lambda i: (i, 0, 0)),
        out_shape=jax.ShapeDtypeStruct((groups, GROUP, total), low_type),
        cost_estimate=cost(20 * sides * rows * GROUP * width, 14 * sides * rows * width),
        compiler_params=limits(),
        name="attend_back",
    )(packed, packed, packed, upstream, branch)
    return slopes.reshape(sides, rows, total)


def limits():
    return pltpu.CompilerParams(vmem_limit_bytes=VMEM_MB * 1024 * 1024)


def cost(flops, moved, special=0):
    return pl.CostEstimate(flops=flops, bytes_accessed=moved, transcendentals=special)


def early(count):
    return lambda i: jnp.minimum(i, count - 1)


def late(count):
    return lambda i: jnp.maximum(i - count, 0)


def tile_spec(width, first, turn):
    per = width // TILE

    def at(i):
        tile = first + turn(i)
        return (0, tile // per, tile % per)

    return pl.BlockSpec((SLABS, width // SLABS, TILE), at)


def side_spec(count, *shape):
    return pl.BlockSpec((1, *shape), lambda i: (i // count, 0, i % count))


def flat(ref):
    return ref[...].reshape(ref.shape[0] * ref.shape[1], ref.shape[2])


def project_kernel(smooth, count, x_ref, here_ref, there_ref, b_ref, *outs):
    def work(w_ref):
        total = dot_nn(x_ref[...], flat(w_ref)) + b_ref[0]
        if smooth:
            cdf = 0.5 * (1.0 + lax.erf(total * 0.7071067811865476))
            density = jnp.exp(-0.5 * total * total) * 0.3989422804014327
            outs[0][0] = (total * cdf).astype(low_type)
            outs[1][0] = (cdf + total * density).astype(low_type)
        else:
            outs[0][0] = total.astype(outs[0].dtype)

    i = pl.program_id(0)
    pl.when(i < count)(lambda: work(here_ref))
    pl.when(i >= count)(lambda: work(there_ref))


def project(x, weights, first, count, bias, kind, smooth=False):
    rows, depth = x.shape
    number = 2 if smooth else 1
    return pl.pallas_call(
        functools.partial(project_kernel, smooth, count),
        grid=(2 * count,),
        in_specs=[
            pl.BlockSpec((rows, depth), lambda i: (0, 0)),
            tile_spec(depth, first, early(count)),
            tile_spec(depth, first, late(count)),
            side_spec(count, 1, TILE),
        ],
        out_specs=[side_spec(count, rows, TILE)] * number,
        out_shape=[jax.ShapeDtypeStruct((2, rows, count * TILE), kind)] * number,
        cost_estimate=cost(4 * rows * depth * count * TILE, 4 * depth * count * TILE),
        compiler_params=limits(),
        name="project",
    )(x, *weights, bias)


def output_kernel(active_ref, w_here, w_there, middle_ref, b_ref, o_ref):
    total = dot_nn(active_ref[0], flat(w_here)) + dot_nn(active_ref[1], flat(w_there))
    o_ref[...] = (total + middle_ref[...] + b_ref[...]).astype(low_type)


def output_rows(active, weights, middle, bias):
    _, rows, depth = active.shape
    width = middle.shape[1]
    tile = width // STEPS
    weight = pl.BlockSpec((SLABS, depth // SLABS, tile), lambda i: (0, 0, i))
    part = pl.BlockSpec((rows, tile), lambda i: (0, i))
    return pl.pallas_call(
        output_kernel,
        grid=(STEPS,),
        in_specs=[
            pl.BlockSpec(active.shape, lambda i: (0, 0, 0)),
            weight,
            weight,
            part,
            pl.BlockSpec((1, tile), lambda i: (0, i)),
        ],
        out_specs=part,
        out_shape=jax.ShapeDtypeStruct((rows, width), low_type),
        cost_estimate=cost(4 * rows * depth * width, 4 * depth * width),
        compiler_params=limits(),
        name="output",
    )(active, *weights, middle, bias)


def active_grad_kernel(count, up_ref, w_here, w_there, slope_ref, o_ref, sum_ref):
    def work(w_ref):
        low = (dot_nt(up_ref[...], flat(w_ref)) * slope_ref[0].astype(wide)).astype(low_type)
        o_ref[0] = low
        sum_ref[0] = jnp.sum(low.astype(wide), axis=0, keepdims=True)

    i = pl.program_id(0)
    pl.when(i < count)(lambda: work(w_here))
    pl.when(i >= count)(lambda: work(w_there))


def active_grad(upstream, weights, slope):
    rows, width = upstream.shape
    depth = slope.shape[2]
    count = depth // TILE
    slabs = SLABS // count

    def weight(turn):
        return pl.BlockSpec((slabs, depth // SLABS, width), lambda i: (turn(i), 0, 0))

    return pl.pallas_call(
        functools.partial(active_grad_kernel, count),
        grid=(2 * count,),
        in_specs=[
            pl.BlockSpec((rows, width), lambda i: (0, 0)),
            weight(early(count)),
            weight(late(count)),
            side_spec(count, rows, TILE),
        ],
        out_specs=[side_spec(count, rows, TILE), side_spec(count, 1, TILE)],
        out_shape=[
            jax.ShapeDtypeStruct((2, rows, depth), low_type),
            jax.ShapeDtypeStruct((2, 1, depth), wide),
        ],
        cost_estimate=cost(4 * rows * depth * width, 6 * depth * width),
        compiler_params=limits(),
        name="active",
    )(upstream, *weights, slope)


def back_tile(left, packed, depth):
    slabs, _, width = packed.shape
    rows = width // SLABS
    total = None
    for block in range(2):
        count = min(depth - block * width, width)
        part = packed[:, pl.ds(block * rows, rows), pl.ds(0, count)].reshape(slabs * rows, count)
        term = dot_nt(left[:, pl.ds(block * width, count)], part)
        total = term if total is None else total + term
    return total


def middle_grad_kernel(place, *refs):
    left, w_here, w_there, middle, gain, up, proj_here, proj_there = refs[:8]
    o_middle, o_branch, o_mixed, sums, acc = refs[8:]
    i = pl.program_id(0)
    tile = acc.shape[1] // STEPS
    columns = pl.ds(pl.multiple_of(i * tile, tile), tile)
    depth = left.shape[2]
    acc[:, columns] = back_tile(left.at[0], w_here, depth) + back_tile(left.at[1], w_there, depth)

    @pl.when(i == STEPS - 1)
    def _():
        first = place[0] == 0
        grad = acc[...]
        scaled, inverse = normalize(middle[...])
        sums[0:1] = jnp.sum(grad * scaled, axis=0, keepdims=True)
        sums[1:2] = jnp.sum(grad, axis=0, keepdims=True)
        total = up[...].astype(wide) + normalize_back(grad * gain[...], scaled, inverse)
        o_middle[...] = total
        branch = total.astype(low_type)
        sums[2:3] = jnp.sum(branch.astype(wide), axis=0, keepdims=True)
        width = branch.shape[1] // 2
        near = jnp.where(first, branch[:, :width], branch[:, width:])
        far = jnp.where(first, branch[:, width:], branch[:, :width])
        o_branch[0] = near
        o_branch[1] = far
        mixed = dot_nt(near, flat(proj_here)) + dot_nt(far, flat(proj_there))
        mixed = mixed.astype(low_type)
        o_mixed[0] = jnp.where(first, mixed[:, :width], mixed[:, width:])
        o_mixed[1] = jnp.where(first, mixed[:, width:], mixed[:, :width])


def few_slabs(width):
    return pl.BlockSpec((SLABS // STEPS, 2 * width // SLABS, width), lambda i: (i, 0, 0))


def middle_grad(place, left, weights, middle, gain, upstream, firsts):
    rows, width = middle.shape
    depth = left.shape[2]
    whole = pl.BlockSpec((rows, width), lambda i: (0, 0))
    pair = pl.BlockSpec((2, rows, width // 2), lambda i: (0, 0, 0))
    halves = jax.ShapeDtypeStruct((2, rows, width // 2), low_type)
    return pl.pallas_call(
        middle_grad_kernel,
        grid=(STEPS,),
        in_specs=[
            pl.BlockSpec(memory_space=pltpu.SMEM),
            pl.BlockSpec(left.shape, lambda i: (0, 0, 0)),
            few_slabs(width),
            few_slabs(width),
            whole,
            pl.BlockSpec((1, width), lambda i: (0, 0)),
            whole,
            tile_spec(width, 3, lambda i: 0),
            tile_spec(width, 3, lambda i: 0),
        ],
        out_specs=[whole, pair, pair, pl.BlockSpec((8, width), lambda i: (0, 0))],
        out_shape=[
            jax.ShapeDtypeStruct((rows, width), wide),
            halves,
            halves,
            jax.ShapeDtypeStruct((8, width), wide),
        ],
        scratch_shapes=[pltpu.VMEM((rows, width), wide)],
        cost_estimate=cost(4 * rows * width * (depth + width // 2), 4 * depth * width),
        compiler_params=limits(),
        name="middle",
    )(place, left, *weights, middle, gain, upstream, *firsts)


def entry_grad_kernel(depth, left, w_here, w_there, inputs, gain, middle, *rest):
    o_ref, sums, side_sums, acc = rest
    i = pl.program_id(0)
    tile = acc.shape[1] // STEPS
    columns = pl.ds(pl.multiple_of(i * tile, tile), tile)
    acc[:, columns] = back_tile(left.at[0], w_here, depth) + back_tile(left.at[1], w_there, depth)

    @pl.when(i == STEPS - 1)
    def _():
        for side in range(2):
            side_sums[side] = jnp.sum(left[side, :, :depth].astype(wide), axis=0, keepdims=True)
        grad = acc[...]
        scaled, inverse = normalize(inputs[...].astype(wide))
        sums[0:1] = jnp.sum(grad * scaled, axis=0, keepdims=True)
        sums[1:2] = jnp.sum(grad, axis=0, keepdims=True)
        total = middle[...] + normalize_back(grad * gain[...], scaled, inverse)
        o_ref[...] = total.astype(low_type)


def entry_grad(left, depth, weights, inputs, gain, middle):
    rows, width = inputs.shape
    whole = pl.BlockSpec((rows, width), lambda i: (0, 0))
    return pl.pallas_call(
        functools.partial(entry_grad_kernel, depth),
        grid=(STEPS,),
        in_specs=[
            pl.BlockSpec(left.shape, lambda i: (0, 0, 0)),
            few_slabs(width),
            few_slabs(width),
            whole,
            pl.BlockSpec((1, width), lambda i: (0, 0)),
            whole,
        ],
        out_specs=[
            whole,
            pl.BlockSpec((8, width), lambda i: (0, 0)),
            pl.BlockSpec((2, 1, depth), lambda i: (0, 0, 0)),
        ],
        out_shape=[
            jax.ShapeDtypeStruct((rows, width), low_type),
            jax.ShapeDtypeStruct((8, width), wide),
            jax.ShapeDtypeStruct((2, 1, depth), wide),
        ],
        scratch_shapes=[pltpu.VMEM((rows, width), wide)],
        cost_estimate=cost(4 * rows * width * depth, 4 * depth * width),
        compiler_params=limits(),
        name="entry",
    )(left, *weights, inputs, gain, middle)


def grad_kernel(pairs, count, extra, chip, *refs):
    out_ref = refs[-1]
    slabs, deep = out_ref.shape[:2]

    def matrix(number):
        ref = refs[number]
        return ref.at[0] if len(ref.shape) == 3 else ref

    for left, right, start, size, row, rows, column in pairs:
        place = pl.ds(start, size)
        total = dot_tn(matrix(left)[...], matrix(right)[:, place])
        total = total + dot_tn(matrix(count + left)[...], matrix(count + right)[:, place])
        total = total.reshape(slabs, rows, size).astype(low_type)
        out_ref[:, pl.ds(row, rows), pl.ds(column, size)] = total
    if extra:
        out_ref[:, pl.ds(deep - SLABS, SLABS)] = refs[2 * count][...]
    if chip is None:
        return
    low_ref, high_ref, *sides = refs[-6:-1]
    i = pl.program_id(0)
    for relative, ref in enumerate(sides):
        ref[0] = out_ref[jnp.bitwise_xor(chip[0], relative)]

    @pl.when(i < LEVELS // 2)
    def _():
        low_ref[0] = out_ref[jnp.bitwise_xor(chip[0], 3)]

    @pl.when(i >= LEVELS // 2)
    def _():
        high_ref[0] = out_ref[jnp.bitwise_xor(chip[0], 3)]


def grad_whole_kernel(pairs, count, extra, *refs):
    grad_kernel(pairs, count, extra, None, *refs)


def weight_grad(chip, own, other, moving, pairs, extra=None):
    rows, depth = own[0][0].shape[-2:]
    width = 1024
    block = depth // STEPS
    slabs = SLABS // STEPS
    deep = sum(p[3] * p[5] for p in pairs) // width
    operands = [array for array, _ in (*own, *other)]

    def spec(index, array, which):
        by = int(index < moving)
        size = block if by else array.shape[-1]
        if array.ndim == 3:
            return pl.BlockSpec((1, rows, size), lambda i: (which, 0, i * by))
        return pl.BlockSpec((rows, size), lambda i: (0, i * by))

    specs = [spec(i, *pair) for pairs_of in (own, other) for i, pair in enumerate(pairs_of)]
    if extra is not None:
        deep += extra.shape[1]
        operands.append(extra)
        specs.append(pl.BlockSpec((slabs, *extra.shape[1:]), lambda i: (i, 0, 0)))
    flops = cost(4 * rows * SLABS * deep * width, 4 * SLABS * deep * width)
    if chip is None:
        return pl.pallas_call(
            functools.partial(grad_whole_kernel, pairs, len(own), extra is not None),
            grid=(STEPS,),
            in_specs=specs,
            out_specs=pl.BlockSpec((slabs, deep, width), lambda i: (i, 0, 0)),
            out_shape=jax.ShapeDtypeStruct((SLABS, deep, width), low_type),
            cost_estimate=flops,
            compiler_params=limits(),
            name="grad",
        )(*operands)
    half = LEVELS // 2

    def block(turn):
        return pl.BlockSpec((1, deep, width), lambda i: (turn(i), 0, 0))

    def shape(levels):
        return jax.ShapeDtypeStruct((levels, deep, width), low_type)

    return pl.pallas_call(
        functools.partial(grad_kernel, pairs, len(own), extra is not None),
        grid=(STEPS,),
        in_specs=[pl.BlockSpec(memory_space=pltpu.SMEM)] + specs,
        out_specs=[block(early(half)), block(late(half))] + [block(lambda i: i)] * 3,
        out_shape=[shape(half)] * 2 + [shape(LEVELS)] * 3,
        scratch_shapes=[pltpu.VMEM((slabs, deep, width), low_type)],
        cost_estimate=flops,
        compiler_params=limits(),
        name="grad",
    )(chip, *operands)


def add_kernel(across_ref, along_ref, from_across, from_along, across_out, along_out):
    along_out[...] = add_low(along_ref[...], from_across[...])
    across_out[...] = add_low(across_ref[...], from_along[...])


def add_corners(across, along, from_across, from_along):
    half, rows, width = from_across.shape

    def block(first):
        return pl.BlockSpec((1, rows, width), lambda i: (first + i, 0, 0))

    return pl.pallas_call(
        add_kernel,
        grid=(half,),
        in_specs=[block(half), block(0), block(0), block(0)],
        out_specs=[block(half), block(0)],
        out_shape=[jax.ShapeDtypeStruct(across.shape, low_type)] * 2,
        input_output_aliases={0: 0, 1: 1},
        cost_estimate=cost(half * rows * width, 12 * half * rows * width),
        compiler_params=limits(),
        name="add",
    )(across, along, from_across, from_along)


def adam_update(weight, grad, first, second, factor, rate, decay):
    clipped = grad * factor
    momentum = beta_one * first + (1.0 - beta_one) * clipped
    variance = beta_two * second + (1.0 - beta_two) * clipped * clipped
    corrected_m = momentum / (1.0 - beta_one**STEP)
    corrected_v = variance / (1.0 - beta_two**STEP)
    updated = weight - rate * (corrected_m / (jnp.sqrt(corrected_v) + epsilon) + decay * weight)
    return (updated, momentum, variance)


def body(
    patches,
    live,
    cotangent,
    w_qkv,
    w_proj,
    w_in,
    w_out,
    vectors,
    first_qkv,
    first_proj,
    first_in,
    first_out,
    first_vectors,
    second_qkv,
    second_proj,
    second_in,
    second_out,
    second_vectors,
):
    core = lax.axis_index(SECTION)
    first = core == 0
    count_dp = lax.axis_size(DP)
    tuned = count_dp == LEVELS * SIDE
    me = 2 * lax.axis_index(Y) + lax.axis_index(X)
    place = core.astype(jnp.int32).reshape(1)
    masters = (w_qkv[0], w_proj[0], w_in[0], w_out[0], vectors[0])
    width = patches.shape[1]
    deep = width // SLABS
    hidden_width = w_in.shape[2]
    count_vectors = vectors.shape[1]
    half_vectors = count_vectors // 2
    half_qkv = w_qkv.shape[2] // 2
    stripe = hidden_width // (2 * count_dp)
    tokens = patches.shape[0] // 2
    images = live.shape[0] // 2
    line = Line()
    layers = (Layer(), Layer())

    def halves_of(array, groups):
        rows, columns = array.shape
        if groups == 1:
            return array[:, : columns // 2], array[:, columns // 2 :]
        shaped = array.reshape(rows, groups, 2, -1)
        return tuple(shaped[:, :, side].reshape(rows, -1) for side in range(2))

    def choose(pair):
        return jnp.where(first, pair[0], pair[1]), jnp.where(first, pair[1], pair[0])

    def join(here, there, axis):
        return jnp.where(
            first,
            jnp.concatenate([here, there], axis=axis),
            jnp.concatenate([there, here], axis=axis),
        )

    def pack(array):
        return jnp.concatenate([array[:, :width], array[:, width:]], axis=0)

    def unpack(array):
        rows = array.shape[0] // 2
        return jnp.concatenate([array[:rows], array[rows:]], axis=1)

    def slabs_of(array):
        shaped = array.reshape(SLABS, -1, 2, width)
        return shaped.transpose(0, 2, 1, 3).reshape(SLABS, -1, width)

    def from_slabs(array):
        shaped = array.reshape(SLABS, 2, -1, width)
        return shaped.transpose(0, 2, 1, 3).reshape(-1, 2 * width)

    lowered = [m.astype(low_type) for m in masters]
    qkv, proj = halves_of(lowered[0], 3), halves_of(lowered[1], 1)
    pairs = {
        1: tuple(jnp.concatenate([a, b], axis=1) for a, b in zip(qkv, proj)),
        2: halves_of(lowered[2], count_dp),
        3: tuple(jnp.split(lowered[3], 2, axis=0)),
    }
    parts = ({}, {})
    if tuned:
        pairs[1] = tuple(pack(a) for a in pairs[1])
        pairs[2] = tuple(pack(a) for a in pairs[2])
        spread = jnp.pad(
            lowered[4], ((0, SLABS - count_vectors), (0, width - lowered[4].shape[1]))
        )
        pairs[0] = (spread, spread)
        names = list(pairs)
        here = jnp.concatenate([choose(pairs[name])[0] for name in names], axis=0)
        there = jnp.concatenate([choose(pairs[name])[1] for name in names], axis=0)
        both = swap_halves(here, there, first)
        start = 0
        for name in names:
            stop = start + pairs[name][0].shape[0]
            for layer in range(2):
                parts[layer][name] = both[layer][start:stop]
            start = stop
    else:
        for name in pairs:
            parts[0][name], parts[1][name] = swap_halves(*choose(pairs[name]), first)
        other = swap_cores(lowered[4])
        parts[0][0] = jnp.where(first, lowered[4], other)
        parts[1][0] = jnp.where(first, other, lowered[4])

    layers[0].x = lax.dynamic_slice_in_dim(patches, core * tokens, tokens, axis=0)

    def target_of(side):
        weighting = lax.dynamic_slice_in_dim(live, side * images, images, axis=0).astype(low_type)
        target = lax.dynamic_slice_in_dim(cotangent, side * tokens, tokens, axis=0)
        target = target.reshape(images, SEQ, width) * weighting.reshape(images, 1, 1)
        return target.reshape(tokens, width)

    layers[1].dy = target_of(core)
    layers[1].dy_other = target_of(1 - core)

    def forward_one(number):
        layer = layers[number]
        (inputs,) = line.sync(layer.x)
        if tuned:
            spread = layer.spread[:, :count_vectors, :deep]
            rows = spread.transpose(1, 0, 2).reshape(count_vectors, width).astype(wide)
        else:
            rows = layer.spread.astype(wide)
        scaled, _ = normalize(inputs.astype(wide))
        hidden = (scaled * rows[0] + rows[1]).astype(low_type)
        query, value = [choose(halves_of(rows[i : i + 1], 1)) for i in (2, 3)]
        zero = jnp.zeros_like(query[0])
        bias = jnp.stack(
            [jnp.concatenate([query[s], zero, value[s]], axis=1) for s in range(2)]
        )
        hidden, bias, layer.rows = line.sync(hidden, bias, rows)
        layer.hidden = hidden
        weights = layer.weights[1]
        (packed,) = project(hidden, weights, 0, half_qkv // TILE, bias, low_type)
        (layer.packed,) = line.sync(packed)

    def forward_two(number):
        layer = layers[number]
        packed, rows, inputs = line.sync(layer.packed, layer.rows, layer.x)
        mixed = attend(packed)
        mixed = join(mixed[0], mixed[1], 1)
        bias = jnp.stack(choose(halves_of(rows[4:5], 1)))
        (branch,) = project(mixed, layer.weights[1], half_qkv // TILE, 1, bias, wide)
        middle = inputs.astype(wide) + join(branch[0], branch[1], 1)
        scaled, _ = normalize(middle)
        hidden = (scaled * rows[5] + rows[6]).astype(low_type)
        layer.mixed, layer.middle, layer.hidden_two = line.sync(mixed, middle, hidden)
        (kept,) = line.sync(jnp.stack([layer.hidden, layer.mixed, layer.hidden_two]))
        layer.kept_other = swap_cores(kept)

    def forward_three(number):
        layer = layers[number]
        hidden, rows, layer.kept_other = line.sync(
            layer.hidden_two, layer.rows, layer.kept_other
        )
        bias = jnp.stack(choose(halves_of(rows[8:12].reshape(1, -1), count_dp)))
        count = hidden_width // 2 // TILE
        pair = project(hidden, layer.weights[2], 0, count, bias, low_type, True)
        layer.active, layer.slope = line.sync(*pair)
        layer.active_other = swap_cores(layer.active[1])

    def forward_four(number):
        layer = layers[number]
        active, middle, rows, layer.active_other = line.sync(
            layer.active, layer.middle, layer.rows, layer.active_other
        )
        output = output_rows(active, layer.weights[3], middle, rows[7:8])
        (layer.block,) = line.sync(output)
        if number == 0:
            layers[1].x = layer.block

    chip = me.astype(jnp.int32).reshape(1) if tuned else None

    def keep(layer, kind, grad):
        layer.chip_grads[kind] = line.sync(*grad) if tuned else line.sync(grad)[0]

    def out_grad(number):
        layer = layers[number]
        active, upstream, *other = line.sync(
            layer.active, layer.dy, layer.active_other, layer.dy_other
        )
        plan = ((0, 1, 0, width, 0, hidden_width // 2 // SLABS, 0),)
        grad = weight_grad(chip, [(active, 0), (upstream, 0)], [(o, 0) for o in other], 1, plan)
        keep(layer, 3, grad)

    def in_grad(number):
        layer = layers[number]
        hidden, grad_pre, kept, other = line.sync(
            layer.hidden_two, layer.grad_pre, layer.kept_other, layer.grad_pre_other
        )
        plan = tuple((0, 1, b * width, width, b * deep, deep, 0) for b in range(2))
        grad = weight_grad(chip, [(hidden, 0), (grad_pre, 0)], [(kept, 2), (other, 0)], 1, plan)
        keep(layer, 2, grad)

    def first_grad(number):
        layer = layers[number]
        rows, rows_other = line.sync(layer.grad_rows, layer.rows_other)
        extra = choose(jnp.split(rows + rows_other, 2, axis=0))[0]
        extra = extra.reshape(half_vectors, SLABS, deep).transpose(1, 0, 2).astype(low_type)
        extra = jnp.pad(extra, ((0, 0), (0, SLABS - half_vectors), (0, width - deep)))
        hidden, mixed, slopes, kept, other, extra = line.sync(
            layer.hidden, layer.mixed, layer.slopes, layer.kept_other, layer.slopes_other, extra
        )
        half = width // 2
        plan = (
            (0, 2, 0, width, 0, deep, 0),
            (0, 2, width, half, deep, deep, 0),
            (1, 2, half_qkv, half, deep, deep, half),
        )
        grad = weight_grad(
            chip,
            [(hidden, 0), (mixed, 0), (slopes, 0)],
            [(kept, 0), (kept, 1), (other, 0)],
            2,
            plan,
            extra,
        )
        keep(layer, 1, grad)

    def backward_two(number):
        layer = layers[number]
        upstream, slope, layer.dy_other = line.sync(layer.dy, layer.slope, layer.dy_other)
        pair = active_grad(upstream, layer.weights[3], slope)
        layer.grad_pre, layer.bias_in = line.sync(*pair)
        layer.grad_pre_other = swap_cores(layer.grad_pre[1])
        layer.bias_out = jnp.sum(upstream.astype(wide), axis=0, keepdims=True)

    def backward_three(number):
        layer = layers[number]
        grad_pre, middle, rows, upstream = line.sync(
            layer.grad_pre, layer.middle, layer.rows, layer.dy
        )
        results = middle_grad(
            place, grad_pre, layer.weights[2], middle, rows[5:6], upstream, layer.weights[1]
        )
        layer.grad_middle, layer.branch, layer.grad_mixed, layer.norm_two = line.sync(*results)

    def backward_four(number):
        layer = layers[number]
        packed, upstream, branch = line.sync(layer.packed, layer.grad_mixed, layer.branch)
        (layer.slopes,) = line.sync(attend_back(packed, upstream, branch))
        layer.slopes_other = swap_cores(layer.slopes[1])

    def backward_five(number):
        layer = layers[number]
        slopes, inputs, rows, grad_middle = line.sync(
            layer.slopes, layer.x, layer.rows, layer.grad_middle
        )
        entry, sums, columns = entry_grad(
            slopes, half_qkv, layer.weights[1], inputs, rows[0:1], grad_middle
        )
        third = half_qkv // 3
        query = join(columns[0, :, :third], columns[1, :, :third], 1)
        value = join(columns[0, :, 2 * third :], columns[1, :, 2 * third :], 1)
        inner = [s.reshape(count_dp, stripe) for s in layer.bias_in]
        bias_in = jnp.where(first, jnp.stack(inner, axis=1), jnp.stack(inner[::-1], axis=1))
        grad_rows = jnp.concatenate(
            [
                sums[0:2],
                query,
                value,
                layer.norm_two[2:3],
                layer.norm_two[0:2],
                layer.bias_out,
                bias_in.reshape(4, width),
            ],
            axis=0,
        )
        layer.entry, layer.grad_rows = line.sync(entry, grad_rows)
        layer.rows_other = swap_cores(layer.grad_rows)
        if number == 1:
            layers[0].dy = layer.entry
            layers[0].dy_other = swap_cores(layer.entry)

    joined = {}
    squares = [jnp.zeros((), wide)]

    def add_squares(kind):
        pair = line.sync(layers[0].grads[kind], layers[1].grads[kind])
        squares[:] = line.sync(squares[0] + sum(jnp.sum(part * part) for part in pair))

    def woven(pair, groups):
        rows = pair[0].shape[0]
        return jnp.stack([p.reshape(rows, groups, -1) for p in pair], axis=2).reshape(rows, -1)

    def join_layers(kind):
        pair = line.sync(layers[0].grads[kind], layers[1].grads[kind])
        got = swap_cores(jnp.where(first, pair[1], pair[0]))
        mine = jnp.where(first, pair[0], pair[1])
        pair = jnp.where(first, mine, got), jnp.where(first, got, mine)
        if kind in (0, 3):
            shards = [jnp.concatenate(pair, axis=0)]
        elif kind == 2:
            shards = [woven([unpack(p) if tuned else p for p in pair], count_dp)]
        else:
            thin = [p[2 * deep : 2 * deep + half_vectors, :deep] for p in pair]
            if tuned:
                pair = [unpack(p[: 2 * deep]) for p in pair]
            shards = [
                woven([p[:, :half_qkv] for p in pair], 3),
                jnp.concatenate([p[:, half_qkv:] for p in pair], axis=1),
            ]
            if tuned:
                shards.append(jnp.concatenate(thin, axis=0))
        joined[kind] = line.sync(*shards)

    def own_tokens(zero, one):
        zero, one = line.sync(zero, one)
        got = swap_cores(jnp.where(first, one, zero))
        return join(jnp.where(first, zero, one), got, 0)

    tokens_out = []

    def token_outputs():
        tokens_out.append(own_tokens(layers[0].block, layers[1].block))
        tokens_out.append(own_tokens(layers[0].entry, layers[1].entry))

    steps = {
        1: forward_one,
        2: forward_two,
        3: forward_three,
        4: forward_four,
        62: backward_two,
        63: backward_three,
        64: backward_four,
        65: backward_five,
        31: first_grad,
        32: in_grad,
        33: out_grad,
    }
    flows = {}
    for index, batch in enumerate(GATHERS):
        values = [parts[key % 10][key // 10] for key in batch]
        if tuned:
            flows[100 + index] = gather_flow(line, values, me, batch, layers)
            continue
        for key, value in zip(batch, values):
            layer = layers[key % 10]
            if key < 10:
                layer.spread = lax.all_gather(value, DP, axis=1, tiled=True)
                continue
            mine = lax.all_gather(value, DP, axis=0, tiled=True)
            mine = mine.reshape(SLABS, -1, width) if key // 10 == 3 else slabs_of(mine)
            layer.weights[key // 10] = (mine, swap_cores(mine))
    if tuned:
        for index, batch in enumerate(SCATTERS):
            flows[200 + index] = scatter_flow(line, batch[0], layers)
    for event in ORDER:
        if event in flows:
            next(flows[event], None)
        elif event // 10 in steps:
            steps[event // 10](event % 10)
        elif event == 500:
            token_outputs()
        elif event > 400 and tuned:
            add_squares(event - 400)
            join_layers(event - 400)
    for key in [key for batch in SCATTERS for key in batch if not tuned]:
        layer = layers[key % 10]
        total = layer.chip_grads[key // 10].astype(wide)
        if key // 10 == 3:
            natural = total.reshape(-1, width)
        else:
            natural = from_slabs(total[:, : 2 * deep])
        layer.grads[key // 10] = lax.psum_scatter(natural, DP, scatter_dimension=0, tiled=True)
        if key // 10 == 1:
            thin = total[:, 2 * deep : 2 * deep + half_vectors, :deep].transpose(1, 0, 2)
            thin = thin.reshape(half_vectors, width)
            layer.grads[0] = lax.psum_scatter(thin, DP, scatter_dimension=1, tiled=True)

    kinds = [kind for kind in layers[0].grads if kind not in joined]
    for kind in kinds:
        add_squares(kind)
    if tuned:
        global_sum = total_of(line, squares[0])
    else:
        global_sum = lax.psum(squares[0], (SECTION, *DP))
    for kind in kinds:
        join_layers(kind)

    thin = joined[1][2] if tuned else joined[0][0]
    shards = (*joined[1][:2], *joined[2], *joined[3], thin)
    global_sum, *shards = line.sync(global_sum, *shards)
    grad_norm = jnp.sqrt(global_sum)
    factor = clip_norm / jnp.maximum(grad_norm, clip_norm)
    blocks, input_grad = tokens_out
    firsts = (first_qkv[0], first_proj[0], first_in[0], first_out[0], first_vectors[0])
    seconds = (second_qkv[0], second_proj[0], second_in[0], second_out[0], second_vectors[0])
    rates = (rate_matrix, rate_matrix, rate_matrix, rate_matrix, rate_vector)
    decays = (decay_matrix, decay_matrix, decay_matrix, decay_matrix, 0.0)
    results = [
        adam_update(w, g, f, s, factor, r, d)
        for w, g, f, s, r, d in zip(masters, shards, firsts, seconds, rates, decays)
    ]
    news = tuple((item[0][None] for item in results))
    momenta = tuple((item[1][None] for item in results))
    variances = tuple((item[2][None] for item in results))
    copies = tuple((n.astype(low_type) for n in news))
    grads_out = tuple((s[None] for s in shards))
    return (
        blocks[None],
        input_grad[None],
        *grads_out,
        grad_norm,
        *news,
        *copies,
        *momenta,
        *variances,
    )


def solution(mesh):
    devices = mesh.devices
    split = devices.reshape(devices.shape[0], devices.shape[1] // SIDE, 2, 2)
    mesh = Mesh(split, (SECTION, *DP))
    tokens = P(DP, None)
    matrix = P(SECTION, DP, None)
    columns = P(SECTION, None, DP)
    group = (matrix, matrix, matrix, matrix, columns)
    in_specs = (tokens, P(DP), tokens, *group, *group, *group)
    out_specs = (matrix, matrix, *group, P(), *group, *group, *group, *group)
    return jax.shard_map(body, mesh=mesh, in_specs=in_specs, out_specs=out_specs, check_vma=False)
```

```python
import functools
import jax
import jax.numpy as jnp
from jax import lax
from jax.experimental import pallas as pl
from jax.experimental.pallas import tpu as pltpu
from jax.sharding import Mesh
from jax.sharding import PartitionSpec as P

HEAD = 64
SEQ = 50
STEP = 10
SIDE = 4
LEVELS = 4
GROUP = 200
SLABS = 16
TILE = 512
STEPS = 4
VMEM_MB = 48
SECTION = "section"
DP = ("z", "y", "x")
X, Y, Z = DP[2], DP[1], DP[0]
GATHERS = ((10, 0, 1), (20,), (30,), (11,), (21,), (31,))
SCATTERS = ((31,), (21,), (11,), (30,), (20,), (10,))
ORDER = (
    100, 105, 102, 101, 103, 100, 103, 100, 103, 101, 104, 100, 100, 10, 101, 103,
    102, 101, 104, 20, 102, 105, 104, 102, 101, 30, 104, 103, 102, 40, 11, 21,
    105, 104, 105, 31, 105, 621, 331, 200, 631, 200, 321, 201, 641, 651, 201, 200,
    620, 330, 201, 203, 311, 202, 203, 320, 630, 202, 204, 201, 640, 203, 650, 202,
    200, 204, 310, 205, 41, 205, 203, 500, 202, 204, 205, 403, 204, 402, 205,
)

norm_epsilon = 1e-06
clip_norm = 1.0
beta_one = 0.9
beta_two = 0.95
rate_matrix = 0.05
rate_vector = 1.0
decay_matrix = 0.1
epsilon = 1e-08
low_type = jnp.bfloat16
wide = jnp.float32


def swap_cores(x):
    return lax.ppermute(x, SECTION, [(0, 1), (1, 0)])


def flip(x, axis):
    return lax.ppermute(x, axis, [(0, 1), (1, 0)])


class Line:
    def __init__(self):
        self.token = jnp.zeros((), wide)

    def sync(self, *values):
        fenced = lax.optimization_barrier((self.token, *values))
        self.token = fenced[0]
        return fenced[1:]


class Layer:
    def __init__(self):
        self.weights = {}
        self.chip_grads = {}
        self.grads = {}


def swap_halves(here, there, first):
    got = swap_cores(there)
    return jnp.where(first, here, got), jnp.where(first, got, here)


def place_blocks(blocks, me, axis):
    shape = list(blocks[0].shape)
    shape.insert(axis, SIDE)
    full = jnp.zeros(shape, blocks[0].dtype)
    for relative, block in enumerate(blocks):
        start = [0] * len(shape)
        start[axis] = jnp.bitwise_xor(me, relative)
        full = lax.dynamic_update_slice(full, jnp.expand_dims(block, axis), start)
    return full


def add_low(left, right):
    return (left.astype(wide) + right.astype(wide)).astype(low_type)


def gather_flow(line, parts, me, keys, layers):
    half = LEVELS // 2
    counts = [part.shape[0] for part in parts]
    extras = {}
    while keys[-1] < 10:
        extras[keys[-1]] = (sum(counts[: len(keys) - 1]), counts[len(keys) - 1])
        keys = keys[:-1]
    counts = counts[: len(keys) - 1] + [sum(counts[len(keys) - 1 :])]
    (part,) = line.sync(jnp.concatenate(parts, axis=0))
    column = lax.all_gather(part, Z, axis=0, tiled=False)
    yield
    (column,) = line.sync(column)
    across = flip(column, X)
    along = flip(column, Y)
    yield
    across, along, column = line.sync(across, along, column)
    corner_low, corner_high = line.sync(along[:half], across[half:])
    corner_low = flip(corner_low, X)
    corner_high = flip(corner_high, Y)
    fulls = []
    start = 0
    for count in counts:
        stop = start + count
        fulls.append(
            place_blocks([piece[:, start:stop] for piece in (column, across, along)], me, 1)
        )
        start = stop
    fulls = line.sync(*fulls)
    yield
    corner_low, corner_high, *fulls = line.sync(corner_low, corner_high, *fulls)
    corner = jnp.bitwise_xor(me, 3)
    start = 0
    for key, count, full in zip(keys, counts, fulls):
        stop = start + count
        full = lax.dynamic_update_slice(full, corner_low[:, None, start:stop], (0, corner, 0, 0))
        full = lax.dynamic_update_slice(
            full, corner_high[:, None, start:stop], (half, corner, 0, 0)
        )
        start = stop
        (own,) = line.sync(full.reshape(LEVELS * SIDE, count, -1))
        for name, (row, size) in extras.items():
            layers[name].spread = own[:, row : row + size]
        other = swap_cores(own)
        yield
        layers[key % 10].weights[key // 10] = line.sync(own, other)
    yield


def scatter_flow(line, key, layers):
    blocks = layers[key % 10].chip_grads[key // 10]
    corner_low, corner_high, own, across, along = line.sync(*blocks)
    from_across = flip(corner_low, X)
    from_along = flip(corner_high, Y)
    yield
    from_across, from_along = line.sync(from_across, from_along)
    across, along = line.sync(*add_corners(across, along, from_across, from_along))
    got_across = flip(across, X)
    got_along = flip(along, Y)
    yield
    got_across, got_along = line.sync(got_across, got_along)
    column = own.astype(wide) + got_across.astype(wide) + got_along.astype(wide)
    (column,) = line.sync(column.astype(low_type))
    total = lax.psum_scatter(column, Z, scatter_dimension=0, tiled=False)
    yield
    (total,) = line.sync(total)
    layers[key % 10].grads[key // 10] = total.astype(wide)
    yield


def total_of(line, value):
    (value,) = line.sync(value + swap_cores(value))
    value = value + flip(value, X)
    value = value + flip(value, Y)
    for bit in (1, 2):
        pairs = [(i, i ^ bit) for i in range(LEVELS)]
        value = value + lax.ppermute(value, Z, pairs)
    return value


def normalize(inputs):
    centered = inputs - jnp.mean(inputs, axis=-1, keepdims=True)
    inverse = lax.rsqrt(jnp.mean(centered * centered, axis=-1, keepdims=True) + norm_epsilon)
    return (centered * inverse, inverse)


def normalize_back(upstream, scaled, inverse):
    return inverse * (
        upstream
        - jnp.mean(upstream, axis=-1, keepdims=True)
        - scaled * jnp.mean(upstream * scaled, axis=-1, keepdims=True)
    )


def dot_nt(left, right):
    return lax.dot_general(left, right, (((1,), (1,)), ((), ())), preferred_element_type=wide)


def dot_nn(left, right):
    return lax.dot_general(left, right, (((1,), (0,)), ((), ())), preferred_element_type=wide)


def dot_tn(left, right):
    return lax.dot_general(left, right, (((0,), (0,)), ((), ())), preferred_element_type=wide)


def same_image(rows):
    image_row = lax.broadcasted_iota(jnp.int32, (rows, rows), 0) // SEQ
    image_col = lax.broadcasted_iota(jnp.int32, (rows, rows), 1) // SEQ
    return image_row == image_col


def attend_kernel(q_ref, k_ref, v_ref, o_ref):
    rows, columns = q_ref.shape[1:]
    mask = same_image(rows)
    lane = lax.broadcasted_iota(jnp.int32, (rows, 2 * HEAD), 1)
    for start in range(0, columns, 2 * HEAD):
        place = pl.ds(start, 2 * HEAD)
        queries, keys, values = q_ref[0, :, place], k_ref[0, :, place], v_ref[0, :, place]
        queries = queries * jnp.asarray(HEAD ** (-0.5), low_type)
        mixed = []
        for head in range(2):
            inside = (lane >= head * HEAD) & (lane < (head + 1) * HEAD)
            own = jnp.where(inside, queries, jnp.zeros_like(queries))
            scores = jnp.where(mask, dot_nt(own, keys), -jnp.inf)
            raised = jnp.exp(scores - jnp.max(scores, axis=1, keepdims=True))
            weights = raised * (1.0 / jnp.sum(raised, axis=1, keepdims=True))
            mixed.append(dot_nn(weights.astype(low_type), values))
        o_ref[0, :, place] = jnp.where(lane < HEAD, mixed[0], mixed[1]).astype(low_type)


def third_at(third, rows, columns):
    return pl.BlockSpec((1, rows, columns), lambda i: (i, 0, third))


def attend(packed):
    sides, rows, columns = packed.shape
    groups, width = sides * rows // GROUP, columns // 3
    packed = packed.reshape(groups, GROUP, columns)
    mixed = pl.pallas_call(
        attend_kernel,
        grid=(groups,),
        in_specs=[third_at(third, GROUP, width) for third in range(3)],
        out_specs=third_at(0, GROUP, width),
        out_shape=jax.ShapeDtypeStruct((groups, GROUP, width), low_type),
        cost_estimate=cost(8 * sides * rows * GROUP * width, 8 * sides * rows * width),
        compiler_params=limits(),
        name="attend",
    )(packed, packed, packed)
    return mixed.reshape(sides, rows, width)


def attend_back_kernel(q_ref, k_ref, v_ref, g_ref, b_ref, d_ref):
    rows, columns = q_ref.shape[1:]
    mask = same_image(rows)
    lane = lax.broadcasted_iota(jnp.int32, (rows, 2 * HEAD), 1)
    scaling = HEAD ** (-0.5)
    lower = lane < HEAD
    d_ref[0, :, pl.ds(3 * columns, columns)] = b_ref[0]
    for start in range(0, columns, 2 * HEAD):
        place = pl.ds(start, 2 * HEAD)
        queries, keys, values = q_ref[0, :, place], k_ref[0, :, place], v_ref[0, :, place]
        upstream = g_ref[0, :, place]
        queries = queries * jnp.asarray(scaling, low_type)
        to_queries, to_keys, to_values = [], [], []
        for head in range(2):
            inside = (lane >= head * HEAD) & (lane < (head + 1) * HEAD)
            zero = jnp.zeros_like(queries)
            own_queries = jnp.where(inside, queries, zero)
            own_upstream = jnp.where(inside, upstream, zero)
            scores = jnp.where(mask, dot_nt(keys, own_queries), -jnp.inf)
            raised = jnp.exp(scores - jnp.max(scores, axis=0, keepdims=True))
            weights = raised * (1.0 / jnp.sum(raised, axis=0, keepdims=True))
            to_values.append(dot_nn(weights.astype(low_type), upstream))
            slope = dot_nt(values, own_upstream)
            inner = jnp.sum(weights * slope, axis=0, keepdims=True)
            change = (weights * (slope - inner)).astype(low_type)
            to_keys.append(dot_nn(change, queries))
            to_queries.append(dot_tn(keys, change))
        turned = jnp.concatenate([to_queries[0][:HEAD], to_queries[1][HEAD:]], axis=0)
        d_ref[0, :, place] = (turned.T * scaling).astype(low_type)
        keys_place = pl.ds(columns + start, 2 * HEAD)
        d_ref[0, :, keys_place] = jnp.where(lower, to_keys[0], to_keys[1]).astype(low_type)
        values_place = pl.ds(2 * columns + start, 2 * HEAD)
        d_ref[0, :, values_place] = jnp.where(lower, to_values[0], to_values[1]).astype(low_type)


def attend_back(packed, upstream, branch):
    sides, rows, columns = packed.shape
    groups, width = sides * rows // GROUP, columns // 3
    packed = packed.reshape(groups, GROUP, columns)
    upstream = upstream.reshape(groups, GROUP, width)
    branch = branch.reshape(groups, GROUP, width)
    total = columns + width
    slopes = pl.pallas_call(
        attend_back_kernel,
        grid=(groups,),
        in_specs=[third_at(third, GROUP, width) for third in (0, 1, 2, 0, 0)],
        out_specs=pl.BlockSpec((1, GROUP, total), lambda i: (i, 0, 0)),
        out_shape=jax.ShapeDtypeStruct((groups, GROUP, total), low_type),
        cost_estimate=cost(20 * sides * rows * GROUP * width, 14 * sides * rows * width),
        compiler_params=limits(),
        name="attend_back",
    )(packed, packed, packed, upstream, branch)
    return slopes.reshape(sides, rows, total)


def limits():
    return pltpu.CompilerParams(vmem_limit_bytes=VMEM_MB * 1024 * 1024)


def cost(flops, moved, special=0):
    return pl.CostEstimate(flops=flops, bytes_accessed=moved, transcendentals=special)


def early(count):
    return lambda i: jnp.minimum(i, count - 1)


def late(count):
    return lambda i: jnp.maximum(i - count, 0)


def tile_spec(width, first, turn):
    per = width // TILE

    def at(i):
        tile = first + turn(i)
        return (0, tile // per, tile % per)

    return pl.BlockSpec((SLABS, width // SLABS, TILE), at)


def side_spec(count, *shape):
    return pl.BlockSpec((1, *shape), lambda i: (i // count, 0, i % count))


def flat(ref):
    return ref[...].reshape(ref.shape[0] * ref.shape[1], ref.shape[2])


def project_kernel(smooth, count, x_ref, here_ref, there_ref, b_ref, *outs):
    def work(w_ref):
        total = dot_nn(x_ref[...], flat(w_ref)) + b_ref[0]
        if smooth:
            cdf = 0.5 * (1.0 + lax.erf(total * 0.7071067811865476))
            density = jnp.exp(-0.5 * total * total) * 0.3989422804014327
            outs[0][0] = (total * cdf).astype(low_type)
            outs[1][0] = (cdf + total * density).astype(low_type)
        else:
            outs[0][0] = total.astype(outs[0].dtype)

    i = pl.program_id(0)
    pl.when(i < count)(lambda: work(here_ref))
    pl.when(i >= count)(lambda: work(there_ref))


def project(x, weights, first, count, bias, kind, smooth=False):
    rows, depth = x.shape
    number = 2 if smooth else 1
    return pl.pallas_call(
        functools.partial(project_kernel, smooth, count),
        grid=(2 * count,),
        in_specs=[
            pl.BlockSpec((rows, depth), lambda i: (0, 0)),
            tile_spec(depth, first, early(count)),
            tile_spec(depth, first, late(count)),
            side_spec(count, 1, TILE),
        ],
        out_specs=[side_spec(count, rows, TILE)] * number,
        out_shape=[jax.ShapeDtypeStruct((2, rows, count * TILE), kind)] * number,
        cost_estimate=cost(4 * rows * depth * count * TILE, 4 * depth * count * TILE),
        compiler_params=limits(),
        name="project",
    )(x, *weights, bias)


def output_kernel(active_ref, w_here, w_there, middle_ref, b_ref, o_ref):
    total = dot_nn(active_ref[0], flat(w_here)) + dot_nn(active_ref[1], flat(w_there))
    o_ref[...] = (total + middle_ref[...] + b_ref[...]).astype(low_type)


def output_rows(active, weights, middle, bias):
    _, rows, depth = active.shape
    width = middle.shape[1]
    tile = width // STEPS
    weight = pl.BlockSpec((SLABS, depth // SLABS, tile), lambda i: (0, 0, i))
    part = pl.BlockSpec((rows, tile), lambda i: (0, i))
    return pl.pallas_call(
        output_kernel,
        grid=(STEPS,),
        in_specs=[
            pl.BlockSpec(active.shape, lambda i: (0, 0, 0)),
            weight,
            weight,
            part,
            pl.BlockSpec((1, tile), lambda i: (0, i)),
        ],
        out_specs=part,
        out_shape=jax.ShapeDtypeStruct((rows, width), low_type),
        cost_estimate=cost(4 * rows * depth * width, 4 * depth * width),
        compiler_params=limits(),
        name="output",
    )(active, *weights, middle, bias)


def active_grad_kernel(count, up_ref, w_here, w_there, slope_ref, o_ref, sum_ref):
    def work(w_ref):
        low = (dot_nt(up_ref[...], flat(w_ref)) * slope_ref[0].astype(wide)).astype(low_type)
        o_ref[0] = low
        sum_ref[0] = jnp.sum(low.astype(wide), axis=0, keepdims=True)

    i = pl.program_id(0)
    pl.when(i < count)(lambda: work(w_here))
    pl.when(i >= count)(lambda: work(w_there))


def active_grad(upstream, weights, slope):
    rows, width = upstream.shape
    depth = slope.shape[2]
    count = depth // TILE
    slabs = SLABS // count

    def weight(turn):
        return pl.BlockSpec((slabs, depth // SLABS, width), lambda i: (turn(i), 0, 0))

    return pl.pallas_call(
        functools.partial(active_grad_kernel, count),
        grid=(2 * count,),
        in_specs=[
            pl.BlockSpec((rows, width), lambda i: (0, 0)),
            weight(early(count)),
            weight(late(count)),
            side_spec(count, rows, TILE),
        ],
        out_specs=[side_spec(count, rows, TILE), side_spec(count, 1, TILE)],
        out_shape=[
            jax.ShapeDtypeStruct((2, rows, depth), low_type),
            jax.ShapeDtypeStruct((2, 1, depth), wide),
        ],
        cost_estimate=cost(4 * rows * depth * width, 6 * depth * width),
        compiler_params=limits(),
        name="active",
    )(upstream, *weights, slope)


def back_tile(left, packed, depth):
    slabs, _, width = packed.shape
    rows = width // SLABS
    total = None
    for block in range(2):
        count = min(depth - block * width, width)
        part = packed[:, pl.ds(block * rows, rows), pl.ds(0, count)].reshape(slabs * rows, count)
        term = dot_nt(left[:, pl.ds(block * width, count)], part)
        total = term if total is None else total + term
    return total


def middle_grad_kernel(place, *refs):
    left, w_here, w_there, middle, gain, up, proj_here, proj_there = refs[:8]
    o_middle, o_branch, o_mixed, sums, acc = refs[8:]
    i = pl.program_id(0)
    tile = acc.shape[1] // STEPS
    columns = pl.ds(pl.multiple_of(i * tile, tile), tile)
    depth = left.shape[2]
    acc[:, columns] = back_tile(left.at[0], w_here, depth) + back_tile(left.at[1], w_there, depth)

    @pl.when(i == STEPS - 1)
    def _():
        first = place[0] == 0
        grad = acc[...]
        scaled, inverse = normalize(middle[...])
        sums[0:1] = jnp.sum(grad * scaled, axis=0, keepdims=True)
        sums[1:2] = jnp.sum(grad, axis=0, keepdims=True)
        total = up[...].astype(wide) + normalize_back(grad * gain[...], scaled, inverse)
        o_middle[...] = total
        branch = total.astype(low_type)
        sums[2:3] = jnp.sum(branch.astype(wide), axis=0, keepdims=True)
        width = branch.shape[1] // 2
        near = jnp.where(first, branch[:, :width], branch[:, width:])
        far = jnp.where(first, branch[:, width:], branch[:, :width])
        o_branch[0] = near
        o_branch[1] = far
        mixed = dot_nt(near, flat(proj_here)) + dot_nt(far, flat(proj_there))
        mixed = mixed.astype(low_type)
        o_mixed[0] = jnp.where(first, mixed[:, :width], mixed[:, width:])
        o_mixed[1] = jnp.where(first, mixed[:, width:], mixed[:, :width])


def few_slabs(width):
    return pl.BlockSpec((SLABS // STEPS, 2 * width // SLABS, width), lambda i: (i, 0, 0))


def middle_grad(place, left, weights, middle, gain, upstream, firsts):
    rows, width = middle.shape
    depth = left.shape[2]
    whole = pl.BlockSpec((rows, width), lambda i: (0, 0))
    pair = pl.BlockSpec((2, rows, width // 2), lambda i: (0, 0, 0))
    halves = jax.ShapeDtypeStruct((2, rows, width // 2), low_type)
    return pl.pallas_call(
        middle_grad_kernel,
        grid=(STEPS,),
        in_specs=[
            pl.BlockSpec(memory_space=pltpu.SMEM),
            pl.BlockSpec(left.shape, lambda i: (0, 0, 0)),
            few_slabs(width),
            few_slabs(width),
            whole,
            pl.BlockSpec((1, width), lambda i: (0, 0)),
            whole,
            tile_spec(width, 3, lambda i: 0),
            tile_spec(width, 3, lambda i: 0),
        ],
        out_specs=[whole, pair, pair, pl.BlockSpec((8, width), lambda i: (0, 0))],
        out_shape=[
            jax.ShapeDtypeStruct((rows, width), wide),
            halves,
            halves,
            jax.ShapeDtypeStruct((8, width), wide),
        ],
        scratch_shapes=[pltpu.VMEM((rows, width), wide)],
        cost_estimate=cost(4 * rows * width * (depth + width // 2), 4 * depth * width),
        compiler_params=limits(),
        name="middle",
    )(place, left, *weights, middle, gain, upstream, *firsts)


def entry_grad_kernel(depth, left, w_here, w_there, inputs, gain, middle, *rest):
    o_ref, sums, side_sums, acc = rest
    i = pl.program_id(0)
    tile = acc.shape[1] // STEPS
    columns = pl.ds(pl.multiple_of(i * tile, tile), tile)
    acc[:, columns] = back_tile(left.at[0], w_here, depth) + back_tile(left.at[1], w_there, depth)

    @pl.when(i == STEPS - 1)
    def _():
        for side in range(2):
            side_sums[side] = jnp.sum(left[side, :, :depth].astype(wide), axis=0, keepdims=True)
        grad = acc[...]
        scaled, inverse = normalize(inputs[...].astype(wide))
        sums[0:1] = jnp.sum(grad * scaled, axis=0, keepdims=True)
        sums[1:2] = jnp.sum(grad, axis=0, keepdims=True)
        total = middle[...] + normalize_back(grad * gain[...], scaled, inverse)
        o_ref[...] = total.astype(low_type)


def entry_grad(left, depth, weights, inputs, gain, middle):
    rows, width = inputs.shape
    whole = pl.BlockSpec((rows, width), lambda i: (0, 0))
    return pl.pallas_call(
        functools.partial(entry_grad_kernel, depth),
        grid=(STEPS,),
        in_specs=[
            pl.BlockSpec(left.shape, lambda i: (0, 0, 0)),
            few_slabs(width),
            few_slabs(width),
            whole,
            pl.BlockSpec((1, width), lambda i: (0, 0)),
            whole,
        ],
        out_specs=[
            whole,
            pl.BlockSpec((8, width), lambda i: (0, 0)),
            pl.BlockSpec((2, 1, depth), lambda i: (0, 0, 0)),
        ],
        out_shape=[
            jax.ShapeDtypeStruct((rows, width), low_type),
            jax.ShapeDtypeStruct((8, width), wide),
            jax.ShapeDtypeStruct((2, 1, depth), wide),
        ],
        scratch_shapes=[pltpu.VMEM((rows, width), wide)],
        cost_estimate=cost(4 * rows * width * depth, 4 * depth * width),
        compiler_params=limits(),
        name="entry",
    )(left, *weights, inputs, gain, middle)


def grad_kernel(pairs, count, extra, chip, *refs):
    out_ref = refs[-1]
    slabs, deep = out_ref.shape[:2]

    def matrix(number):
        ref = refs[number]
        return ref.at[0] if len(ref.shape) == 3 else ref

    for left, right, start, size, row, rows, column in pairs:
        place = pl.ds(start, size)
        total = dot_tn(matrix(left)[...], matrix(right)[:, place])
        total = total + dot_tn(matrix(count + left)[...], matrix(count + right)[:, place])
        total = total.reshape(slabs, rows, size).astype(low_type)
        out_ref[:, pl.ds(row, rows), pl.ds(column, size)] = total
    if extra:
        out_ref[:, pl.ds(deep - SLABS, SLABS)] = refs[2 * count][...]
    if chip is None:
        return
    low_ref, high_ref, *sides = refs[-6:-1]
    i = pl.program_id(0)
    for relative, ref in enumerate(sides):
        ref[0] = out_ref[jnp.bitwise_xor(chip[0], relative)]

    @pl.when(i < LEVELS // 2)
    def _():
        low_ref[0] = out_ref[jnp.bitwise_xor(chip[0], 3)]

    @pl.when(i >= LEVELS // 2)
    def _():
        high_ref[0] = out_ref[jnp.bitwise_xor(chip[0], 3)]


def grad_whole_kernel(pairs, count, extra, *refs):
    grad_kernel(pairs, count, extra, None, *refs)


def weight_grad(chip, own, other, moving, pairs, extra=None):
    rows, depth = own[0][0].shape[-2:]
    width = 1024
    block = depth // STEPS
    slabs = SLABS // STEPS
    deep = sum(p[3] * p[5] for p in pairs) // width
    operands = [array for array, _ in (*own, *other)]

    def spec(index, array, which):
        by = int(index < moving)
        size = block if by else array.shape[-1]
        if array.ndim == 3:
            return pl.BlockSpec((1, rows, size), lambda i: (which, 0, i * by))
        return pl.BlockSpec((rows, size), lambda i: (0, i * by))

    specs = [spec(i, *pair) for pairs_of in (own, other) for i, pair in enumerate(pairs_of)]
    if extra is not None:
        deep += extra.shape[1]
        operands.append(extra)
        specs.append(pl.BlockSpec((slabs, *extra.shape[1:]), lambda i: (i, 0, 0)))
    flops = cost(4 * rows * SLABS * deep * width, 4 * SLABS * deep * width)
    if chip is None:
        return pl.pallas_call(
            functools.partial(grad_whole_kernel, pairs, len(own), extra is not None),
            grid=(STEPS,),
            in_specs=specs,
            out_specs=pl.BlockSpec((slabs, deep, width), lambda i: (i, 0, 0)),
            out_shape=jax.ShapeDtypeStruct((SLABS, deep, width), low_type),
            cost_estimate=flops,
            compiler_params=limits(),
            name="grad",
        )(*operands)
    half = LEVELS // 2

    def block(turn):
        return pl.BlockSpec((1, deep, width), lambda i: (turn(i), 0, 0))

    def shape(levels):
        return jax.ShapeDtypeStruct((levels, deep, width), low_type)

    return pl.pallas_call(
        functools.partial(grad_kernel, pairs, len(own), extra is not None),
        grid=(STEPS,),
        in_specs=[pl.BlockSpec(memory_space=pltpu.SMEM)] + specs,
        out_specs=[block(early(half)), block(late(half))] + [block(lambda i: i)] * 3,
        out_shape=[shape(half)] * 2 + [shape(LEVELS)] * 3,
        scratch_shapes=[pltpu.VMEM((slabs, deep, width), low_type)],
        cost_estimate=flops,
        compiler_params=limits(),
        name="grad",
    )(chip, *operands)


def add_kernel(across_ref, along_ref, from_across, from_along, across_out, along_out):
    along_out[...] = add_low(along_ref[...], from_across[...])
    across_out[...] = add_low(across_ref[...], from_along[...])


def add_corners(across, along, from_across, from_along):
    half, rows, width = from_across.shape

    def block(first):
        return pl.BlockSpec((1, rows, width), lambda i: (first + i, 0, 0))

    return pl.pallas_call(
        add_kernel,
        grid=(half,),
        in_specs=[block(half), block(0), block(0), block(0)],
        out_specs=[block(half), block(0)],
        out_shape=[jax.ShapeDtypeStruct(across.shape, low_type)] * 2,
        input_output_aliases={0: 0, 1: 1},
        cost_estimate=cost(half * rows * width, 12 * half * rows * width),
        compiler_params=limits(),
        name="add",
    )(across, along, from_across, from_along)


def adam_update(weight, grad, first, second, factor, rate, decay):
    clipped = grad * factor
    momentum = beta_one * first + (1.0 - beta_one) * clipped
    variance = beta_two * second + (1.0 - beta_two) * clipped * clipped
    corrected_m = momentum / (1.0 - beta_one**STEP)
    corrected_v = variance / (1.0 - beta_two**STEP)
    updated = weight - rate * (corrected_m / (jnp.sqrt(corrected_v) + epsilon) + decay * weight)
    return (updated, momentum, variance)


def body(
    patches,
    live,
    cotangent,
    w_qkv,
    w_proj,
    w_in,
    w_out,
    vectors,
    first_qkv,
    first_proj,
    first_in,
    first_out,
    first_vectors,
    second_qkv,
    second_proj,
    second_in,
    second_out,
    second_vectors,
):
    core = lax.axis_index(SECTION)
    first = core == 0
    count_dp = lax.axis_size(DP)
    tuned = count_dp == LEVELS * SIDE
    me = 2 * lax.axis_index(Y) + lax.axis_index(X)
    place = core.astype(jnp.int32).reshape(1)
    masters = (w_qkv[0], w_proj[0], w_in[0], w_out[0], vectors[0])
    width = patches.shape[1]
    deep = width // SLABS
    hidden_width = w_in.shape[2]
    count_vectors = vectors.shape[1]
    half_vectors = count_vectors // 2
    half_qkv = w_qkv.shape[2] // 2
    stripe = hidden_width // (2 * count_dp)
    tokens = patches.shape[0] // 2
    images = live.shape[0] // 2
    line = Line()
    layers = (Layer(), Layer())

    def halves_of(array, groups):
        rows, columns = array.shape
        if groups == 1:
            return array[:, : columns // 2], array[:, columns // 2 :]
        shaped = array.reshape(rows, groups, 2, -1)
        return tuple(shaped[:, :, side].reshape(rows, -1) for side in range(2))

    def choose(pair):
        return jnp.where(first, pair[0], pair[1]), jnp.where(first, pair[1], pair[0])

    def join(here, there, axis):
        return jnp.where(
            first,
            jnp.concatenate([here, there], axis=axis),
            jnp.concatenate([there, here], axis=axis),
        )

    def pack(array):
        return jnp.concatenate([array[:, :width], array[:, width:]], axis=0)

    def unpack(array):
        rows = array.shape[0] // 2
        return jnp.concatenate([array[:rows], array[rows:]], axis=1)

    def slabs_of(array):
        shaped = array.reshape(SLABS, -1, 2, width)
        return shaped.transpose(0, 2, 1, 3).reshape(SLABS, -1, width)

    def from_slabs(array):
        shaped = array.reshape(SLABS, 2, -1, width)
        return shaped.transpose(0, 2, 1, 3).reshape(-1, 2 * width)

    lowered = [m.astype(low_type) for m in masters]
    qkv, proj = halves_of(lowered[0], 3), halves_of(lowered[1], 1)
    pairs = {
        1: tuple(jnp.concatenate([a, b], axis=1) for a, b in zip(qkv, proj)),
        2: halves_of(lowered[2], count_dp),
        3: tuple(jnp.split(lowered[3], 2, axis=0)),
    }
    parts = ({}, {})
    if tuned:
        pairs[1] = tuple(pack(a) for a in pairs[1])
        pairs[2] = tuple(pack(a) for a in pairs[2])
        spread = jnp.pad(
            lowered[4], ((0, SLABS - count_vectors), (0, width - lowered[4].shape[1]))
        )
        pairs[0] = (spread, spread)
        for names in ((1, 0), (3, 2)):
            here = jnp.concatenate([choose(pairs[name])[0] for name in names], axis=0)
            there = jnp.concatenate([choose(pairs[name])[1] for name in names], axis=0)
            both = swap_halves(here, there, first)
            start = 0
            for name in names:
                stop = start + pairs[name][0].shape[0]
                for layer in range(2):
                    parts[layer][name] = both[layer][start:stop]
                start = stop
    else:
        for name in pairs:
            parts[0][name], parts[1][name] = swap_halves(*choose(pairs[name]), first)
        other = swap_cores(lowered[4])
        parts[0][0] = jnp.where(first, lowered[4], other)
        parts[1][0] = jnp.where(first, other, lowered[4])

    layers[0].x = lax.dynamic_slice_in_dim(patches, core * tokens, tokens, axis=0)

    def target_of(side):
        weighting = lax.dynamic_slice_in_dim(live, side * images, images, axis=0).astype(low_type)
        target = lax.dynamic_slice_in_dim(cotangent, side * tokens, tokens, axis=0)
        target = target.reshape(images, SEQ, width) * weighting.reshape(images, 1, 1)
        return target.reshape(tokens, width)

    layers[1].dy = target_of(core)
    layers[1].dy_other = target_of(1 - core)

    def forward_one(number):
        layer = layers[number]
        (inputs,) = line.sync(layer.x)
        if tuned:
            spread = layer.spread[:, :count_vectors, :deep]
            rows = spread.transpose(1, 0, 2).reshape(count_vectors, width).astype(wide)
        else:
            rows = layer.spread.astype(wide)
        scaled, _ = normalize(inputs.astype(wide))
        hidden = (scaled * rows[0] + rows[1]).astype(low_type)
        query, value = [choose(halves_of(rows[i : i + 1], 1)) for i in (2, 3)]
        zero = jnp.zeros_like(query[0])
        bias = jnp.stack(
            [jnp.concatenate([query[s], zero, value[s]], axis=1) for s in range(2)]
        )
        hidden, bias, layer.rows = line.sync(hidden, bias, rows)
        layer.hidden = hidden
        weights = layer.weights[1]
        (packed,) = project(hidden, weights, 0, half_qkv // TILE, bias, low_type)
        (layer.packed,) = line.sync(packed)

    def forward_two(number):
        layer = layers[number]
        packed, rows, inputs = line.sync(layer.packed, layer.rows, layer.x)
        mixed = attend(packed)
        mixed = join(mixed[0], mixed[1], 1)
        bias = jnp.stack(choose(halves_of(rows[4:5], 1)))
        (branch,) = project(mixed, layer.weights[1], half_qkv // TILE, 1, bias, wide)
        middle = inputs.astype(wide) + join(branch[0], branch[1], 1)
        scaled, _ = normalize(middle)
        hidden = (scaled * rows[5] + rows[6]).astype(low_type)
        layer.mixed, layer.middle, layer.hidden_two = line.sync(mixed, middle, hidden)
        (kept,) = line.sync(jnp.stack([layer.hidden, layer.mixed, layer.hidden_two]))
        layer.kept_other = swap_cores(kept)

    def forward_three(number):
        layer = layers[number]
        hidden, rows, layer.kept_other = line.sync(
            layer.hidden_two, layer.rows, layer.kept_other
        )
        bias = jnp.stack(choose(halves_of(rows[8:12].reshape(1, -1), count_dp)))
        count = hidden_width // 2 // TILE
        pair = project(hidden, layer.weights[2], 0, count, bias, low_type, True)
        layer.active, layer.slope = line.sync(*pair)
        layer.active_other = swap_cores(layer.active[1])

    def forward_four(number):
        layer = layers[number]
        active, middle, rows, layer.active_other = line.sync(
            layer.active, layer.middle, layer.rows, layer.active_other
        )
        output = output_rows(active, layer.weights[3], middle, rows[7:8])
        (layer.block,) = line.sync(output)
        if number == 0:
            layers[1].x = layer.block

    chip = me.astype(jnp.int32).reshape(1) if tuned else None

    def keep(layer, kind, grad):
        layer.chip_grads[kind] = line.sync(*grad) if tuned else line.sync(grad)[0]

    def out_grad(number):
        layer = layers[number]
        active, upstream, *other = line.sync(
            layer.active, layer.dy, layer.active_other, layer.dy_other
        )
        plan = ((0, 1, 0, width, 0, hidden_width // 2 // SLABS, 0),)
        grad = weight_grad(chip, [(active, 0), (upstream, 0)], [(o, 0) for o in other], 1, plan)
        keep(layer, 3, grad)

    def in_grad(number):
        layer = layers[number]
        hidden, grad_pre, kept, other = line.sync(
            layer.hidden_two, layer.grad_pre, layer.kept_other, layer.grad_pre_other
        )
        plan = tuple((0, 1, b * width, width, b * deep, deep, 0) for b in range(2))
        grad = weight_grad(chip, [(hidden, 0), (grad_pre, 0)], [(kept, 2), (other, 0)], 1, plan)
        keep(layer, 2, grad)

    def first_grad(number):
        layer = layers[number]
        rows, rows_other = line.sync(layer.grad_rows, layer.rows_other)
        extra = choose(jnp.split(rows + rows_other, 2, axis=0))[0]
        extra = extra.reshape(half_vectors, SLABS, deep).transpose(1, 0, 2).astype(low_type)
        extra = jnp.pad(extra, ((0, 0), (0, SLABS - half_vectors), (0, width - deep)))
        hidden, mixed, slopes, kept, other, extra = line.sync(
            layer.hidden, layer.mixed, layer.slopes, layer.kept_other, layer.slopes_other, extra
        )
        half = width // 2
        plan = (
            (0, 2, 0, width, 0, deep, 0),
            (0, 2, width, half, deep, deep, 0),
            (1, 2, half_qkv, half, deep, deep, half),
        )
        grad = weight_grad(
            chip,
            [(hidden, 0), (mixed, 0), (slopes, 0)],
            [(kept, 0), (kept, 1), (other, 0)],
            2,
            plan,
            extra,
        )
        keep(layer, 1, grad)

    def backward_two(number):
        layer = layers[number]
        upstream, slope, layer.dy_other = line.sync(layer.dy, layer.slope, layer.dy_other)
        pair = active_grad(upstream, layer.weights[3], slope)
        layer.grad_pre, layer.bias_in = line.sync(*pair)
        layer.grad_pre_other = swap_cores(layer.grad_pre[1])
        layer.bias_out = jnp.sum(upstream.astype(wide), axis=0, keepdims=True)

    def backward_three(number):
        layer = layers[number]
        grad_pre, middle, rows, upstream = line.sync(
            layer.grad_pre, layer.middle, layer.rows, layer.dy
        )
        results = middle_grad(
            place, grad_pre, layer.weights[2], middle, rows[5:6], upstream, layer.weights[1]
        )
        layer.grad_middle, layer.branch, layer.grad_mixed, layer.norm_two = line.sync(*results)

    def backward_four(number):
        layer = layers[number]
        packed, upstream, branch = line.sync(layer.packed, layer.grad_mixed, layer.branch)
        (layer.slopes,) = line.sync(attend_back(packed, upstream, branch))
        layer.slopes_other = swap_cores(layer.slopes[1])

    def backward_five(number):
        layer = layers[number]
        slopes, inputs, rows, grad_middle = line.sync(
            layer.slopes, layer.x, layer.rows, layer.grad_middle
        )
        entry, sums, columns = entry_grad(
            slopes, half_qkv, layer.weights[1], inputs, rows[0:1], grad_middle
        )
        third = half_qkv // 3
        query = join(columns[0, :, :third], columns[1, :, :third], 1)
        value = join(columns[0, :, 2 * third :], columns[1, :, 2 * third :], 1)
        inner = [s.reshape(count_dp, stripe) for s in layer.bias_in]
        bias_in = jnp.where(first, jnp.stack(inner, axis=1), jnp.stack(inner[::-1], axis=1))
        grad_rows = jnp.concatenate(
            [
                sums[0:2],
                query,
                value,
                layer.norm_two[2:3],
                layer.norm_two[0:2],
                layer.bias_out,
                bias_in.reshape(4, width),
            ],
            axis=0,
        )
        layer.entry, layer.grad_rows = line.sync(entry, grad_rows)
        layer.rows_other = swap_cores(layer.grad_rows)
        if number == 1:
            layers[0].dy = layer.entry
            layers[0].dy_other = swap_cores(layer.entry)

    joined = {}
    squares = [jnp.zeros((), wide)]

    def add_squares(kind):
        pair = line.sync(layers[0].grads[kind], layers[1].grads[kind])
        squares[:] = line.sync(squares[0] + sum(jnp.sum(part * part) for part in pair))

    def woven(pair, groups):
        rows = pair[0].shape[0]
        return jnp.stack([p.reshape(rows, groups, -1) for p in pair], axis=2).reshape(rows, -1)

    def join_layers(kind):
        pair = line.sync(layers[0].grads[kind], layers[1].grads[kind])
        got = swap_cores(jnp.where(first, pair[1], pair[0]))
        mine = jnp.where(first, pair[0], pair[1])
        pair = jnp.where(first, mine, got), jnp.where(first, got, mine)
        if kind in (0, 3):
            shards = [jnp.concatenate(pair, axis=0)]
        elif kind == 2:
            shards = [woven([unpack(p) if tuned else p for p in pair], count_dp)]
        else:
            thin = [p[2 * deep : 2 * deep + half_vectors, :deep] for p in pair]
            if tuned:
                pair = [unpack(p[: 2 * deep]) for p in pair]
            shards = [
                woven([p[:, :half_qkv] for p in pair], 3),
                jnp.concatenate([p[:, half_qkv:] for p in pair], axis=1),
            ]
            if tuned:
                shards.append(jnp.concatenate(thin, axis=0))
        joined[kind] = line.sync(*shards)

    def own_tokens(zero, one):
        zero, one = line.sync(zero, one)
        got = swap_cores(jnp.where(first, one, zero))
        return join(jnp.where(first, zero, one), got, 0)

    tokens_out = []

    def token_outputs():
        tokens_out.append(own_tokens(layers[0].block, layers[1].block))
        tokens_out.append(own_tokens(layers[0].entry, layers[1].entry))

    steps = {
        1: forward_one,
        2: forward_two,
        3: forward_three,
        4: forward_four,
        62: backward_two,
        63: backward_three,
        64: backward_four,
        65: backward_five,
        31: first_grad,
        32: in_grad,
        33: out_grad,
    }
    flows = {}
    for index, batch in enumerate(GATHERS):
        values = [parts[key % 10][key // 10] for key in batch]
        if tuned:
            flows[100 + index] = gather_flow(line, values, me, batch, layers)
            continue
        for key, value in zip(batch, values):
            layer = layers[key % 10]
            if key < 10:
                layer.spread = lax.all_gather(value, DP, axis=1, tiled=True)
                continue
            mine = lax.all_gather(value, DP, axis=0, tiled=True)
            mine = mine.reshape(SLABS, -1, width) if key // 10 == 3 else slabs_of(mine)
            layer.weights[key // 10] = (mine, swap_cores(mine))
    if tuned:
        for index, batch in enumerate(SCATTERS):
            flows[200 + index] = scatter_flow(line, batch[0], layers)
    for event in ORDER:
        if event in flows:
            next(flows[event], None)
        elif event // 10 in steps:
            steps[event // 10](event % 10)
        elif event == 500:
            token_outputs()
        elif event > 400 and tuned:
            add_squares(event - 400)
            join_layers(event - 400)
    for key in [key for batch in SCATTERS for key in batch if not tuned]:
        layer = layers[key % 10]
        total = layer.chip_grads[key // 10].astype(wide)
        if key // 10 == 3:
            natural = total.reshape(-1, width)
        else:
            natural = from_slabs(total[:, : 2 * deep])
        layer.grads[key // 10] = lax.psum_scatter(natural, DP, scatter_dimension=0, tiled=True)
        if key // 10 == 1:
            thin = total[:, 2 * deep : 2 * deep + half_vectors, :deep].transpose(1, 0, 2)
            thin = thin.reshape(half_vectors, width)
            layer.grads[0] = lax.psum_scatter(thin, DP, scatter_dimension=1, tiled=True)

    kinds = [kind for kind in layers[0].grads if kind not in joined]
    for kind in kinds:
        add_squares(kind)
    if tuned:
        global_sum = total_of(line, squares[0])
    else:
        global_sum = lax.psum(squares[0], (SECTION, *DP))
    for kind in kinds:
        join_layers(kind)

    thin = joined[1][2] if tuned else joined[0][0]
    shards = (*joined[1][:2], *joined[2], *joined[3], thin)
    global_sum, *shards = line.sync(global_sum, *shards)
    grad_norm = jnp.sqrt(global_sum)
    factor = clip_norm / jnp.maximum(grad_norm, clip_norm)
    blocks, input_grad = tokens_out
    firsts = (first_qkv[0], first_proj[0], first_in[0], first_out[0], first_vectors[0])
    seconds = (second_qkv[0], second_proj[0], second_in[0], second_out[0], second_vectors[0])
    rates = (rate_matrix, rate_matrix, rate_matrix, rate_matrix, rate_vector)
    decays = (decay_matrix, decay_matrix, decay_matrix, decay_matrix, 0.0)
    results = [
        adam_update(w, g, f, s, factor, r, d)
        for w, g, f, s, r, d in zip(masters, shards, firsts, seconds, rates, decays)
    ]
    news = tuple((item[0][None] for item in results))
    momenta = tuple((item[1][None] for item in results))
    variances = tuple((item[2][None] for item in results))
    copies = tuple((n.astype(low_type) for n in news))
    grads_out = tuple((s[None] for s in shards))
    return (
        blocks[None],
        input_grad[None],
        *grads_out,
        grad_norm,
        *news,
        *copies,
        *momenta,
        *variances,
    )


def solution(mesh):
    devices = mesh.devices
    split = devices.reshape(devices.shape[0], devices.shape[1] // SIDE, 2, 2)
    mesh = Mesh(split, (SECTION, *DP))
    tokens = P(DP, None)
    matrix = P(SECTION, DP, None)
    columns = P(SECTION, None, DP)
    group = (matrix, matrix, matrix, matrix, columns)
    in_specs = (tokens, P(DP), tokens, *group, *group, *group)
    out_specs = (matrix, matrix, *group, P(), *group, *group, *group, *group)
    return jax.shard_map(body, mesh=mesh, in_specs=in_specs, out_specs=out_specs, check_vma=False)
```
